256 devices in a mesh: slab: 32 (over z, x), group: 8 (over y, core).
Axes of the slice: x: 4, y: 4, z: 8, core: 2. Of those that a mesh axis runs over, the one named last changes fastest.
Arguments:
- right_side: float32 [64, 32768], P(None, ('slab', 'group')), may hold values from -6 to 6
- fine_blocks: float32 [3, 64, 64, 32768], P(None, None, None, ('slab', 'group')), may hold values from -2 to 4
- fine_inverse: float32 [64, 64, 32768], P(None, None, ('slab', 'group')), may hold values from -0.1 to 0.6
- pattern: int32 [2, 32768], P(None, ('slab', 'group')), may hold values 0 or 1
- tentative: float32 [4, 64, 32768], P(None, None, ('slab', 'group')), may hold values from -5 to 5
- slot_map: int32 [2048, 64], P(('slab', 'group')), may hold values from 0 to 63, each once within a row
- coarse_inverse: float32 [64, 64, 2048], P(None, None, ('slab', 'group')), may hold values from -0.002 to 0.21
- coarse_lower: float32 [64, 64, 2048], P(None, None, ('slab', 'group')), may hold values from -10.1 to 0.1
Outputs:
- solution: float32 [64, 32768], P(None, ('slab', 'group'))
- coarse_error: float32 [64, 2048], P(None, ('slab', 'group'))
The draws below stay inside these ranges and needn't reach their ends.
All inputs are finite; a program needn't handle non-finite values. No bound on the sum of `pattern` on one device may be relied on, other than what follows from the above.
Results may differ from the reference program's by a relative error of at most 0.0003.
Values sent between devices are 32-bit elements; how exact they have to be, the bound alone decides.
A program may use at most 64 MiB of HBM per device.

```python
import math
import jax
import jax.numpy as jnp
from jax import lax

W = 64
CW = 64
NMODE = 4
SWEEPS = 2
NB = 32768
COARSE_BLOCKS = 2048


def fine_diagonal(key):
    return jax.random.uniform(key, (W, NB), minval=2.0, maxval=3.0)


def coarse_scales(key):
    return jax.random.uniform(key, (CW, COARSE_BLOCKS), minval=5.0, maxval=10.0)


def coarse_rates(key, slow_share):
    key = jax.random.fold_in(key, 77)
    key_category, key_sluggish_rate, key_quick_rate, key_spike, key_levels = jax.random.split(key, 5)
    slow_flag = (jax.random.uniform(key_category, (CW, 1)) < slow_share).astype(jnp.float32)
    slow_rate = jnp.exp(-math.log(10.0) * jax.random.uniform(key_sluggish_rate, (CW, 1), minval=0.2, maxval=0.8) / COARSE_BLOCKS)
    fast_rate = jnp.exp(-1.0 / jax.random.uniform(key_quick_rate, (CW, 1), minval=30.0, maxval=50.0))
    decay_rates = slow_flag * slow_rate + (1.0 - slow_flag) * fast_rate
    spike_factor = (jax.random.uniform(key_spike, (1, COARSE_BLOCKS)) < 3.0 / COARSE_BLOCKS).astype(jnp.float32)
    level_count = jax.random.uniform(key_levels, (CW, COARSE_BLOCKS), minval=0.5, maxval=0.8)
    return decay_rates * (1.0 - spike_factor * (1.0 - level_count))


def draw_fine_blocks(key, part):
    diagonal = fine_diagonal(key)
    key = jax.random.fold_in(key, 3)
    key_noise, key_couple = jax.random.split(key)
    noise = jax.random.truncated_normal(key_noise, -4.0, 4.0, (3, W, W, NB)) * (0.5 / math.sqrt(W))
    coupling = jax.random.uniform(key_couple, (2, W, NB), minval=0.3, maxval=0.8)
    eye = jnp.eye(W, dtype=jnp.float32)[:, :, None]
    lower_part = -eye * coupling[0][:, None, :]
    centre_part = eye * diagonal[:, None, :]
    upper_part = -eye * coupling[1][:, None, :]
    return jnp.stack([lower_part, centre_part, upper_part]) + noise


def draw_fine_inverse(key, part):
    diagonal = fine_diagonal(key)
    key = jax.random.fold_in(key, 4)
    noise = jax.random.truncated_normal(key, -4.0, 4.0, (W, W, NB)) * (0.05 / math.sqrt(W))
    eye = jnp.eye(W, dtype=jnp.float32)[:, :, None]
    return eye * (1.0 / diagonal)[:, None, :] + noise


def draw_coarse_inverse(key, part):
    scales = coarse_scales(key)
    decay_rates = coarse_rates(key, 0.5)
    key = jax.random.fold_in(key, 5)
    noise = jax.random.truncated_normal(key, -3.0, 3.0, (CW, CW, COARSE_BLOCKS)) * 0.0003
    eye = jnp.eye(CW, dtype=jnp.float32)[:, :, None]
    return eye * (decay_rates / scales)[:, None, :] + noise


def draw_coarse_lower(key, part):
    scales = coarse_scales(key)
    key = jax.random.fold_in(key, 9)
    noise = jax.random.truncated_normal(key, -3.0, 3.0, (CW, CW, COARSE_BLOCKS)) * 0.015
    eye = jnp.eye(CW, dtype=jnp.float32)[:, :, None]
    return -eye * scales[:, None, :] + noise


def with_ends(drawn, key, low, top_value):
    longest = drawn.shape.index(max(drawn.shape))
    spots = []
    for shift in (0, 1):
        where = [jax.random.randint(jax.random.fold_in(key, axis), (), 0, length) for axis, length in enumerate(drawn.shape)]
        where[longest] = (where[longest] + shift) % drawn.shape[longest]
        spots.append(tuple(where))
    return drawn.at[spots[0]].set(low).at[spots[1]].set(top_value)


def levels(own_key, shape, cuts, smallest, high):
    def one(dim, shards_of):
        heights = jax.random.uniform(jax.random.fold_in(jax.random.fold_in(own_key, 6), dim), (shards_of,), jnp.float32, smallest / len(cuts), high / len(cuts))
        return jnp.repeat(jnp.exp(heights), shape[dim] // shards_of).reshape((-1,) + (1,) * (len(shape) - dim - 1))

    gain = one(*cuts[0])
    for cut in cuts[1:]:
        gain = gain * one(*cut)
    return gain


def scatter_about(own_key, shape, spread, reach, pieces=(), held_as=jnp.bfloat16):
    factor_of = levels(own_key, shape, pieces, -0.22, 0.18) if pieces else 1.0
    array = jax.random.normal(own_key, shape, jnp.float32) * spread * factor_of
    return jnp.minimum(jnp.maximum(array, -reach), reach).astype(held_as)


def setup_inputs(seed: int = 0) -> dict:
    streams_of = jax.random.split(jax.random.key(seed), 9)
    return {
        "right_side": scatter_about(streams_of[0], (W, NB), 1.0, 6.0, ((1, 256),), jnp.float32),
        "fine_blocks": draw_fine_blocks(jax.random.fold_in(streams_of[8], 71), 0),
        "fine_inverse": draw_fine_inverse(jax.random.fold_in(streams_of[8], 71), 0),
        "pattern": with_ends((jax.random.randint(streams_of[3], (2, NB), 0, 8) < 7).astype(jnp.int32), jax.random.fold_in(streams_of[3], 1), 0, 1),
        "tentative": scatter_about(streams_of[4], (NMODE, W, NB), 1.0, 5.0, ((2, 256),), jnp.float32),
        "slot_map": jax.vmap(lambda own: jax.random.permutation(own, CW))(jax.random.split(streams_of[5], COARSE_BLOCKS)).reshape((COARSE_BLOCKS, CW)).astype(jnp.int32),
        "coarse_inverse": draw_coarse_inverse(jax.random.fold_in(streams_of[8], 71), 0),
        "coarse_lower": draw_coarse_lower(jax.random.fold_in(streams_of[8], 71), 0),
    }


damping = 0.8
smoothing = 0.67
highest = lax.Precision.HIGHEST

def fine_apply(iterate, blocks, pattern):
    border = jnp.zeros((iterate.shape[0], 1), jnp.float32)
    previous = jnp.concatenate([border, iterate[:, :-1]], axis=1) * pattern[0].astype(jnp.float32)[None, :]
    following = jnp.concatenate([iterate[:, 1:], border], axis=1) * pattern[1].astype(jnp.float32)[None, :]
    product = jnp.einsum('abn,bn->an', blocks[0], previous, precision=highest)
    product = product + jnp.einsum('abn,bn->an', blocks[1], iterate, precision=highest)
    return product + jnp.einsum('abn,bn->an', blocks[2], following, precision=highest)

def block_apply(inverse, iterate):
    return jnp.einsum('abn,bn->an', inverse, iterate, precision=highest)

def selector_of(slot_map):
    block_width = slot_map.shape[1]
    return (slot_map[:, :, None] == jnp.arange(block_width, dtype=jnp.int32)[None, None, :]).astype(jnp.float32)

def restrict(residue, tentative, slot_map):
    num_modes = tentative.shape[0]
    num_blocks = slot_map.shape[0]
    block_width = slot_map.shape[1]
    weights = jnp.einsum('man,an->mn', tentative, residue, precision=highest) * (1.0 / math.sqrt(residue.shape[0]))
    weights = weights.reshape(num_modes, num_blocks, block_width // num_modes).transpose(1, 2, 0).reshape(num_blocks, block_width)
    return jnp.einsum('jqs,jq->sj', selector_of(slot_map), weights, precision=highest)

def extend(coarse, tentative, slot_map):
    num_modes = tentative.shape[0]
    num_blocks = slot_map.shape[0]
    block_width = slot_map.shape[1]
    weights = jnp.einsum('jqs,sj->jq', selector_of(slot_map), coarse, precision=highest)
    weights = weights.reshape(num_blocks, block_width // num_modes, num_modes).transpose(2, 0, 1).reshape(num_modes, -1)
    return jnp.einsum('man,mn->an', tentative, weights, precision=highest) * (1.0 / math.sqrt(tentative.shape[1]))

def coarse_sweep(coarse_rhs, coarse_inverse, coarse_lower, incoming):

    def advance(carried, items):
        rhs_block, inverse_block, lower_block = items
        solved = jnp.dot(inverse_block, rhs_block - jnp.dot(lower_block, carried, precision=highest), precision=highest)
        return (solved, solved)
    unused, solved_all = lax.scan(advance, incoming, (coarse_rhs.T, jnp.moveaxis(coarse_inverse, 2, 0), jnp.moveaxis(coarse_lower, 2, 0)))
    return solved_all.T

def reference(right_side, fine_blocks, fine_inverse, pattern, tentative, slot_map, coarse_inverse, coarse_lower):
    solution = damping * block_apply(fine_inverse, right_side)
    for sweep_index in range(SWEEPS - 1):
        solution = solution + damping * block_apply(fine_inverse, right_side - fine_apply(solution, fine_blocks, pattern))
    residue = right_side - fine_apply(solution, fine_blocks, pattern)
    coarse_rhs = restrict(residue, tentative, slot_map)
    coarse_error = coarse_sweep(coarse_rhs, coarse_inverse, coarse_lower, jnp.zeros((coarse_rhs.shape[0],), jnp.float32))
    correction = extend(coarse_error, tentative, slot_map)
    solution = solution + correction - smoothing * block_apply(fine_inverse, fine_apply(correction, fine_blocks, pattern))
    for sweep_index in range(SWEEPS):
        solution = solution + damping * block_apply(fine_inverse, right_side - fine_apply(solution, fine_blocks, pattern))
    return (solution, coarse_error)
```

```python
import functools
import math

import jax
import jax.numpy as jnp
from jax import lax
from jax.experimental import pallas as pl
from jax.experimental.pallas import tpu as pltpu
from jax.sharding import PartitionSpec as P

DAMP = 0.8
SMOOTH = 0.67
F32 = jnp.float32
BF16 = jnp.bfloat16
MESH = pl.DeviceIdType.MESH

NN = (((1,), (0,)), ((), ()))
NT = (((1,), (1,)), ((), ()))


def split(x):
    hi = x.astype(BF16)
    return hi, (x - hi.astype(F32)).astype(BF16)


def dot1(a, b, dims=NN):
    return lax.dot_general(a, b, dims, preferred_element_type=F32)


def dot3(a, b, dims=NN):
    ah, al = split(a)
    bh, bl = split(b)
    return dot1(ah, bh, dims) + (dot1(ah, bl, dims) + dot1(al, bh, dims))


def dot2(a, b, dims=NN):
    ah, al = split(a)
    return dot1(ah, b, dims) + dot1(al, b, dims)


def iota(shape, dim):
    return lax.broadcasted_iota(jnp.int32, shape, dim)


def fold_rows(parts):
    row = iota((8, 128), 0)

    def mix(a, b, mask, shift):
        return jnp.where(mask, a, b) + pltpu.roll(jnp.where(mask, b, a), shift, 0)

    q = [parts[(i + 3) % 8] for i in range(8)]
    y = [mix(q[k], q[k + 4], ((row - k) & 7) < 4, 4) for k in range(4)]
    z = [mix(y[k], y[k + 2], ((row - k) & 3) >= 2, 2) for k in range(2)]
    return mix(z[0], z[1], (row & 1) == 1, 1)


def row_sum(x):
    x = x + pltpu.roll(x, 4, 0)
    x = x + pltpu.roll(x, 2, 0)
    return x + pltpu.roll(x, 1, 0)


def matvec(terms, width, emit):
    def one(g, unused):
        parts = []
        for a in range(8):
            total = None
            for load, v in terms:
                product = load(g * 8 + a) * v
                total = product if total is None else total + product
            parts.append(jnp.sum(total.reshape(width // 8, 8, 128), axis=0))
        emit(pl.ds(pl.multiple_of(g * 8, 8), 8), fold_rows(parts))
        return unused

    lax.fori_loop(0, width // 8, one, 0)


def pack_matrix(m):
    return jnp.concatenate([m[:32, :], m[32:, :]], axis=1)


def unpack_matrix(p):
    return jnp.concatenate([p[:, :64], p[:, 64:]], axis=0)


def scan_products(ref, count):
    half = 1
    while half < count:
        for start in range(0, count, 2 * half):
            mid = start + half
            left = pl.ds(start * 64, half * 64)
            ref[left, :] = dot3(ref[left, :], ref[pl.ds(mid * 64, 64), :])
        half *= 2


def scan_prefix(ref, count):
    half = 1
    while half < count:
        for start in range(0, count, 2 * half):
            mid = start + half
            right = pl.ds(mid * 64, half * 64)
            ref[right, :] = dot3(ref[right, :], ref[pl.ds((mid - 1) * 64, 64), :])
        half *= 2


def diagonal(x, count):
    return jnp.where(iota(x.shape, 0) == iota(x.shape, 1) // 64, x, 0.0)


def lanes_folded(x):
    t = x[:, 0:128] + x[:, 128:256] + x[:, 256:384] + x[:, 384:512]
    return t[:, :64] + t[:, 64:]


def padded(x):
    return jnp.concatenate([x, jnp.zeros_like(x)], axis=1)


def kernel(
    nz, nx, ng,
    b_h, f_h, i_h, pat_h, tent_h, slot_h, ci_h, cl_h,
    sol_ref, ce_ref,
    F, I, b, pat, tent, slot, ci, cl,
    work, res, corr,
    cis, Zl, Pl, Z1, Zm1, Z2, Zm2, Zm3,
    Xl, W1, W2, W3,
    RM1, RM2, RM3, RV1, RV2, RV3, halo_out, halo_in,
    load_sem, m_send, m_recv, v_send, v_recv, h_send, h_recv,
):
    slab, g = lax.axis_index("slab"), lax.axis_index("group")
    z, x = slab // nx, slab % nx
    ns = nz * nx

    copies = []
    for k, (src, dst) in enumerate(
        [(ci_h, ci), (cl_h, cl), (i_h, I), (b_h, b), (slot_h, slot), (pat_h, pat),
         (f_h.at[1], F.at[1]), (f_h.at[0], F.at[0]), (f_h.at[2], F.at[2]), (tent_h, tent)]
    ):
        copy = pltpu.make_async_copy(src, dst, load_sem.at[k])
        copy.start()
        copies.append(copy)
    ci_c, cl_c, i_c, b_c, slot_c, pat_c, f1_c, f0_c, f2_c, tent_c = copies

    def in_group(o):
        return (slab, lax.rem(g + o, ng))

    def along_x(o):
        return (z * nx + lax.rem(x + o, nx), g)

    def along_z(o):
        return (lax.rem(z + o, nz) * nx + x, g)

    at_end, at_start = g == ng - 1, g == 0
    right = (jnp.where(at_end, lax.rem(slab + 1, ns), slab), lax.rem(g + 1, ng))
    left = (jnp.where(at_start, lax.rem(slab + ns - 1, ns), slab), lax.rem(g + ng - 1, ng))

    barrier = pltpu.get_barrier_semaphore()
    peers = [in_group(o) for o in range(1, ng)] + [along_x(o) for o in range(1, nx)]
    peers += [along_z(o) for o in range(1, nz)] + [right, left]
    for peer in peers:
        pl.semaphore_signal(barrier, inc=1, device_id=peer, device_id_type=MESH)

    row64, lane64 = iota((64, 64), 0), iota((64, 64), 1)
    eye = (row64 == lane64).astype(F32)
    ci_c.wait()
    cl_c.wait()
    for j in range(8):
        cij = ci[:, j, :]
        cis[pl.ds(j * 64, 64), :] = cij
        m = -dot3(cij, cl[:, j, :])
        Pl[pl.ds(j * 64, 64), :] = m
        e = m.T
        Zl[pl.ds(j * 64, 64), :] = e
        Xl[pl.ds(j * 64, 64), :] = e
    scan_products(Zl, 8)

    pl.semaphore_wait(barrier, len(peers))

    def gather_start(ref, own, target, count, send, recv):
        started = []
        for o in range(1, count):
            copy = pltpu.make_async_remote_copy(
                src_ref=ref.at[own],
                dst_ref=ref.at[own],
                send_sem=send.at[o],
                recv_sem=recv.at[own],
                device_id=target(o),
                device_id_type=MESH,
            )
            copy.start()
            started.append(copy)
        return started

    def gather_wait(started, ref, own, count, recv):
        for o in range(1, count):
            other = lax.rem(own + o, count)
            pltpu.make_async_copy(ref.at[other], ref.at[other], recv.at[other]).wait()
        for copy in started:
            copy.wait_send()

    RM1[g] = pack_matrix(Zl[0:64, :])
    rm1 = gather_start(RM1, g, in_group, ng, m_send.at[0], m_recv.at[0])

    lane8, lane = iota((8, 128), 1), iota((64, 128), 1)
    has_left = jnp.logical_not(jnp.logical_and(slab == 0, at_start))
    has_right = jnp.logical_not(jnp.logical_and(slab == ns - 1, at_end))

    def halo_start(turn, ref):
        to_right, to_left = jnp.zeros((8, 128), F32), jnp.zeros((8, 128), F32)
        for k in range(8):
            piece = ref[pl.ds(8 * k, 8), :]
            to_right = jnp.where(lane8 == k, pltpu.roll(piece, k + 1, 1), to_right)
            to_left = jnp.where(lane8 == k, pltpu.roll(piece, k, 1) if k else piece, to_left)
        halo_out[turn, 0] = to_right
        halo_out[turn, 1] = to_left
        started = []
        for side, peer in ((0, right), (1, left)):
            copy = pltpu.make_async_remote_copy(
                src_ref=halo_out.at[turn, side],
                dst_ref=halo_in.at[turn, side],
                send_sem=h_send.at[turn, side],
                recv_sem=h_recv.at[turn, side],
                device_id=peer,
                device_id_type=MESH,
            )
            copy.start()
            started.append(copy)
        return started

    def fine_apply(turn, ref, started, emit):
        for copy in started:
            copy.wait()
        from_left = jnp.where(has_left, halo_in[turn, 0], 0.0)
        from_right = jnp.where(has_right, halo_in[turn, 1], 0.0)
        value = ref[...]
        before, after = [], []
        for k in range(8):
            piece = value[8 * k : 8 * k + 8]
            edge = pltpu.roll(from_left, (128 - k) % 128, 1) if k else from_left
            before.append(jnp.where(lane8 == 0, edge, pltpu.roll(piece, 1, 1)))
            edge = pltpu.roll(from_right, 127 - k, 1)
            after.append(jnp.where(lane8 == 127, edge, pltpu.roll(piece, 127, 1)))
        previous = jnp.concatenate(before, axis=0) * pat[0:1, :].astype(F32)
        following = jnp.concatenate(after, axis=0) * pat[1:2, :].astype(F32)
        matvec(
            [
                (lambda a: F[1, a], value),
                (lambda a: F[0, a], previous),
                (lambda a: F[2, a], following),
            ],
            64,
            emit,
        )

    def block_apply(value, emit):
        matvec([(lambda a: I[a], value)], 64, emit)

    def to_residue(rows, y):
        res[rows, :] = b[rows, :] - y

    def sweep(turn, ref, started):
        fine_apply(turn, ref, started, to_residue)

        def emit(rows, y):
            ref[rows, :] = ref[rows, :] + DAMP * y

        block_apply(res[...], emit)

    def first(rows, y):
        work[rows, :] = DAMP * y

    i_c.wait()
    b_c.wait()
    block_apply(b[...], first)
    h0 = halo_start(0, work)

    slot_c.wait()
    q, col = iota((64, 512), 0), iota((64, 512), 1)
    pick = (q == (col % 16) * 4 + col // 128).astype(BF16)
    own_block = iota((8, 512), 0) == (iota((8, 512), 1) % 128) // 16
    slots = dot1(slot[...].astype(F32).astype(BF16), pick)
    slots = row_sum(jnp.where(own_block, slots, 0.0))
    slots = jnp.concatenate([slots] * 8, axis=0)
    GT = (slots == q.astype(F32)).astype(BF16)

    pat_c.wait()
    f0_c.wait()
    f1_c.wait()
    f2_c.wait()
    sweep(0, work, h0)
    h1 = halo_start(1, work)

    def upward(started, ref, own, count, recv, full, masked):
        gather_wait(started, ref, own, count, recv)
        for k in range(count):
            e = unpack_matrix(ref[k])
            rows = pl.ds(k * 64, 64)
            if full is not None:
                full[rows, :] = e
            masked[rows, :] = jnp.where(k < own, e, eye)
        if full is not None:
            scan_products(full, count)
        scan_products(masked, count)

    def later(ref, h, count):
        return ref[pl.ds((h + 1) * 64, 64), :] if h + 1 < count else eye

    upward(rm1, RM1, g, ng, m_recv.at[0], Z1, Zm1)
    RM2[x] = pack_matrix(Z1[0:64, :])
    rm2 = gather_start(RM2, x, along_x, nx, m_send.at[1], m_recv.at[1])
    for h in range(ng):
        W1[pl.ds(h * 64, 64), :] = jnp.concatenate(
            [later(Z1, h, ng), jnp.where(h < g, later(Zm1, h, ng), 0.0)], axis=1
        )

    fine_apply(1, work, h1, to_residue)
    tent_c.wait()
    residue = res[...]
    values = []
    for m in range(4):
        weight = jnp.sum((tent[m] * residue).reshape(8, 8, 128), axis=0)
        values.append(row_sum(weight) * (1.0 / math.sqrt(64)))
    spread = jnp.where(own_block, jnp.concatenate(values, axis=1), 0.0)
    rhs = dot2(spread, GT, NT)
    offsets = diagonal(dot3(rhs, cis[...], NT), 8)
    after_own = jnp.concatenate([Zl[64:512, :], eye], axis=0)
    RV1[g] = padded(row_sum(dot3(offsets, after_own)))
    rv1 = gather_start(RV1, g, in_group, ng, v_send.at[0], v_recv.at[0])

    upward(rm2, RM2, x, nx, m_recv.at[1], Z2, Zm2)
    RM3[z] = pack_matrix(Z2[0:64, :])
    rm3 = gather_start(RM3, z, along_z, nz, m_send.at[2], m_recv.at[2])
    for h in range(nx):
        W2[pl.ds(h * 64, 64), :] = jnp.concatenate(
            [later(Z2, h, nx), jnp.where(h < x, later(Zm2, h, nx), 0.0)], axis=1
        )

    own = lanes_folded(offsets)
    row8 = iota((8, 64), 0)
    carried = jnp.broadcast_to(own[0:1], (8, 64))
    local = carried
    for j in range(1, 8):
        carried = dot3(carried, Xl[pl.ds(j * 64, 64), :]) + own[j : j + 1]
        local = jnp.where(row8 >= j, carried, local)
    scan_prefix(Pl, 8)

    def inflow(ref, weights, count):
        total = None
        for h in range(count):
            term = dot3(ref[h][:, :64], weights[pl.ds(h * 64, 64), :])
            total = term if total is None else total + term
        return total

    gather_wait(rv1, RV1, g, ng, v_recv.at[0])
    flow1 = inflow(RV1, W1, ng)
    RV2[x] = padded(flow1[:, :64])
    rv2 = gather_start(RV2, x, along_x, nx, v_send.at[1], v_recv.at[1])

    upward(rm3, RM3, z, nz, m_recv.at[2], None, Zm3)
    A1 = Zm1[0:64, :]
    A21 = dot3(Zm2[0:64, :], A1)
    for h in range(nz):
        W3[pl.ds(h * 64, 64), :] = jnp.where(h < z, later(Zm3, h, nz), 0.0)
    W3[...] = dot3(W3[...], A21)

    gather_wait(rv2, RV2, x, nx, v_recv.at[1])
    flow2 = inflow(RV2, W2, nx)
    RV3[z] = padded(flow2[:, :64])
    rv3 = gather_start(RV3, z, along_z, nz, v_send.at[2], v_recv.at[2])
    nearer = dot3(flow2[:, 64:], A1) + flow1[:, 64:]
    gather_wait(rv3, RV3, z, nz, v_recv.at[2])
    incoming = inflow(RV3, W3, nz) + nearer

    coarse = local + lanes_folded(diagonal(dot3(incoming, Pl[...], NT), 8))
    ce_ref[...] = coarse
    weights = jnp.where(own_block, dot2(coarse, GT), 0.0)
    total = None
    for m in range(4):
        w = row_sum(weights[:, m * 128 : m * 128 + 128]) * (1.0 / math.sqrt(64))
        term = tent[m] * jnp.concatenate([w] * 8, axis=0)
        total = term if total is None else total + term
    corr[...] = total
    h2 = halo_start(2, corr)

    def to_res(rows, y):
        res[rows, :] = y

    fine_apply(2, corr, h2, to_res)

    def prolong(rows, y):
        work[rows, :] = work[rows, :] + corr[rows, :] - SMOOTH * y

    block_apply(res[...], prolong)
    h3 = halo_start(3, work)
    sweep(3, work, h3)
    h4 = halo_start(4, work)
    sweep(4, work, h4)
    sol_ref[...] = work[...]


def body(nz, nx, ng, right_side, fine_blocks, fine_inverse, pattern, tentative, slot_map, coarse_inverse, coarse_lower):
    vmem = lambda *shape: pltpu.VMEM(shape, F32)
    dma = lambda *shape: pltpu.SemaphoreType.DMA(shape)
    top = max(nz, nx, ng)
    scratch = [
        vmem(3, 64, 64, 128), vmem(64, 64, 128), vmem(64, 128), pltpu.VMEM((2, 128), jnp.int32), vmem(4, 64, 128),
        pltpu.VMEM((8, 64), jnp.int32), vmem(64, 8, 64), vmem(64, 8, 64),
        vmem(64, 128), vmem(64, 128), vmem(64, 128),
        vmem(512, 64), vmem(512, 64), vmem(512, 64), vmem(ng * 64, 64), vmem(ng * 64, 64),
        vmem(nx * 64, 64), vmem(nx * 64, 64), vmem(nz * 64, 64),
        vmem(512, 64), vmem(ng * 64, 128), vmem(nx * 64, 128), vmem(nz * 64, 64),
        vmem(ng, 32, 128), vmem(nx, 32, 128), vmem(nz, 32, 128),
        vmem(ng, 8, 128), vmem(nx, 8, 128), vmem(nz, 8, 128),
        vmem(5, 2, 8, 128), vmem(5, 2, 8, 128),
        dma(10), dma(3, top), dma(3, top), dma(3, top), dma(3, top), dma(5, 2), dma(5, 2),
    ]
    result, coarse = pl.pallas_call(
        functools.partial(kernel, nz, nx, ng),
        out_shape=(
            jax.ShapeDtypeStruct((64, 128), F32),
            jax.ShapeDtypeStruct((8, 64), F32),
        ),
        in_specs=[pl.BlockSpec(memory_space=pl.ANY)] * 8,
        out_specs=(
            pl.BlockSpec(memory_space=pltpu.VMEM),
            pl.BlockSpec(memory_space=pltpu.VMEM),
        ),
        scratch_shapes=scratch,
        compiler_params=pltpu.CompilerParams(
            collective_id=0, has_side_effects=True, vmem_limit_bytes=32 * 2**20
        ),
        name="v_cycle",
    )(
        right_side, fine_blocks, fine_inverse, pattern, tentative, slot_map,
        jnp.transpose(coarse_inverse, (0, 2, 1)), jnp.transpose(coarse_lower, (0, 2, 1)),
    )
    return result, coarse.T


def solution(mesh):
    slabs, ng = mesh.shape["slab"], mesh.shape["group"]
    nx = 4 if slabs % 4 == 0 and slabs > 4 else 2
    both = ("slab", "group")
    in_specs = (
        P(None, both), P(None, None, None, both), P(None, None, both), P(None, both), P(None, None, both),
        P(both, None), P(None, None, both), P(None, None, both),
    )
    return jax.shard_map(
        functools.partial(body, slabs // nx, nx, ng),
        mesh=mesh,
        in_specs=in_specs,
        out_specs=(P(None, both), P(None, both)),
        check_vma=False,
    )
```

```python
import functools
import math

import jax
import jax.numpy as jnp
from jax import lax
from jax.experimental import pallas as pl
from jax.experimental.pallas import tpu as pltpu
from jax.sharding import PartitionSpec as P

DAMP = 0.8
SMOOTH = 0.67
F32 = jnp.float32
BF16 = jnp.bfloat16
MESH = pl.DeviceIdType.MESH

NN = (((1,), (0,)), ((), ()))
NT = (((1,), (1,)), ((), ()))


def split(x):
    hi = x.astype(BF16)
    return hi, (x - hi.astype(F32)).astype(BF16)


def dot1(a, b, dims=NN):
    return lax.dot_general(a, b, dims, preferred_element_type=F32)


def split3(x):
    hi = x.astype(BF16)
    rest = x - hi.astype(F32)
    mid = rest.astype(BF16)
    return hi, mid, (rest - mid.astype(F32)).astype(BF16)


def halves(t):
    n = t.shape[1] // 2
    return t[:, :n] + t[:, n:]


def dot4(a, b):
    w = jnp.concatenate(split(b), axis=1)
    if a.shape[0] < 64:
        t = dot1(jnp.concatenate(split(a), axis=0), w)
        return halves(t[: a.shape[0]] + t[a.shape[0] :])
    return halves(dot1(jnp.concatenate(split(a), axis=1), jnp.concatenate([w, w], axis=0)))


def dot4_nt(a, b):
    t = dot1(jnp.concatenate(split(a), axis=0), jnp.concatenate(split(b), axis=0), NT)
    return halves(t[: a.shape[0]] + t[a.shape[0] :])


def dot9(a, b):
    w = jnp.concatenate(split3(b), axis=1)
    t = dot1(jnp.concatenate(split3(a), axis=1), jnp.concatenate([w] * 3, axis=0))
    return t[:, :64] + (t[:, 64:128] + t[:, 128:])


def dot2(a, b, dims=NN):
    t = dot1(jnp.concatenate(split(a), axis=0), b, dims)
    return t[: a.shape[0]] + t[a.shape[0] :]


def iota(shape, dim):
    return lax.broadcasted_iota(jnp.int32, shape, dim)


def fold_rows(parts):
    row = iota((8, 128), 0)

    def mix(a, b, mask, shift):
        return jnp.where(mask, a, b) + pltpu.roll(jnp.where(mask, b, a), shift, 0)

    q = [parts[(i + 3) % 8] for i in range(8)]
    y = [mix(q[k], q[k + 4], ((row - k) & 7) < 4, 4) for k in range(4)]
    z = [mix(y[k], y[k + 2], ((row - k) & 3) >= 2, 2) for k in range(2)]
    return mix(z[0], z[1], (row & 1) == 1, 1)


def row_sum(x):
    x = x + pltpu.roll(x, 4, 0)
    x = x + pltpu.roll(x, 2, 0)
    return x + pltpu.roll(x, 1, 0)


def matvec(terms, width, emit):
    def one(g, unused):
        parts = []
        for a in range(8):
            total = None
            for load, v in terms:
                product = load(g * 8 + a) * v
                total = product if total is None else total + product
            parts.append(jnp.sum(total.reshape(width // 8, 8, 128), axis=0))
        emit(pl.ds(pl.multiple_of(g * 8, 8), 8), fold_rows(parts))
        return unused

    lax.fori_loop(0, width // 8, one, 0)


def pack_matrix(m):
    return jnp.concatenate([m[:32, :], m[32:, :]], axis=1)


def unpack_matrix(p):
    return jnp.concatenate([p[:, :64], p[:, 64:]], axis=0)


def scan_products(ref, count, dot=dot4):
    half = 1
    while half < count:
        for start in range(0, count, 2 * half):
            mid = start + half
            left = pl.ds(start * 64, half * 64)
            ref[left, :] = dot(ref[left, :], ref[pl.ds(mid * 64, 64), :])
        half *= 2


def scan_prefix(ref, count):
    half = 1
    while half < count:
        for start in range(0, count, 2 * half):
            mid = start + half
            right = pl.ds(mid * 64, half * 64)
            ref[right, :] = dot4(ref[right, :], ref[pl.ds((mid - 1) * 64, 64), :])
        half *= 2


def diagonal(x, count):
    return jnp.where(iota(x.shape, 0) == iota(x.shape, 1) // 64, x, 0.0)


def lanes_folded(x):
    t = x[:, 0:128] + x[:, 128:256] + x[:, 256:384] + x[:, 384:512]
    return t[:, :64] + t[:, 64:]


def padded(x):
    return jnp.concatenate([x, jnp.zeros_like(x)], axis=1)


def kernel(
    nz, nx, ng,
    b_h, f_h, i_h, pat_h, tent_h, slot_h, ci_h, cl_h,
    sol_ref, ce_ref,
    F, I, b, pat, tent, slot, ci, cl,
    work, res, corr,
    cis, Zl, Pl, Z1, Zm1, Z2, Zm2, Zm3,
    Xl, W1, W2, W3,
    RM1, RM2, RM3, RV1, RV2, RV3, halo_out, halo_in,
    load_sem, m_send, m_recv, v_send, v_recv, h_send, h_recv,
):
    slab, g = lax.axis_index("slab"), lax.axis_index("group")
    z, x = slab // nx, slab % nx
    ns = nz * nx

    copies = []
    for k, (src, dst) in enumerate(
        [(ci_h, ci), (cl_h, cl), (i_h, I), (b_h, b), (slot_h, slot), (pat_h, pat),
         (f_h.at[1], F.at[1]), (f_h.at[0], F.at[0]), (f_h.at[2], F.at[2]), (tent_h, tent)]
    ):
        copy = pltpu.make_async_copy(src, dst, load_sem.at[k])
        copy.start()
        copies.append(copy)
    ci_c, cl_c, i_c, b_c, slot_c, pat_c, f1_c, f0_c, f2_c, tent_c = copies

    def in_group(o):
        return (slab, lax.rem(g + o, ng))

    def along_x(o):
        return (z * nx + lax.rem(x + o, nx), g)

    def along_z(o):
        return (lax.rem(z + o, nz) * nx + x, g)

    at_end, at_start = g == ng - 1, g == 0
    right = (jnp.where(at_end, lax.rem(slab + 1, ns), slab), lax.rem(g + 1, ng))
    left = (jnp.where(at_start, lax.rem(slab + ns - 1, ns), slab), lax.rem(g + ng - 1, ng))

    barrier = pltpu.get_barrier_semaphore()
    peers = [in_group(o) for o in range(1, ng)] + [along_x(o) for o in range(1, nx)]
    peers += [along_z(o) for o in range(1, nz)] + [right, left]
    for peer in peers:
        pl.semaphore_signal(barrier, inc=1, device_id=peer, device_id_type=MESH)

    row64, lane64 = iota((64, 64), 0), iota((64, 64), 1)
    eye = (row64 == lane64).astype(F32)
    ci_c.wait()
    cl_c.wait()
    for j in range(8):
        cij = ci[:, j, :]
        cis[pl.ds(j * 64, 64), :] = cij
        m = -dot9(cij, cl[:, j, :])
        Pl[pl.ds(j * 64, 64), :] = m
        e = m.T
        Zl[pl.ds(j * 64, 64), :] = e
        Xl[pl.ds(j * 64, 64), :] = e
    scan_products(Zl, 8, dot9)

    pl.semaphore_wait(barrier, len(peers))

    def gather_start(ref, own, target, count, send, recv):
        started = []
        for o in range(1, count):
            copy = pltpu.make_async_remote_copy(
                src_ref=ref.at[own],
                dst_ref=ref.at[own],
                send_sem=send.at[o],
                recv_sem=recv.at[own],
                device_id=target(o),
                device_id_type=MESH,
            )
            copy.start()
            started.append(copy)
        return started

    def gather_wait(started, ref, own, count, recv):
        for o in range(1, count):
            other = lax.rem(own + o, count)
            pltpu.make_async_copy(ref.at[other], ref.at[other], recv.at[other]).wait()
        for copy in started:
            copy.wait_send()

    RM1[g] = pack_matrix(Zl[0:64, :])
    rm1 = gather_start(RM1, g, in_group, ng, m_send.at[0], m_recv.at[0])

    lane8, lane = iota((8, 128), 1), iota((64, 128), 1)
    has_left = jnp.logical_not(jnp.logical_and(slab == 0, at_start))
    has_right = jnp.logical_not(jnp.logical_and(slab == ns - 1, at_end))

    def halo_start(turn, ref):
        to_right, to_left = jnp.zeros((8, 128), F32), jnp.zeros((8, 128), F32)
        for k in range(8):
            piece = ref[pl.ds(8 * k, 8), :]
            to_right = jnp.where(lane8 == k, pltpu.roll(piece, k + 1, 1), to_right)
            to_left = jnp.where(lane8 == k, pltpu.roll(piece, k, 1) if k else piece, to_left)
        halo_out[turn, 0] = to_right
        halo_out[turn, 1] = to_left
        started = []
        for side, peer in ((0, right), (1, left)):
            copy = pltpu.make_async_remote_copy(
                src_ref=halo_out.at[turn, side],
                dst_ref=halo_in.at[turn, side],
                send_sem=h_send.at[turn, side],
                recv_sem=h_recv.at[turn, side],
                device_id=peer,
                device_id_type=MESH,
            )
            copy.start()
            started.append(copy)
        return started

    def fine_apply(turn, ref, started, emit):
        for copy in started:
            copy.wait()
        from_left = jnp.where(has_left, halo_in[turn, 0], 0.0)
        from_right = jnp.where(has_right, halo_in[turn, 1], 0.0)
        value = ref[...]
        before, after = [], []
        for k in range(8):
            piece = value[8 * k : 8 * k + 8]
            edge = pltpu.roll(from_left, (128 - k) % 128, 1) if k else from_left
            before.append(jnp.where(lane8 == 0, edge, pltpu.roll(piece, 1, 1)))
            edge = pltpu.roll(from_right, 127 - k, 1)
            after.append(jnp.where(lane8 == 127, edge, pltpu.roll(piece, 127, 1)))
        previous = jnp.concatenate(before, axis=0) * pat[0:1, :].astype(F32)
        following = jnp.concatenate(after, axis=0) * pat[1:2, :].astype(F32)
        matvec(
            [
                (lambda a: F[1, a], value),
                (lambda a: F[0, a], previous),
                (lambda a: F[2, a], following),
            ],
            64,
            emit,
        )

    def block_apply(value, emit):
        matvec([(lambda a: I[a], value)], 64, emit)

    def to_residue(rows, y):
        res[rows, :] = b[rows, :] - y

    def sweep(turn, ref, started):
        fine_apply(turn, ref, started, to_residue)

        def emit(rows, y):
            ref[rows, :] = ref[rows, :] + DAMP * y

        block_apply(res[...], emit)

    def first(rows, y):
        work[rows, :] = DAMP * y

    i_c.wait()
    b_c.wait()
    block_apply(b[...], first)
    h0 = halo_start(0, work)

    slot_c.wait()
    q, col = iota((64, 512), 0), iota((64, 512), 1)
    pick = (q == (col % 16) * 4 + col // 128).astype(BF16)
    own_block = iota((8, 512), 0) == (iota((8, 512), 1) % 128) // 16
    slots = dot1(slot[...].astype(F32).astype(BF16), pick)
    slots = row_sum(jnp.where(own_block, slots, 0.0))
    slots = jnp.concatenate([slots] * 8, axis=0)
    GT = (slots == q.astype(F32)).astype(BF16)

    pat_c.wait()
    f0_c.wait()
    f1_c.wait()
    f2_c.wait()
    sweep(0, work, h0)
    h1 = halo_start(1, work)

    def upward(started, ref, own, count, recv, full, masked):
        gather_wait(started, ref, own, count, recv)
        for k in range(count):
            e = unpack_matrix(ref[k])
            rows = pl.ds(k * 64, 64)
            if full is not None:
                full[rows, :] = e
            masked[rows, :] = jnp.where(k < own, e, eye)
        if full is not None:
            scan_products(full, count)
        scan_products(masked, count)

    def later(ref, h, count):
        return ref[pl.ds((h + 1) * 64, 64), :] if h + 1 < count else eye

    upward(rm1, RM1, g, ng, m_recv.at[0], Z1, Zm1)
    RM2[x] = pack_matrix(Z1[0:64, :])
    rm2 = gather_start(RM2, x, along_x, nx, m_send.at[1], m_recv.at[1])
    def weigh(ref, h, parts):
        ref[pl.ds(h * 64, 64), :] = jnp.concatenate(split(jnp.concatenate(parts, axis=1)), axis=1)

    for h in range(ng):
        weigh(W1, h, [later(Z1, h, ng), jnp.where(h < g, later(Zm1, h, ng), 0.0)])

    fine_apply(1, work, h1, to_residue)
    tent_c.wait()
    residue = res[...]
    values = []
    for m in range(4):
        weight = jnp.sum((tent[m] * residue).reshape(8, 8, 128), axis=0)
        values.append(row_sum(weight) * (1.0 / math.sqrt(64)))
    spread = jnp.where(own_block, jnp.concatenate(values, axis=1), 0.0)
    rhs = dot2(spread, GT, NT)
    offsets = diagonal(dot4_nt(rhs, cis[...]), 8)
    after_own = jnp.concatenate([Zl[64:512, :], eye], axis=0)
    RV1[g] = padded(row_sum(halves(dot2(offsets, jnp.concatenate(split(after_own), axis=1)))))
    rv1 = gather_start(RV1, g, in_group, ng, v_send.at[0], v_recv.at[0])

    upward(rm2, RM2, x, nx, m_recv.at[1], Z2, Zm2)
    RM3[z] = pack_matrix(Z2[0:64, :])
    rm3 = gather_start(RM3, z, along_z, nz, m_send.at[2], m_recv.at[2])
    for h in range(nx):
        weigh(W2, h, [later(Z2, h, nx), jnp.where(h < x, later(Zm2, h, nx), 0.0)])

    own = lanes_folded(offsets)
    row8 = iota((8, 64), 0)
    carried = jnp.broadcast_to(own[0:1], (8, 64))
    local = carried
    for j in range(1, 8):
        carried = dot4(carried, Xl[pl.ds(j * 64, 64), :]) + own[j : j + 1]
        local = jnp.where(row8 >= j, carried, local)
    scan_prefix(Pl, 8)

    def inflow(ref, weights, count):
        flat = [ref[h] + pltpu.roll(ref[h + 1], 64, 1) for h in range(0, count, 2)]
        return halves(dot2(jnp.concatenate(flat, axis=1), weights[...]))

    gather_wait(rv1, RV1, g, ng, v_recv.at[0])
    flow1 = inflow(RV1, W1, ng)
    RV2[x] = padded(flow1[:, :64])
    rv2 = gather_start(RV2, x, along_x, nx, v_send.at[1], v_recv.at[1])

    upward(rm3, RM3, z, nz, m_recv.at[2], None, Zm3)
    A1 = Zm1[0:64, :]
    A21 = dot4(Zm2[0:64, :], A1)
    for h in range(nz):
        weigh(W3, h, [dot4(jnp.where(h < z, later(Zm3, h, nz), 0.0), A21)])

    gather_wait(rv2, RV2, x, nx, v_recv.at[1])
    flow2 = inflow(RV2, W2, nx)
    RV3[z] = padded(flow2[:, :64])
    rv3 = gather_start(RV3, z, along_z, nz, v_send.at[2], v_recv.at[2])
    nearer = dot4(flow2[:, 64:], A1) + flow1[:, 64:]
    gather_wait(rv3, RV3, z, nz, v_recv.at[2])
    incoming = inflow(RV3, W3, nz) + nearer

    coarse = local + lanes_folded(diagonal(dot4_nt(incoming, Pl[...]), 8))
    ce_ref[...] = coarse
    weights = jnp.where(own_block, dot2(coarse, GT), 0.0)
    total = None
    for m in range(4):
        w = row_sum(weights[:, m * 128 : m * 128 + 128]) * (1.0 / math.sqrt(64))
        term = tent[m] * jnp.concatenate([w] * 8, axis=0)
        total = term if total is None else total + term
    corr[...] = total
    h2 = halo_start(2, corr)

    def to_res(rows, y):
        res[rows, :] = y

    fine_apply(2, corr, h2, to_res)

    def prolong(rows, y):
        work[rows, :] = work[rows, :] + corr[rows, :] - SMOOTH * y

    block_apply(res[...], prolong)
    h3 = halo_start(3, work)
    sweep(3, work, h3)
    h4 = halo_start(4, work)
    sweep(4, work, h4)
    sol_ref[...] = work[...]


def body(nz, nx, ng, right_side, fine_blocks, fine_inverse, pattern, tentative, slot_map, coarse_inverse, coarse_lower):
    vmem = lambda *shape: pltpu.VMEM(shape, F32)
    dma = lambda *shape: pltpu.SemaphoreType.DMA(shape)
    top = max(nz, nx, ng)
    scratch = [
        vmem(3, 64, 64, 128), vmem(64, 64, 128), vmem(64, 128), pltpu.VMEM((2, 128), jnp.int32), vmem(4, 64, 128),
        pltpu.VMEM((8, 64), jnp.int32), vmem(64, 8, 64), vmem(64, 8, 64),
        vmem(64, 128), vmem(64, 128), vmem(64, 128),
        vmem(512, 64), vmem(512, 64), vmem(512, 64), vmem(ng * 64, 64), vmem(ng * 64, 64),
        vmem(nx * 64, 64), vmem(nx * 64, 64), vmem(nz * 64, 64),
        vmem(512, 64),
        pltpu.VMEM((ng * 64, 256), BF16), pltpu.VMEM((nx * 64, 256), BF16), pltpu.VMEM((nz * 64, 128), BF16),
        vmem(ng, 32, 128), vmem(nx, 32, 128), vmem(nz, 32, 128),
        vmem(ng, 8, 128), vmem(nx, 8, 128), vmem(nz, 8, 128),
        vmem(5, 2, 8, 128), vmem(5, 2, 8, 128),
        dma(10), dma(3, top), dma(3, top), dma(3, top), dma(3, top), dma(5, 2), dma(5, 2),
    ]
    result, coarse = pl.pallas_call(
        functools.partial(kernel, nz, nx, ng),
        out_shape=(
            jax.ShapeDtypeStruct((64, 128), F32),
            jax.ShapeDtypeStruct((8, 64), F32),
        ),
        in_specs=[pl.BlockSpec(memory_space=pl.ANY)] * 8,
        out_specs=(
            pl.BlockSpec(memory_space=pltpu.VMEM),
            pl.BlockSpec(memory_space=pltpu.VMEM),
        ),
        scratch_shapes=scratch,
        compiler_params=pltpu.CompilerParams(
            collective_id=0, has_side_effects=True, vmem_limit_bytes=60 * 2**20
        ),
        name="v_cycle",
    )(
        right_side, fine_blocks, fine_inverse, pattern, tentative, slot_map,
        jnp.transpose(coarse_inverse, (0, 2, 1)), jnp.transpose(coarse_lower, (0, 2, 1)),
    )
    return result, coarse.T


def solution(mesh):
    slabs, ng = mesh.shape["slab"], mesh.shape["group"]
    nx = 4 if slabs % 4 == 0 and slabs > 4 else 2
    both = ("slab", "group")
    in_specs = (
        P(None, both), P(None, None, None, both), P(None, None, both), P(None, both), P(None, None, both),
        P(both, None), P(None, None, both), P(None, None, both),
    )
    return jax.shard_map(
        functools.partial(body, slabs // nx, nx, ng),
        mesh=mesh,
        in_specs=in_specs,
        out_specs=(P(None, both), P(None, both)),
        check_vma=False,
    )
```

```python
import functools
import math

import jax
import jax.numpy as jnp
from jax import lax
from jax.experimental import pallas as pl
from jax.experimental.pallas import tpu as pltpu
from jax.sharding import PartitionSpec as P

DAMP = 0.8
SMOOTH = 0.67
F32 = jnp.float32
BF16 = jnp.bfloat16
MESH = pl.DeviceIdType.MESH

NN = (((1,), (0,)), ((), ()))
NT = (((1,), (1,)), ((), ()))


def split(x):
    hi = x.astype(BF16)
    return hi, (x - hi.astype(F32)).astype(BF16)


def dot1(a, b, dims=NN):
    return lax.dot_general(a, b, dims, preferred_element_type=F32)


def split3(x):
    hi = x.astype(BF16)
    rest = x - hi.astype(F32)
    mid = rest.astype(BF16)
    return hi, mid, (rest - mid.astype(F32)).astype(BF16)


def halves(t):
    n = t.shape[1] // 2
    return t[:, :n] + t[:, n:]


def dot4(a, b):
    w = jnp.concatenate(split(b), axis=1)
    if a.shape[0] < 64:
        t = dot1(jnp.concatenate(split(a), axis=0), w)
        return halves(t[: a.shape[0]] + t[a.shape[0] :])
    return halves(dot1(jnp.concatenate(split(a), axis=1), jnp.concatenate([w, w], axis=0)))


def dot4_nt(a, b):
    t = dot1(jnp.concatenate(split(a), axis=0), jnp.concatenate(split(b), axis=0), NT)
    return halves(t[: a.shape[0]] + t[a.shape[0] :])


def dot9(a, b):
    w = jnp.concatenate(split3(b), axis=1)
    t = dot1(jnp.concatenate(split3(a), axis=1), jnp.concatenate([w] * 3, axis=0))
    return t[:, :64] + (t[:, 64:128] + t[:, 128:])


def dot2(a, b, dims=NN):
    t = dot1(jnp.concatenate(split(a), axis=0), b, dims)
    return t[: a.shape[0]] + t[a.shape[0] :]


def iota(shape, dim):
    return lax.broadcasted_iota(jnp.int32, shape, dim)


def fold_rows(parts):
    row = iota((8, 128), 0)

    def mix(a, b, mask, shift):
        return jnp.where(mask, a, b) + pltpu.roll(jnp.where(mask, b, a), shift, 0)

    q = [parts[(i + 3) % 8] for i in range(8)]
    y = [mix(q[k], q[k + 4], ((row - k) & 7) < 4, 4) for k in range(4)]
    z = [mix(y[k], y[k + 2], ((row - k) & 3) >= 2, 2) for k in range(2)]
    return mix(z[0], z[1], (row & 1) == 1, 1)


def row_sum(x):
    x = x + pltpu.roll(x, 4, 0)
    x = x + pltpu.roll(x, 2, 0)
    return x + pltpu.roll(x, 1, 0)


def matvec(terms, width, emit):
    def one(g, unused):
        parts = []
        for a in range(8):
            total = None
            for load, v in terms:
                product = load(g * 8 + a) * v
                total = product if total is None else total + product
            parts.append(jnp.sum(total.reshape(width // 8, 8, 128), axis=0))
        emit(pl.ds(pl.multiple_of(g * 8, 8), 8), fold_rows(parts))
        return unused

    lax.fori_loop(0, width // 8, one, 0)


def pack_matrix(m):
    return jnp.concatenate([m[:32, :], m[32:, :]], axis=1)


def unpack_matrix(p):
    return jnp.concatenate([p[:, :64], p[:, 64:]], axis=0)


def scan_products(ref, count, dot=dot4):
    half = 1
    while half < count:
        for start in range(0, count, 2 * half):
            mid = start + half
            left = pl.ds(start * 64, half * 64)
            ref[left, :] = dot(ref[left, :], ref[pl.ds(mid * 64, 64), :])
        half *= 2


def scan_prefix(ref, count):
    half = 1
    while half < count:
        for start in range(0, count, 2 * half):
            mid = start + half
            right = pl.ds(mid * 64, half * 64)
            ref[right, :] = dot4(ref[right, :], ref[pl.ds((mid - 1) * 64, 64), :])
        half *= 2


def diagonal(x, count):
    return jnp.where(iota(x.shape, 0) == iota(x.shape, 1) // 64, x, 0.0)


def lanes_folded(x):
    t = x[:, 0:128] + x[:, 128:256] + x[:, 256:384] + x[:, 384:512]
    return t[:, :64] + t[:, 64:]


def padded(x):
    return jnp.concatenate([x, jnp.zeros_like(x)], axis=1)


def kernel(
    nz, nx, ng,
    b_h, f_h, i_h, pat_h, tent_h, slot_h, ci_h, cl_h,
    sol_ref, ce_ref,
    F, I, b, pat, tent, slot, ci, cl,
    work, res, corr,
    cis, Zl, Pl, Z1, Zm1, Z2, Zm2, Zm3,
    Xl, W1, W2, W3,
    RM1, RM2, RM3, RV1, RV2, RV3, halo_out, halo_in,
    Hc, msg, n_mat, n_tent, n_b, n_s, n_slot, n_pat, n_first, n_off, off_out, chalo, first_out,
    load_sem, m_send, m_recv, v_send, v_recv, h_send, h_recv, n_send, n_recv, f_send, f_recv,
):
    slab, g = lax.axis_index("slab"), lax.axis_index("group")
    z, x = slab // nx, slab % nx
    ns = nz * nx

    copies = []
    for k, (src, dst) in enumerate(
        [(ci_h, ci), (cl_h, cl), (i_h, I), (b_h, b), (slot_h, slot), (pat_h, pat),
         (f_h.at[1], F.at[1]), (f_h.at[0], F.at[0]), (f_h.at[2], F.at[2]), (tent_h, tent)]
    ):
        copy = pltpu.make_async_copy(src, dst, load_sem.at[k])
        copy.start()
        copies.append(copy)
    ci_c, cl_c, i_c, b_c, slot_c, pat_c, f1_c, f0_c, f2_c, tent_c = copies

    def in_group(o):
        return (slab, lax.rem(g + o, ng))

    def along_x(o):
        return (z * nx + lax.rem(x + o, nx), g)

    def along_z(o):
        return (lax.rem(z + o, nz) * nx + x, g)

    at_end, at_start = g == ng - 1, g == 0
    right = (jnp.where(at_end, lax.rem(slab + 1, ns), slab), lax.rem(g + 1, ng))
    left = (jnp.where(at_start, lax.rem(slab + ns - 1, ns), slab), lax.rem(g + ng - 1, ng))

    barrier = pltpu.get_barrier_semaphore()
    peers = [in_group(o) for o in range(1, ng)] + [along_x(o) for o in range(1, nx)]
    peers += [along_z(o) for o in range(1, nz)] + [right, left]
    for peer in peers:
        pl.semaphore_signal(barrier, inc=1, device_id=peer, device_id_type=MESH)

    row64, lane64 = iota((64, 64), 0), iota((64, 64), 1)
    eye = (row64 == lane64).astype(F32)
    ci_c.wait()
    cl_c.wait()
    for j in range(8):
        cij = ci[:, j, :]
        cis[pl.ds(j * 64, 64), :] = cij
        m = -dot9(cij, cl[:, j, :])
        Pl[pl.ds(j * 64, 64), :] = m
        e = m.T
        Zl[pl.ds(j * 64, 64), :] = e
        Xl[pl.ds(j * 64, 64), :] = e
    scan_products(Zl, 8, dot9)

    pl.semaphore_wait(barrier, len(peers))

    def gather_start(ref, own, target, count, send, recv):
        started = []
        for o in range(1, count):
            copy = pltpu.make_async_remote_copy(
                src_ref=ref.at[own],
                dst_ref=ref.at[own],
                send_sem=send.at[o],
                recv_sem=recv.at[own],
                device_id=target(o),
                device_id_type=MESH,
            )
            copy.start()
            started.append(copy)
        return started

    def gather_wait(started, ref, own, count, recv):
        for o in range(1, count):
            other = lax.rem(own + o, count)
            pltpu.make_async_copy(ref.at[other], ref.at[other], recv.at[other]).wait()
        for copy in started:
            copy.wait_send()

    RM1[g] = pack_matrix(Zl[0:64, :])
    rm1 = gather_start(RM1, g, in_group, ng, m_send.at[0], m_recv.at[0])

    lane8, lane = iota((8, 128), 1), iota((64, 128), 1)
    has_left = jnp.logical_not(jnp.logical_and(slab == 0, at_start))
    has_right = jnp.logical_not(jnp.logical_and(slab == ns - 1, at_end))

    def halo_start(turn, ref):
        to_right, to_left = jnp.zeros((8, 128), F32), jnp.zeros((8, 128), F32)
        for k in range(8):
            piece = ref[pl.ds(8 * k, 8), :]
            to_right = jnp.where(lane8 == k, pltpu.roll(piece, k + 1, 1), to_right)
            to_left = jnp.where(lane8 == k, pltpu.roll(piece, k, 1) if k else piece, to_left)
        halo_out[turn, 0] = to_right
        halo_out[turn, 1] = to_left
        started = []
        for side, peer in ((0, right), (1, left)):
            copy = pltpu.make_async_remote_copy(
                src_ref=halo_out.at[turn, side],
                dst_ref=halo_in.at[turn, side],
                send_sem=h_send.at[turn, side],
                recv_sem=h_recv.at[turn, side],
                device_id=peer,
                device_id_type=MESH,
            )
            copy.start()
            started.append(copy)
        return started

    def apply_with(value, left_of, right_of, emit):
        before, after = [], []
        for k in range(8):
            piece = value[8 * k : 8 * k + 8]
            before.append(jnp.where(lane8 == 0, left_of(k), pltpu.roll(piece, 1, 1)))
            after.append(jnp.where(lane8 == 127, right_of(k), pltpu.roll(piece, 127, 1)))
        previous = jnp.concatenate(before, axis=0) * pat[0:1, :].astype(F32)
        following = jnp.concatenate(after, axis=0) * pat[1:2, :].astype(F32)
        matvec(
            [
                (lambda a: F[1, a], value),
                (lambda a: F[0, a], previous),
                (lambda a: F[2, a], following),
            ],
            64,
            emit,
        )

    def fine_apply(turn, ref, started, emit):
        for copy in started:
            copy.wait()
        from_left = jnp.where(has_left, halo_in[turn, 0], 0.0)
        from_right = jnp.where(has_right, halo_in[turn, 1], 0.0)

        def left_of(k):
            return pltpu.roll(from_left, 128 - k, 1) if k else from_left

        def right_of(k):
            return pltpu.roll(from_right, 127 - k, 1)

        apply_with(ref[...], left_of, right_of, emit)

    def block_apply(value, emit):
        matvec([(lambda a: I[a], value)], 64, emit)

    def to_residue(rows, y):
        res[rows, :] = b[rows, :] - y

    def sweep(turn, ref, started):
        fine_apply(turn, ref, started, to_residue)

        def emit(rows, y):
            ref[rows, :] = ref[rows, :] + DAMP * y

        block_apply(res[...], emit)

    def first(rows, y):
        work[rows, :] = DAMP * y

    i_c.wait()
    b_c.wait()
    block_apply(b[...], first)
    h0 = halo_start(0, work)

    slot_c.wait()
    q, col = iota((64, 512), 0), iota((64, 512), 1)
    pick = (q == (col % 16) * 4 + col // 128).astype(BF16)
    own_block = iota((8, 512), 0) == (iota((8, 512), 1) % 128) // 16
    slots = dot1(slot[...].astype(F32).astype(BF16), pick)
    slots = row_sum(jnp.where(own_block, slots, 0.0))
    slots = jnp.concatenate([slots] * 8, axis=0)
    GT = (slots == q.astype(F32)).astype(BF16)

    pat_c.wait()
    f0_c.wait()
    f1_c.wait()
    f2_c.wait()
    sweep(0, work, h0)
    h1 = halo_start(1, work)

    def upward(started, ref, own, count, recv, full, masked):
        gather_wait(started, ref, own, count, recv)
        for k in range(count):
            e = unpack_matrix(ref[k])
            rows = pl.ds(k * 64, 64)
            if full is not None:
                full[rows, :] = e
            masked[rows, :] = jnp.where(k < own, e, eye)
        if full is not None:
            scan_products(full, count)
        scan_products(masked, count)

    def later(ref, h, count):
        return ref[pl.ds((h + 1) * 64, 64), :] if h + 1 < count else eye

    upward(rm1, RM1, g, ng, m_recv.at[0], Z1, Zm1)
    RM2[x] = pack_matrix(Z1[0:64, :])
    rm2 = gather_start(RM2, x, along_x, nx, m_send.at[1], m_recv.at[1])
    def weigh(ref, h, parts):
        ref[pl.ds(h * 64, 64), :] = jnp.concatenate(split(jnp.concatenate(parts, axis=1)), axis=1)

    for h in range(ng):
        weigh(W1, h, [later(Z1, h, ng), jnp.where(h < g, later(Zm1, h, ng), 0.0)])

    fine_apply(1, work, h1, to_residue)
    tent_c.wait()
    residue = res[...]
    values = []
    for m in range(4):
        weight = jnp.sum((tent[m] * residue).reshape(8, 8, 128), axis=0)
        values.append(row_sum(weight) * (1.0 / math.sqrt(64)))
    spread = jnp.where(own_block, jnp.concatenate(values, axis=1), 0.0)
    rhs = dot2(spread, GT, NT)
    offsets = diagonal(dot4_nt(rhs, cis[...]), 8)
    after_own = jnp.concatenate([Zl[64:512, :], eye], axis=0)
    RV1[g] = padded(row_sum(halves(dot2(offsets, jnp.concatenate(split(after_own), axis=1)))))
    rv1 = gather_start(RV1, g, in_group, ng, v_send.at[0], v_recv.at[0])

    own = lanes_folded(offsets)
    off_out[...] = padded(own)
    first_out[...] = pack_matrix(Pl[0:64, :])
    beside = []
    for side, peer in ((0, right), (1, left)):
        for k, (src, dst) in enumerate(
            [(work, n_s), (b, n_b), (tent, n_tent), (slot, n_slot), (pat, n_pat)]
        ):
            copy = pltpu.make_async_remote_copy(
                src_ref=src,
                dst_ref=dst.at[side],
                send_sem=n_send.at[side, k],
                recv_sem=n_recv.at[side, k],
                device_id=peer,
                device_id_type=MESH,
            )
            copy.start()
            beside.append(copy)
    for k, (src, dst) in enumerate([(first_out, n_first), (off_out, n_off)]):
        copy = pltpu.make_async_remote_copy(
            src_ref=src,
            dst_ref=dst,
            send_sem=f_send.at[k],
            recv_sem=f_recv.at[k],
            device_id=left,
            device_id_type=MESH,
        )
        copy.start()
        beside.append(copy)

    def gathered(t, load):
        def one(A, unused):
            to_right, to_left = jnp.zeros((8, 128), F32), jnp.zeros((8, 128), F32)
            for u in range(8):
                whole = load(A * 8 + u)
                edge = jnp.zeros((8, 128), F32)
                for k in range(8):
                    piece = pltpu.roll(whole[8 * k : 8 * k + 8], (2 + 16 * k) % 128, 1)
                    edge = jnp.where(lane8 // 16 == k, piece, edge)
                here = (lane8 % 16) // 2 == u
                to_right = jnp.where(here, pltpu.roll(edge, 2 * u, 1) if u else edge, to_right)
                shift = (2 * u - 2) % 128
                to_left = jnp.where(here, pltpu.roll(edge, shift, 1) if shift else edge, to_left)
            msg[0, t, A] = to_right
            msg[1, t, A] = to_left
            return unused

        lax.fori_loop(0, 8, one, 0)

    for t in range(3):
        gathered(t, lambda a, t=t: F[t, a])
    gathered(3, lambda a: I[a])
    for side, peer in ((0, right), (1, left)):
        copy = pltpu.make_async_remote_copy(
            src_ref=msg.at[side],
            dst_ref=n_mat.at[side],
            send_sem=n_send.at[side, 5],
            recv_sem=n_recv.at[side, 5],
            device_id=peer,
            device_id_type=MESH,
        )
        copy.start()
        beside.append(copy)

    upward(rm2, RM2, x, nx, m_recv.at[1], Z2, Zm2)
    RM3[z] = pack_matrix(Z2[0:64, :])
    rm3 = gather_start(RM3, z, along_z, nz, m_send.at[2], m_recv.at[2])
    for h in range(nx):
        weigh(W2, h, [later(Z2, h, nx), jnp.where(h < x, later(Zm2, h, nx), 0.0)])

    row8 = iota((8, 64), 0)
    carried = jnp.broadcast_to(own[0:1], (8, 64))
    local = carried
    for j in range(1, 8):
        carried = dot4(carried, Xl[pl.ds(j * 64, 64), :]) + own[j : j + 1]
        local = jnp.where(row8 >= j, carried, local)
    scan_prefix(Pl, 8)

    def inflow(ref, weights, count):
        flat = [ref[h] + pltpu.roll(ref[h + 1], 64, 1) for h in range(0, count, 2)]
        return halves(dot2(jnp.concatenate(flat, axis=1), weights[...]))

    gather_wait(rv1, RV1, g, ng, v_recv.at[0])
    flow1 = inflow(RV1, W1, ng)
    RV2[x] = padded(flow1[:, :64])
    rv2 = gather_start(RV2, x, along_x, nx, v_send.at[1], v_recv.at[1])

    upward(rm3, RM3, z, nz, m_recv.at[2], None, Zm3)
    A1 = Zm1[0:64, :]
    A21 = dot4(Zm2[0:64, :], A1)
    for h in range(nz):
        weigh(W3, h, [dot4(jnp.where(h < z, later(Zm3, h, nz), 0.0), A21)])

    gather_wait(rv2, RV2, x, nx, v_recv.at[1])
    flow2 = inflow(RV2, W2, nx)
    RV3[z] = padded(flow2[:, :64])
    rv3 = gather_start(RV3, z, along_z, nz, v_send.at[2], v_recv.at[2])
    nearer = dot4(flow2[:, 64:], A1) + flow1[:, 64:]
    for copy in beside:
        copy.wait()
    spot = lane % 16
    valid = jnp.logical_or(
        jnp.logical_and(spot < 3, has_left),
        jnp.logical_and(jnp.logical_and(spot >= 8, spot < 11), has_right),
    )

    def repeated(v):
        for shift in (16, 32, 64):
            v = v + pltpu.roll(v, shift, 1)
        return v

    def around(from_left, from_right):
        mine = jnp.where(lane < 3, pltpu.roll(from_left, 3, 1), 0.0)
        mine = jnp.where(jnp.logical_and(lane >= 8, lane < 11), pltpu.roll(from_right, 8, 1), mine)
        return repeated(mine)

    def with_ends(v, ref):
        first_own = jnp.where(lane == 3, pltpu.roll(ref[...], 3, 1), 0.0)
        return v + repeated(jnp.where(lane == 7, pltpu.roll(ref[...], 8, 1), first_own))

    b_halo = around(n_b[0], n_b[1])
    s_halo = around(n_s[0], n_s[1])
    tent_halo = [around(n_tent[0, m], n_tent[1, m]) for m in range(4)]
    pat_halo = [
        around(
            jnp.broadcast_to(n_pat[0, r : r + 1, :].astype(F32), (64, 128)),
            jnp.broadcast_to(n_pat[1, r : r + 1, :].astype(F32), (64, 128)),
        )
        for r in range(2)
    ]

    def placed(A, unused):
        for t in range(4):
            from_left, from_right = n_mat[0, t, A], n_mat[1, t, A]
            place = lane8 % 16
            at_left = jnp.logical_or(place == 1, place == 2)
            at_right = jnp.logical_or(place == 8, place == 9)
            for u in range(8):
                p = jnp.where(at_left, pltpu.roll(from_left, (1 - 2 * u) % 128, 1), 0.0)
                shift = (8 - 2 * u) % 128
                q = pltpu.roll(from_right, shift, 1) if shift else from_right
                Hc[t, A * 8 + u] = jnp.where(at_right, q, p)
        return unused

    lax.fori_loop(0, 8, placed, 0)

    place = iota((64, 512), 1) % 128
    asked = jnp.where(place < 3, place + 13, place - 8) * 4 + col // 128
    pick_halo = (q == asked).astype(BF16)
    ends = jnp.concatenate([n_slot[0, 7:8, :], n_slot[1, 0:1, :]] + [n_slot[1, 0:1, :]] * 6, axis=0)
    slots = dot1(ends.astype(F32).astype(BF16), pick_halo)
    which = (iota((8, 512), 1) % 128 >= 8).astype(jnp.int32) == iota((8, 512), 0)
    slots = row_sum(jnp.where(which, slots, 0.0))
    GT_halo = (jnp.concatenate([slots] * 8, axis=0) == q.astype(F32)).astype(BF16)
    M_next = unpack_matrix(n_first[...])
    P_next = dot4(M_next, Pl[448:512, :])
    local_next = dot4_nt(carried, M_next) + n_off[0:1, :64]

    def halo_matvec(terms, finish):
        packed = []
        for t, v in terms:
            p = jnp.zeros((8, 128), F32)
            for k in range(8):
                p = jnp.where(lane8 // 16 == k, v[8 * k : 8 * k + 8], p)
            packed.append((t, p))

        def one(A, unused):
            parts = []
            for u in range(8):
                total = None
                for t, p in packed:
                    term = Hc[t, A * 8 + u] * p
                    total = term if total is None else total + term
                parts.append(total)
            finish(pl.ds(pl.multiple_of(A * 8, 8), 8), repeated(fold_rows(parts)))
            return unused

        lax.fori_loop(0, 8, one, 0)

    def halo_apply(v, finish):
        halo_matvec(
            [
                (1, v),
                (0, pltpu.roll(v, 1, 1) * pat_halo[0]),
                (2, pltpu.roll(v, 127, 1) * pat_halo[1]),
            ],
            finish,
        )

    gather_wait(rv3, RV3, z, nz, v_recv.at[2])
    incoming = inflow(RV3, W3, nz) + nearer

    coarse = local + lanes_folded(diagonal(dot4_nt(incoming, Pl[...]), 8))
    ce_ref[...] = coarse
    weights = jnp.where(own_block, dot2(coarse, GT), 0.0)
    total = None
    for m in range(4):
        w = row_sum(weights[:, m * 128 : m * 128 + 128]) * (1.0 / math.sqrt(64))
        term = tent[m] * jnp.concatenate([w] * 8, axis=0)
        total = term if total is None else total + term
    corr[...] = total
    next_first = dot4_nt(incoming, P_next) + local_next
    two = jnp.concatenate([incoming[0:1], next_first[0:1]] + [next_first[0:1]] * 6, axis=0)
    weights = jnp.where(which, dot2(two, GT_halo), 0.0)
    total = None
    for m in range(4):
        w = row_sum(weights[:, m * 128 : m * 128 + 128]) * (1.0 / math.sqrt(64))
        term = tent_halo[m] * repeated(jnp.where(lane8 < 16, w, 0.0)[0:8])[0:1, :]
        total = term if total is None else total + term
    c_halo = with_ends(jnp.where(valid, total, 0.0), corr)

    def post(ref, halo, emit):
        def left_of(k):
            return pltpu.roll(halo[8 * k : 8 * k + 8], 126, 1)

        def right_of(k):
            return pltpu.roll(halo[8 * k : 8 * k + 8], 119, 1)

        apply_with(ref[...], left_of, right_of, emit)

    def to_res(rows, y):
        res[rows, :] = y

    def to_halo(rows, y):
        chalo[rows, :] = y

    post(corr, c_halo, to_res)

    def prolong(rows, y):
        sol_ref[rows, :] = work[rows, :] + corr[rows, :] - SMOOTH * y

    block_apply(res[...], prolong)
    halo_apply(c_halo, to_halo)
    halo_matvec([(3, chalo[...])], to_halo)
    s_halo = jnp.where(valid, s_halo + c_halo - SMOOTH * chalo[...], 0.0)
    s_ends = with_ends(s_halo, sol_ref)

    def smooth(rows, y):
        sol_ref[rows, :] = sol_ref[rows, :] + DAMP * y

    post(sol_ref, s_ends, to_residue)
    block_apply(res[...], smooth)
    halo_apply(s_ends, to_halo)
    halo_matvec([(3, b_halo - chalo[...])], to_halo)
    s_halo = jnp.where(valid, s_halo + DAMP * chalo[...], 0.0)
    post(sol_ref, s_halo, to_residue)
    block_apply(res[...], smooth)


def body(nz, nx, ng, right_side, fine_blocks, fine_inverse, pattern, tentative, slot_map, coarse_inverse, coarse_lower):
    vmem = lambda *shape: pltpu.VMEM(shape, F32)
    dma = lambda *shape: pltpu.SemaphoreType.DMA(shape)
    top = max(nz, nx, ng)
    scratch = [
        vmem(3, 64, 64, 128), vmem(64, 64, 128), vmem(64, 128), pltpu.VMEM((2, 128), jnp.int32), vmem(4, 64, 128),
        pltpu.VMEM((8, 64), jnp.int32), vmem(64, 8, 64), vmem(64, 8, 64),
        vmem(64, 128), vmem(64, 128), vmem(64, 128),
        vmem(512, 64), vmem(512, 64), vmem(512, 64), vmem(ng * 64, 64), vmem(ng * 64, 64),
        vmem(nx * 64, 64), vmem(nx * 64, 64), vmem(nz * 64, 64),
        vmem(512, 64),
        pltpu.VMEM((ng * 64, 256), BF16), pltpu.VMEM((nx * 64, 256), BF16), pltpu.VMEM((nz * 64, 128), BF16),
        vmem(ng, 32, 128), vmem(nx, 32, 128), vmem(nz, 32, 128),
        vmem(ng, 8, 128), vmem(nx, 8, 128), vmem(nz, 8, 128),
        vmem(2, 2, 8, 128), vmem(2, 2, 8, 128),
        vmem(4, 64, 8, 128), vmem(2, 4, 8, 8, 128), vmem(2, 4, 8, 8, 128), vmem(2, 4, 64, 128), vmem(2, 64, 128),
        vmem(2, 64, 128), pltpu.VMEM((2, 8, 64), jnp.int32), pltpu.VMEM((2, 2, 128), jnp.int32),
        vmem(32, 128), vmem(8, 128), vmem(8, 128), vmem(64, 128), vmem(32, 128),
        dma(10), dma(3, top), dma(3, top), dma(3, top), dma(3, top), dma(2, 2), dma(2, 2),
        dma(2, 6), dma(2, 6), dma(2), dma(2),
    ]
    result, coarse = pl.pallas_call(
        functools.partial(kernel, nz, nx, ng),
        out_shape=(
            jax.ShapeDtypeStruct((64, 128), F32),
            jax.ShapeDtypeStruct((8, 64), F32),
        ),
        in_specs=[pl.BlockSpec(memory_space=pl.ANY)] * 8,
        out_specs=(
            pl.BlockSpec(memory_space=pltpu.VMEM),
            pl.BlockSpec(memory_space=pltpu.VMEM),
        ),
        scratch_shapes=scratch,
        compiler_params=pltpu.CompilerParams(
            collective_id=0, has_side_effects=True, vmem_limit_bytes=60 * 2**20
        ),
        name="v_cycle",
    )(
        right_side, fine_blocks, fine_inverse, pattern, tentative, slot_map,
        jnp.transpose(coarse_inverse, (0, 2, 1)), jnp.transpose(coarse_lower, (0, 2, 1)),
    )
    return result, coarse.T


def solution(mesh):
    slabs, ng = mesh.shape["slab"], mesh.shape["group"]
    nx = 4 if slabs % 4 == 0 and slabs > 4 else 2
    both = ("slab", "group")
    in_specs = (
        P(None, both), P(None, None, None, both), P(None, None, both), P(None, both), P(None, None, both),
        P(both, None), P(None, None, both), P(None, None, both),
    )
    return jax.shard_map(
        functools.partial(body, slabs // nx, nx, ng),
        mesh=mesh,
        in_specs=in_specs,
        out_specs=(P(None, both), P(None, both)),
        check_vma=False,
    )
```

```python
import functools
import math

import jax
import jax.numpy as jnp
from jax import lax
from jax.experimental import pallas as pl
from jax.experimental.pallas import tpu as pltpu
from jax.sharding import PartitionSpec as P

DAMP = 0.8
SMOOTH = 0.67
F32 = jnp.float32
BF16 = jnp.bfloat16
MESH = pl.DeviceIdType.MESH

NN = (((1,), (0,)), ((), ()))
NT = (((1,), (1,)), ((), ()))


def split(x):
    hi = x.astype(BF16)
    return hi, (x - hi.astype(F32)).astype(BF16)


def dot1(a, b, dims=NN):
    return lax.dot_general(a, b, dims, preferred_element_type=F32)


def halves(t):
    n = t.shape[1] // 2
    return t[:, :n] + t[:, n:]


def dotf(a, b, dims=NN):
    return lax.dot_general(a, b, dims, precision=lax.Precision.HIGHEST, preferred_element_type=F32)


def dot2(a, b, dims=NN):
    t = dot1(jnp.concatenate(split(a), axis=0), b, dims)
    return t[: a.shape[0]] + t[a.shape[0] :]


def iota(shape, dim):
    return lax.broadcasted_iota(jnp.int32, shape, dim)


def fold_rows(parts):
    row = iota((8, 128), 0)

    def mix(a, b, mask, shift):
        return jnp.where(mask, a, b) + pltpu.roll(jnp.where(mask, b, a), shift, 0)

    q = [parts[(i + 3) % 8] for i in range(8)]
    y = [mix(q[k], q[k + 4], ((row - k) & 7) < 4, 4) for k in range(4)]
    z = [mix(y[k], y[k + 2], ((row - k) & 3) >= 2, 2) for k in range(2)]
    return mix(z[0], z[1], (row & 1) == 1, 1)


def row_sum(x):
    x = x + pltpu.roll(x, 4, 0)
    x = x + pltpu.roll(x, 2, 0)
    return x + pltpu.roll(x, 1, 0)


def matvec(terms, width, emit):
    def one(g, unused):
        parts = []
        for a in range(8):
            total = None
            for load, v in terms:
                product = load(g * 8 + a) * v
                total = product if total is None else total + product
            parts.append(jnp.sum(total.reshape(width // 8, 8, 128), axis=0))
        emit(pl.ds(pl.multiple_of(g * 8, 8), 8), fold_rows(parts))
        return unused

    lax.fori_loop(0, width // 8, one, 0)


def pack_matrix(m):
    return jnp.concatenate([m[:32, :], m[32:, :]], axis=1)


def unpack_matrix(p):
    return jnp.concatenate([p[:, :64], p[:, 64:]], axis=0)


def scan_products(refs, count):
    half = 1
    while half < count:
        for start in range(0, count, 2 * half):
            mid = start + half
            left = pl.ds(start * 64, half * 64)
            for ref in refs:
                ref[left, :] = dotf(ref[left, :], ref[pl.ds(mid * 64, 64), :])
        half *= 2


def scan_prefix(ref, count):
    half = 1
    while half < count:
        for start in range(0, count, 2 * half):
            mid = start + half
            right = pl.ds(mid * 64, half * 64)
            ref[right, :] = dotf(ref[right, :], ref[pl.ds((mid - 1) * 64, 64), :])
        half *= 2


def diagonal(x, count):
    return jnp.where(iota(x.shape, 0) == iota(x.shape, 1) // 64, x, 0.0)


def lanes_folded(x):
    t = x[:, 0:128] + x[:, 128:256] + x[:, 256:384] + x[:, 384:512]
    return t[:, :64] + t[:, 64:]


def padded(x):
    return jnp.concatenate([x, jnp.zeros_like(x)], axis=1)


def kernel(
    nz, nx, ng,
    b_h, f_h, i_h, pat_h, tent_h, slot_h, ci_h, cl_h,
    sol_ref, ce_ref,
    F, I, b, pat, tent, slot, ci, cl,
    work, res, corr,
    cis, Zl, Pl, Z1, Zm1, Z2, Zm2, Zm3,
    Xl, W1, W2, W3,
    RM1, RM2, RM3, RV1, RV2, RV3, halo_out, halo_in,
    Hc, msg, n_mat, n_tent, n_b, n_s, n_slot, n_pat, n_first, n_off, off_out, chalo, first_out,
    load_sem, m_send, m_recv, v_send, v_recv, h_send, h_recv, n_send, n_recv, f_send, f_recv,
):
    slab, g = lax.axis_index("slab"), lax.axis_index("group")
    z, x = slab // nx, slab % nx
    ns = nz * nx

    copies = []
    for k, (src, dst) in enumerate(
        [(ci_h, ci), (cl_h, cl), (i_h, I), (b_h, b), (slot_h, slot), (pat_h, pat),
         (f_h.at[1], F.at[1]), (f_h.at[0], F.at[0]), (f_h.at[2], F.at[2]), (tent_h, tent)]
    ):
        copy = pltpu.make_async_copy(src, dst, load_sem.at[k])
        copy.start()
        copies.append(copy)
    ci_c, cl_c, i_c, b_c, slot_c, pat_c, f1_c, f0_c, f2_c, tent_c = copies

    def in_group(o):
        return (slab, lax.rem(g + o, ng))

    def along_x(o):
        return (z * nx + lax.rem(x + o, nx), g)

    def along_z(o):
        return (lax.rem(z + o, nz) * nx + x, g)

    at_end, at_start = g == ng - 1, g == 0
    right = (jnp.where(at_end, lax.rem(slab + 1, ns), slab), lax.rem(g + 1, ng))
    left = (jnp.where(at_start, lax.rem(slab + ns - 1, ns), slab), lax.rem(g + ng - 1, ng))

    barrier = pltpu.get_barrier_semaphore()
    peers = [in_group(o) for o in range(1, ng)] + [along_x(o) for o in range(1, nx)]
    peers += [along_z(o) for o in range(1, nz)] + [right, left]
    for peer in peers:
        pl.semaphore_signal(barrier, inc=1, device_id=peer, device_id_type=MESH)

    row64, lane64 = iota((64, 64), 0), iota((64, 64), 1)
    eye = (row64 == lane64).astype(F32)
    ci_c.wait()
    cl_c.wait()
    for j in range(8):
        cij = ci[:, j, :]
        cis[pl.ds(j * 64, 64), :] = cij
        m = -dotf(cij, cl[:, j, :])
        Pl[pl.ds(j * 64, 64), :] = m
        e = m.T
        Zl[pl.ds(j * 64, 64), :] = e
        Xl[pl.ds(j * 64, 64), :] = e
    scan_products([Zl], 8)

    pl.semaphore_wait(barrier, len(peers))

    def gather_start(ref, own, target, count, send, recv):
        started = []
        for o in range(1, count):
            copy = pltpu.make_async_remote_copy(
                src_ref=ref.at[own],
                dst_ref=ref.at[own],
                send_sem=send.at[o],
                recv_sem=recv.at[own],
                device_id=target(o),
                device_id_type=MESH,
            )
            copy.start()
            started.append(copy)
        return started

    def gather_wait(started, ref, own, count, recv):
        for o in range(1, count):
            other = lax.rem(own + o, count)
            pltpu.make_async_copy(ref.at[other], ref.at[other], recv.at[other]).wait()
        for copy in started:
            copy.wait_send()

    RM1[g] = pack_matrix(Zl[0:64, :])
    rm1 = gather_start(RM1, g, in_group, ng, m_send.at[0], m_recv.at[0])

    lane8, lane = iota((8, 128), 1), iota((64, 128), 1)
    has_left = jnp.logical_not(jnp.logical_and(slab == 0, at_start))
    has_right = jnp.logical_not(jnp.logical_and(slab == ns - 1, at_end))

    def halo_start(turn, ref):
        to_right, to_left = jnp.zeros((8, 128), F32), jnp.zeros((8, 128), F32)
        for k in range(8):
            piece = ref[pl.ds(8 * k, 8), :]
            to_right = jnp.where(lane8 == k, pltpu.roll(piece, k + 1, 1), to_right)
            to_left = jnp.where(lane8 == k, pltpu.roll(piece, k, 1) if k else piece, to_left)
        halo_out[turn, 0] = to_right
        halo_out[turn, 1] = to_left
        started = []
        for side, peer in ((0, right), (1, left)):
            copy = pltpu.make_async_remote_copy(
                src_ref=halo_out.at[turn, side],
                dst_ref=halo_in.at[turn, side],
                send_sem=h_send.at[turn, side],
                recv_sem=h_recv.at[turn, side],
                device_id=peer,
                device_id_type=MESH,
            )
            copy.start()
            started.append(copy)
        return started

    def apply_with(value, left_of, right_of, emit):
        before, after = [], []
        for k in range(8):
            piece = value[8 * k : 8 * k + 8]
            before.append(jnp.where(lane8 == 0, left_of(k), pltpu.roll(piece, 1, 1)))
            after.append(jnp.where(lane8 == 127, right_of(k), pltpu.roll(piece, 127, 1)))
        previous = jnp.concatenate(before, axis=0) * pat[0:1, :].astype(F32)
        following = jnp.concatenate(after, axis=0) * pat[1:2, :].astype(F32)
        matvec(
            [
                (lambda a: F[1, a], value),
                (lambda a: F[0, a], previous),
                (lambda a: F[2, a], following),
            ],
            64,
            emit,
        )

    def fine_apply(turn, ref, started, emit):
        for copy in started:
            copy.wait()
        from_left = jnp.where(has_left, halo_in[turn, 0], 0.0)
        from_right = jnp.where(has_right, halo_in[turn, 1], 0.0)

        def left_of(k):
            return pltpu.roll(from_left, 128 - k, 1) if k else from_left

        def right_of(k):
            return pltpu.roll(from_right, 127 - k, 1)

        apply_with(ref[...], left_of, right_of, emit)

    def block_apply(value, emit):
        matvec([(lambda a: I[a], value)], 64, emit)

    def to_residue(rows, y):
        res[rows, :] = b[rows, :] - y

    def sweep(turn, ref, started):
        fine_apply(turn, ref, started, to_residue)

        def emit(rows, y):
            ref[rows, :] = ref[rows, :] + DAMP * y

        block_apply(res[...], emit)

    def first(rows, y):
        work[rows, :] = DAMP * y

    i_c.wait()
    b_c.wait()
    block_apply(b[...], first)
    h0 = halo_start(0, work)

    slot_c.wait()
    q, col = iota((64, 512), 0), iota((64, 512), 1)
    pick = (q == (col % 16) * 4 + col // 128).astype(BF16)
    own_block = iota((8, 512), 0) == (iota((8, 512), 1) % 128) // 16
    slots = dot1(slot[...].astype(F32).astype(BF16), pick)
    slots = row_sum(jnp.where(own_block, slots, 0.0))
    slots = jnp.concatenate([slots] * 8, axis=0)
    GT = (slots == q.astype(F32)).astype(BF16)

    def gathered(t, load):
        def one(A, unused):
            to_right, to_left = jnp.zeros((8, 128), F32), jnp.zeros((8, 128), F32)
            for u in range(8):
                whole = load(A * 8 + u)
                edge = jnp.zeros((8, 128), F32)
                for k in range(8):
                    piece = pltpu.roll(whole[8 * k : 8 * k + 8], (2 + 16 * k) % 128, 1)
                    edge = jnp.where(lane8 // 16 == k, piece, edge)
                here = (lane8 % 16) // 2 == u
                to_right = jnp.where(here, pltpu.roll(edge, 2 * u, 1) if u else edge, to_right)
                shift = (2 * u - 2) % 128
                to_left = jnp.where(here, pltpu.roll(edge, shift, 1) if shift else edge, to_left)
            msg[0, t, A] = to_right
            msg[1, t, A] = to_left
            return unused

        lax.fori_loop(0, 8, one, 0)

    f1_c.wait()
    gathered(1, lambda a: F[1, a])
    f0_c.wait()
    gathered(0, lambda a: F[0, a])
    pat_c.wait()
    f2_c.wait()
    sweep(0, work, h0)
    h1 = halo_start(1, work)

    def upward(started, ref, own, count, recv, full, masked):
        gather_wait(started, ref, own, count, recv)
        for k in range(count):
            e = unpack_matrix(ref[k])
            rows = pl.ds(k * 64, 64)
            if full is not None:
                full[rows, :] = e
            masked[rows, :] = jnp.where(k < own, e, eye)
        scan_products([masked] if full is None else [full, masked], count)

    def later(ref, h, count):
        return ref[pl.ds((h + 1) * 64, 64), :] if h + 1 < count else eye

    upward(rm1, RM1, g, ng, m_recv.at[0], Z1, Zm1)
    RM2[x] = pack_matrix(Z1[0:64, :])
    rm2 = gather_start(RM2, x, along_x, nx, m_send.at[1], m_recv.at[1])
    def weigh(ref, h, parts):
        ref[pl.ds(h * 64, 64), :] = jnp.concatenate(split(jnp.concatenate(parts, axis=1)), axis=1)

    for h in range(ng):
        weigh(W1, h, [later(Z1, h, ng), jnp.where(h < g, later(Zm1, h, ng), 0.0)])

    fine_apply(1, work, h1, to_residue)
    tent_c.wait()
    residue = res[...]
    values = []
    for m in range(4):
        weight = jnp.sum((tent[m] * residue).reshape(8, 8, 128), axis=0)
        values.append(row_sum(weight) * (1.0 / math.sqrt(64)))
    spread = jnp.where(own_block, jnp.concatenate(values, axis=1), 0.0)
    rhs = dot2(spread, GT, NT)
    offsets = diagonal(dotf(rhs, cis[...], NT), 8)
    after_own = jnp.concatenate([Zl[64:512, :], eye], axis=0)
    RV1[g] = padded(row_sum(dotf(offsets, after_own)))
    rv1 = gather_start(RV1, g, in_group, ng, v_send.at[0], v_recv.at[0])

    upward(rm2, RM2, x, nx, m_recv.at[1], Z2, Zm2)
    RM3[z] = pack_matrix(Z2[0:64, :])
    rm3 = gather_start(RM3, z, along_z, nz, m_send.at[2], m_recv.at[2])
    for h in range(nx):
        weigh(W2, h, [later(Z2, h, nx), jnp.where(h < x, later(Zm2, h, nx), 0.0)])

    own = lanes_folded(offsets)
    off_out[...] = padded(own)
    first_out[...] = pack_matrix(Pl[0:64, :])
    beside = []
    for side, peer in ((0, right), (1, left)):
        for k, (src, dst) in enumerate(
            [(work, n_s), (b, n_b), (tent, n_tent), (slot, n_slot), (pat, n_pat)]
        ):
            copy = pltpu.make_async_remote_copy(
                src_ref=src,
                dst_ref=dst.at[side],
                send_sem=n_send.at[side, k],
                recv_sem=n_recv.at[side, k],
                device_id=peer,
                device_id_type=MESH,
            )
            copy.start()
            beside.append(copy)
    for k, (src, dst) in enumerate([(first_out, n_first), (off_out, n_off)]):
        copy = pltpu.make_async_remote_copy(
            src_ref=src,
            dst_ref=dst,
            send_sem=f_send.at[k],
            recv_sem=f_recv.at[k],
            device_id=left,
            device_id_type=MESH,
        )
        copy.start()
        beside.append(copy)

    gathered(2, lambda a: F[2, a])

    def inflow(ref, weights, count):
        flat = [ref[h] + pltpu.roll(ref[h + 1], 64, 1) for h in range(0, count, 2)]
        return halves(dot2(jnp.concatenate(flat, axis=1), weights[...]))


    gather_wait(rv1, RV1, g, ng, v_recv.at[0])
    flow1 = inflow(RV1, W1, ng)
    RV2[x] = padded(flow1[:, :64])
    rv2 = gather_start(RV2, x, along_x, nx, v_send.at[1], v_recv.at[1])

    gathered(3, lambda a: I[a])
    for side, peer in ((0, right), (1, left)):
        copy = pltpu.make_async_remote_copy(
            src_ref=msg.at[side],
            dst_ref=n_mat.at[side],
            send_sem=n_send.at[side, 5],
            recv_sem=n_recv.at[side, 5],
            device_id=peer,
            device_id_type=MESH,
        )
        copy.start()
        beside.append(copy)

    scan_prefix(Pl, 8)


    gather_wait(rv2, RV2, x, nx, v_recv.at[1])
    flow2 = inflow(RV2, W2, nx)
    RV3[z] = padded(flow2[:, :64])
    rv3 = gather_start(RV3, z, along_z, nz, v_send.at[2], v_recv.at[2])

    upward(rm3, RM3, z, nz, m_recv.at[2], None, Zm3)
    A1 = Zm1[0:64, :]
    A21 = dotf(Zm2[0:64, :], A1)
    for h in range(nz):
        weigh(W3, h, [dotf(jnp.where(h < z, later(Zm3, h, nz), 0.0), A21)])

    row8 = iota((8, 64), 0)
    carried = jnp.broadcast_to(own[0:1], (8, 64))
    local = carried
    for j in range(1, 8):
        carried = dotf(carried, Xl[pl.ds(j * 64, 64), :]) + own[j : j + 1]
        local = jnp.where(row8 >= j, carried, local)
    nearer = dotf(flow2[:, 64:], A1) + flow1[:, 64:]
    for copy in beside:
        copy.wait()
    spot = lane % 16
    valid = jnp.logical_or(
        jnp.logical_and(spot < 3, has_left),
        jnp.logical_and(jnp.logical_and(spot >= 8, spot < 11), has_right),
    )

    def repeated(v):
        for shift in (16, 32, 64):
            v = v + pltpu.roll(v, shift, 1)
        return v

    def beyond(from_left, from_right):
        at = iota(from_left.shape, 1)
        mine = jnp.where(at < 3, pltpu.roll(from_left, 3, 1), 0.0)
        return jnp.where(jnp.logical_and(at >= 8, at < 11), pltpu.roll(from_right, 8, 1), mine)

    def own_ends(ref):
        first_own = jnp.where(lane == 3, pltpu.roll(ref[...], 3, 1), 0.0)
        return jnp.where(lane == 7, pltpu.roll(ref[...], 8, 1), first_own)

    b_halo = repeated(beyond(n_b[0], n_b[1]))
    s_halo = repeated(beyond(n_s[0], n_s[1]))
    tent_halo = [beyond(n_tent[0, m], n_tent[1, m]) for m in range(4)]
    pat_halo = []
    for r in range(2):
        rows = [jnp.broadcast_to(n_pat[e, r : r + 1, :].astype(F32), (8, 128)) for e in range(2)]
        pat_halo.append(jnp.concatenate([repeated(beyond(*rows))] * 8, axis=0))

    def placed(A, unused):
        for t in range(4):
            from_left, from_right = n_mat[0, t, A], n_mat[1, t, A]
            place = lane8 % 16
            at_left = jnp.logical_or(place == 1, place == 2)
            at_right = jnp.logical_or(place == 8, place == 9)
            for u in range(8):
                p = jnp.where(at_left, pltpu.roll(from_left, (1 - 2 * u) % 128, 1), 0.0)
                shift = (8 - 2 * u) % 128
                q = pltpu.roll(from_right, shift, 1) if shift else from_right
                Hc[t, A * 8 + u] = jnp.where(at_right, q, p)
        return unused

    lax.fori_loop(0, 8, placed, 0)

    place = iota((64, 512), 1) % 128
    asked = jnp.where(place < 3, place + 13, place - 8) * 4 + col // 128
    pick_halo = (q == asked).astype(BF16)
    ends = jnp.concatenate([n_slot[0, 7:8, :], n_slot[1, 0:1, :]] + [n_slot[1, 0:1, :]] * 6, axis=0)
    slots = dot1(ends.astype(F32).astype(BF16), pick_halo)
    which = (iota((8, 512), 1) % 128 >= 8).astype(jnp.int32) == iota((8, 512), 0)
    slots = row_sum(jnp.where(which, slots, 0.0))
    GT_halo = (jnp.concatenate([slots] * 8, axis=0) == q.astype(F32)).astype(BF16)
    M_next = unpack_matrix(n_first[...])
    P_next = dotf(M_next, Pl[448:512, :])
    local_next = dotf(carried, M_next, NT) + n_off[0:1, :64]

    def halo_matvec(terms, finish):
        packed = []
        for t, v in terms:
            p = jnp.zeros((8, 128), F32)
            for k in range(8):
                p = jnp.where(lane8 // 16 == k, v[8 * k : 8 * k + 8], p)
            packed.append((t, p))

        def one(A, unused):
            parts = []
            for u in range(8):
                total = None
                for t, p in packed:
                    term = Hc[t, A * 8 + u] * p
                    total = term if total is None else total + term
                parts.append(total)
            finish(pl.ds(pl.multiple_of(A * 8, 8), 8), repeated(fold_rows(parts)))
            return unused

        lax.fori_loop(0, 8, one, 0)

    def halo_apply(v, finish):
        halo_matvec(
            [
                (1, v),
                (0, pltpu.roll(v, 1, 1) * pat_halo[0]),
                (2, pltpu.roll(v, 127, 1) * pat_halo[1]),
            ],
            finish,
        )

    gather_wait(rv3, RV3, z, nz, v_recv.at[2])
    incoming = inflow(RV3, W3, nz) + nearer

    coarse = local + lanes_folded(diagonal(dotf(incoming, Pl[...], NT), 8))
    ce_ref[...] = coarse
    weights = jnp.where(own_block, dot2(coarse, GT), 0.0)
    total = None
    for m in range(4):
        w = row_sum(weights[:, m * 128 : m * 128 + 128]) * (1.0 / math.sqrt(64))
        term = tent[m] * jnp.concatenate([w] * 8, axis=0)
        total = term if total is None else total + term
    corr[...] = total
    next_first = dotf(incoming, P_next, NT) + local_next
    two = jnp.concatenate([incoming[0:1], next_first[0:1]] + [next_first[0:1]] * 6, axis=0)
    weights = jnp.where(which, dot2(two, GT_halo), 0.0)
    total = None
    for m in range(4):
        w = row_sum(weights[:, m * 128 : m * 128 + 128]) * (1.0 / math.sqrt(64))
        term = tent_halo[m] * jnp.concatenate([w] * 8, axis=0)
        total = term if total is None else total + term
    c_halo = repeated(jnp.where(valid, total, 0.0) + own_ends(corr))

    def post(ref, halo, emit):
        def left_of(k):
            return pltpu.roll(halo[8 * k : 8 * k + 8], 126, 1)

        def right_of(k):
            return pltpu.roll(halo[8 * k : 8 * k + 8], 119, 1)

        apply_with(ref[...], left_of, right_of, emit)

    def to_res(rows, y):
        res[rows, :] = y

    def to_halo(rows, y):
        chalo[rows, :] = y

    post(corr, c_halo, to_res)

    def prolong(rows, y):
        sol_ref[rows, :] = work[rows, :] + corr[rows, :] - SMOOTH * y

    block_apply(res[...], prolong)
    halo_apply(c_halo, to_halo)
    halo_matvec([(3, chalo[...])], to_halo)
    s_halo = jnp.where(valid, s_halo + c_halo - SMOOTH * chalo[...], 0.0)
    s_ends = s_halo + repeated(own_ends(sol_ref))

    def smooth(rows, y):
        sol_ref[rows, :] = sol_ref[rows, :] + DAMP * y

    post(sol_ref, s_ends, to_residue)
    block_apply(res[...], smooth)
    halo_apply(s_ends, to_halo)
    halo_matvec([(3, b_halo - chalo[...])], to_halo)
    s_halo = jnp.where(valid, s_halo + DAMP * chalo[...], 0.0)
    post(sol_ref, s_halo, to_residue)
    block_apply(res[...], smooth)


def body(nz, nx, ng, right_side, fine_blocks, fine_inverse, pattern, tentative, slot_map, coarse_inverse, coarse_lower):
    vmem = lambda *shape: pltpu.VMEM(shape, F32)
    dma = lambda *shape: pltpu.SemaphoreType.DMA(shape)
    top = max(nz, nx, ng)
    scratch = [
        vmem(3, 64, 64, 128), vmem(64, 64, 128), vmem(64, 128), pltpu.VMEM((2, 128), jnp.int32), vmem(4, 64, 128),
        pltpu.VMEM((8, 64), jnp.int32), vmem(64, 8, 64), vmem(64, 8, 64),
        vmem(64, 128), vmem(64, 128), vmem(64, 128),
        vmem(512, 64), vmem(512, 64), vmem(512, 64), vmem(ng * 64, 64), vmem(ng * 64, 64),
        vmem(nx * 64, 64), vmem(nx * 64, 64), vmem(nz * 64, 64),
        vmem(512, 64),
        pltpu.VMEM((ng * 64, 256), BF16), pltpu.VMEM((nx * 64, 256), BF16), pltpu.VMEM((nz * 64, 128), BF16),
        vmem(ng, 32, 128), vmem(nx, 32, 128), vmem(nz, 32, 128),
        vmem(ng, 8, 128), vmem(nx, 8, 128), vmem(nz, 8, 128),
        vmem(2, 2, 8, 128), vmem(2, 2, 8, 128),
        vmem(4, 64, 8, 128), vmem(2, 4, 8, 8, 128), vmem(2, 4, 8, 8, 128), vmem(2, 4, 64, 128), vmem(2, 64, 128),
        vmem(2, 64, 128), pltpu.VMEM((2, 8, 64), jnp.int32), pltpu.VMEM((2, 2, 128), jnp.int32),
        vmem(32, 128), vmem(8, 128), vmem(8, 128), vmem(64, 128), vmem(32, 128),
        dma(10), dma(3, top), dma(3, top), dma(3, top), dma(3, top), dma(2, 2), dma(2, 2),
        dma(2, 6), dma(2, 6), dma(2), dma(2),
    ]
    result, coarse = pl.pallas_call(
        functools.partial(kernel, nz, nx, ng),
        out_shape=(
            jax.ShapeDtypeStruct((64, 128), F32),
            jax.ShapeDtypeStruct((8, 64), F32),
        ),
        in_specs=[pl.BlockSpec(memory_space=pl.ANY)] * 8,
        out_specs=(
            pl.BlockSpec(memory_space=pltpu.VMEM),
            pl.BlockSpec(memory_space=pltpu.VMEM),
        ),
        scratch_shapes=scratch,
        compiler_params=pltpu.CompilerParams(
            collective_id=0, has_side_effects=True, vmem_limit_bytes=60 * 2**20
        ),
        name="v_cycle",
    )(
        right_side, fine_blocks, fine_inverse, pattern, tentative, slot_map,
        jnp.transpose(coarse_inverse, (0, 2, 1)), jnp.transpose(coarse_lower, (0, 2, 1)),
    )
    return result, coarse.T


def solution(mesh):
    slabs, ng = mesh.shape["slab"], mesh.shape["group"]
    nx = 4 if slabs % 4 == 0 and slabs > 4 else 2
    both = ("slab", "group")
    in_specs = (
        P(None, both), P(None, None, None, both), P(None, None, both), P(None, both), P(None, None, both),
        P(both, None), P(None, None, both), P(None, None, both),
    )
    return jax.shard_map(
        functools.partial(body, slabs // nx, nx, ng),
        mesh=mesh,
        in_specs=in_specs,
        out_specs=(P(None, both), P(None, both)),
        check_vma=False,
    )
```

```python
import functools
import math

import jax
import jax.numpy as jnp
from jax import lax
from jax.experimental import pallas as pl
from jax.experimental.pallas import tpu as pltpu
from jax.sharding import PartitionSpec as P

DAMP = 0.8
SMOOTH = 0.67
F32 = jnp.float32
BF16 = jnp.bfloat16
MESH = pl.DeviceIdType.MESH

NN = (((1,), (0,)), ((), ()))
NT = (((1,), (1,)), ((), ()))


def split(x):
    hi = x.astype(BF16)
    return hi, (x - hi.astype(F32)).astype(BF16)


def dot1(a, b, dims=NN):
    return lax.dot_general(a, b, dims, preferred_element_type=F32)


def halves(t):
    n = t.shape[1] // 2
    return t[:, :n] + t[:, n:]


def dotf(a, b, dims=NN):
    return lax.dot_general(a, b, dims, precision=lax.Precision.HIGHEST, preferred_element_type=F32)


def dot2(a, b, dims=NN):
    t = dot1(jnp.concatenate(split(a), axis=0), b, dims)
    return t[: a.shape[0]] + t[a.shape[0] :]


def iota(shape, dim):
    return lax.broadcasted_iota(jnp.int32, shape, dim)


def fold(parts, axis):
    step = 1 if axis == 0 else 16
    at = iota((8, 128), axis) // step

    def mix(a, b, mask, shift):
        return jnp.where(mask, a, b) + pltpu.roll(jnp.where(mask, b, a), shift * step, axis)

    q = [parts[(i + 3) % 8] for i in range(8)]
    y = [mix(q[k], q[k + 4], ((at - k) & 7) < 4, 4) for k in range(4)]
    z = [mix(y[k], y[k + 2], ((at - k) & 3) >= 2, 2) for k in range(2)]
    return mix(z[0], z[1], (at & 1) == 1, 1)


def row_sum(x):
    x = x + pltpu.roll(x, 4, 0)
    x = x + pltpu.roll(x, 2, 0)
    return x + pltpu.roll(x, 1, 0)


def matvec(terms, width, emit):
    def one(g, unused):
        parts = []
        for a in range(8):
            total = None
            for load, v in terms:
                product = load(g * 8 + a) * v
                total = product if total is None else total + product
            parts.append(jnp.sum(total.reshape(width // 8, 8, 128), axis=0))
        emit(pl.ds(pl.multiple_of(g * 8, 8), 8), fold(parts, 0))
        return unused

    lax.fori_loop(0, width // 8, one, 0)


def pack_matrix(m):
    return jnp.concatenate([m[:32, :], m[32:, :]], axis=1)


def unpack_matrix(p):
    return jnp.concatenate([p[:, :64], p[:, 64:]], axis=0)


def scan_products(refs, count):
    half = 1
    while half < count:
        for start in range(0, count, 2 * half):
            mid = start + half
            left = pl.ds(start * 64, half * 64)
            for ref in refs:
                ref[left, :] = dotf(ref[left, :], ref[pl.ds(mid * 64, 64), :])
        half *= 2


def scan_prefix(ref, count):
    half = 1
    while half < count:
        for start in range(0, count, 2 * half):
            mid = start + half
            right = pl.ds(mid * 64, half * 64)
            ref[right, :] = dotf(ref[right, :], ref[pl.ds((mid - 1) * 64, 64), :])
        half *= 2


def diagonal(x, count):
    return jnp.where(iota(x.shape, 0) == iota(x.shape, 1) // 64, x, 0.0)


def lanes_folded(x):
    t = x[:, 0:128] + x[:, 128:256] + x[:, 256:384] + x[:, 384:512]
    return t[:, :64] + t[:, 64:]


def padded(x):
    return jnp.concatenate([x, jnp.zeros_like(x)], axis=1)


def kernel(
    nz, nx, ng,
    b_h, f_h, i_h, pat_h, tent_h, slot_h, ci_h, cl_h,
    sol_ref, ce_ref,
    F, I, b, pat, tent, slot, ci, cl,
    work, res, corr,
    cis, Zl, Pl, Z1, Zm1, Z2, Zm2, Zm3,
    Xl, W1, W2, W3,
    RM1, RM2, RM3, RV1, RV2, RV3, halo_out, halo_in,
    Hc, msg, n_mat, n_tent, n_b, n_s, n_slot, n_pat, n_first, n_off, off_out, first_out,
    load_sem, m_send, m_recv, v_send, v_recv, h_send, h_recv, n_send, n_recv, f_send, f_recv,
):
    slab, g = lax.axis_index("slab"), lax.axis_index("group")
    z, x = slab // nx, slab % nx
    ns = nz * nx

    copies = []
    for k, (src, dst) in enumerate(
        [(ci_h, ci), (cl_h, cl), (i_h, I), (b_h, b), (slot_h, slot), (pat_h, pat),
         (f_h.at[1], F.at[1]), (f_h.at[0], F.at[0]), (f_h.at[2], F.at[2]), (tent_h, tent)]
    ):
        copy = pltpu.make_async_copy(src, dst, load_sem.at[k])
        copy.start()
        copies.append(copy)
    ci_c, cl_c, i_c, b_c, slot_c, pat_c, f1_c, f0_c, f2_c, tent_c = copies

    def in_group(o):
        return (slab, lax.rem(g + o, ng))

    def along_x(o):
        return (z * nx + lax.rem(x + o, nx), g)

    def along_z(o):
        return (lax.rem(z + o, nz) * nx + x, g)

    at_end, at_start = g == ng - 1, g == 0
    right = (jnp.where(at_end, lax.rem(slab + 1, ns), slab), lax.rem(g + 1, ng))
    left = (jnp.where(at_start, lax.rem(slab + ns - 1, ns), slab), lax.rem(g + ng - 1, ng))

    barrier = pltpu.get_barrier_semaphore()
    peers = [in_group(o) for o in range(1, ng)] + [along_x(o) for o in range(1, nx)]
    peers += [along_z(o) for o in range(1, nz)] + [right, left]
    for peer in peers:
        pl.semaphore_signal(barrier, inc=1, device_id=peer, device_id_type=MESH)

    row64, lane64 = iota((64, 64), 0), iota((64, 64), 1)
    eye = (row64 == lane64).astype(F32)
    ci_c.wait()
    cl_c.wait()
    for j in range(8):
        cij = ci[:, j, :]
        cis[pl.ds(j * 64, 64), :] = cij
        m = -dotf(cij, cl[:, j, :])
        Pl[pl.ds(j * 64, 64), :] = m
        e = m.T
        Zl[pl.ds(j * 64, 64), :] = e
        Xl[pl.ds(j * 64, 64), :] = e
    scan_products([Zl], 8)

    pl.semaphore_wait(barrier, len(peers))

    def gather_start(ref, own, target, count, send, recv):
        started = []
        for o in range(1, count):
            copy = pltpu.make_async_remote_copy(
                src_ref=ref.at[own],
                dst_ref=ref.at[own],
                send_sem=send.at[o],
                recv_sem=recv.at[own],
                device_id=target(o),
                device_id_type=MESH,
            )
            copy.start()
            started.append(copy)
        return started

    def gather_wait(started, ref, own, count, recv):
        for o in range(1, count):
            other = lax.rem(own + o, count)
            pltpu.make_async_copy(ref.at[other], ref.at[other], recv.at[other]).wait()
        for copy in started:
            copy.wait_send()

    RM1[g] = pack_matrix(Zl[0:64, :])
    rm1 = gather_start(RM1, g, in_group, ng, m_send.at[0], m_recv.at[0])

    lane8, lane = iota((8, 128), 1), iota((64, 128), 1)
    has_left = jnp.logical_not(jnp.logical_and(slab == 0, at_start))
    has_right = jnp.logical_not(jnp.logical_and(slab == ns - 1, at_end))

    def halo_start(turn, ref):
        to_right, to_left = jnp.zeros((8, 128), F32), jnp.zeros((8, 128), F32)
        for k in range(8):
            piece = ref[pl.ds(8 * k, 8), :]
            to_right = jnp.where(lane8 == k, pltpu.roll(piece, k + 1, 1), to_right)
            to_left = jnp.where(lane8 == k, pltpu.roll(piece, k, 1) if k else piece, to_left)
        halo_out[turn, 0] = to_right
        halo_out[turn, 1] = to_left
        started = []
        for side, peer in ((0, right), (1, left)):
            copy = pltpu.make_async_remote_copy(
                src_ref=halo_out.at[turn, side],
                dst_ref=halo_in.at[turn, side],
                send_sem=h_send.at[turn, side],
                recv_sem=h_recv.at[turn, side],
                device_id=peer,
                device_id_type=MESH,
            )
            copy.start()
            started.append(copy)
        return started

    def apply_with(value, left_of, right_of, emit):
        before, after = [], []
        for k in range(8):
            piece = value[8 * k : 8 * k + 8]
            before.append(jnp.where(lane8 == 0, left_of(k), pltpu.roll(piece, 1, 1)))
            after.append(jnp.where(lane8 == 127, right_of(k), pltpu.roll(piece, 127, 1)))
        previous = jnp.concatenate(before, axis=0) * pat[0:1, :].astype(F32)
        following = jnp.concatenate(after, axis=0) * pat[1:2, :].astype(F32)
        matvec(
            [
                (lambda a: F[1, a], value),
                (lambda a: F[0, a], previous),
                (lambda a: F[2, a], following),
            ],
            64,
            emit,
        )

    def fine_apply(turn, ref, started, emit):
        for copy in started:
            copy.wait()
        from_left = jnp.where(has_left, halo_in[turn, 0], 0.0)
        from_right = jnp.where(has_right, halo_in[turn, 1], 0.0)

        def left_of(k):
            return pltpu.roll(from_left, 128 - k, 1) if k else from_left

        def right_of(k):
            return pltpu.roll(from_right, 127 - k, 1)

        apply_with(ref[...], left_of, right_of, emit)

    def block_apply(value, emit):
        matvec([(lambda a: I[a], value)], 64, emit)

    def to_residue(rows, y):
        res[rows, :] = b[rows, :] - y

    def sweep(turn, ref, started):
        fine_apply(turn, ref, started, to_residue)

        def emit(rows, y):
            ref[rows, :] = ref[rows, :] + DAMP * y

        block_apply(res[...], emit)

    def first(rows, y):
        work[rows, :] = DAMP * y

    i_c.wait()
    b_c.wait()
    block_apply(b[...], first)
    h0 = halo_start(0, work)

    slot_c.wait()
    q, col = iota((64, 512), 0), iota((64, 512), 1)
    pick = (q == (col % 16) * 4 + col // 128).astype(BF16)
    own_block = iota((8, 512), 0) == (iota((8, 512), 1) % 128) // 16
    slots = dot1(slot[...].astype(F32).astype(BF16), pick)
    slots = row_sum(jnp.where(own_block, slots, 0.0))
    slots = jnp.concatenate([slots] * 8, axis=0)
    GT = (slots == q.astype(F32)).astype(BF16)

    def gathered(t, load):
        def one(A, unused):
            to_right, to_left = jnp.zeros((8, 128), F32), jnp.zeros((8, 128), F32)
            for u in range(8):
                whole = load(A * 8 + u)
                edge = jnp.zeros((8, 128), F32)
                for k in range(8):
                    piece = pltpu.roll(whole[8 * k : 8 * k + 8], (2 + 16 * k) % 128, 1)
                    edge = jnp.where(lane8 // 16 == k, piece, edge)
                here = (lane8 % 16) // 2 == u
                to_right = jnp.where(here, pltpu.roll(edge, 2 * u, 1) if u else edge, to_right)
                shift = (2 * u - 2) % 128
                to_left = jnp.where(here, pltpu.roll(edge, shift, 1) if shift else edge, to_left)
            msg[0, t, A] = to_right
            msg[1, t, A] = to_left
            return unused

        lax.fori_loop(0, 8, one, 0)

    f1_c.wait()
    gathered(1, lambda a: F[1, a])
    f0_c.wait()
    gathered(0, lambda a: F[0, a])
    pat_c.wait()
    f2_c.wait()
    sweep(0, work, h0)
    h1 = halo_start(1, work)

    def upward(started, ref, own, count, recv, full, masked):
        gather_wait(started, ref, own, count, recv)
        for k in range(count):
            e = unpack_matrix(ref[k])
            rows = pl.ds(k * 64, 64)
            if full is not None:
                full[rows, :] = e
            masked[rows, :] = jnp.where(k < own, e, eye)
        scan_products([masked] if full is None else [full, masked], count)

    def later(ref, h, count):
        return ref[pl.ds((h + 1) * 64, 64), :] if h + 1 < count else eye

    upward(rm1, RM1, g, ng, m_recv.at[0], Z1, Zm1)
    RM2[x] = pack_matrix(Z1[0:64, :])
    rm2 = gather_start(RM2, x, along_x, nx, m_send.at[1], m_recv.at[1])
    def weigh(ref, h, parts):
        ref[pl.ds(h * 64, 64), :] = jnp.concatenate(split(jnp.concatenate(parts, axis=1)), axis=1)

    for h in range(ng):
        weigh(W1, h, [later(Z1, h, ng), jnp.where(h < g, later(Zm1, h, ng), 0.0)])

    fine_apply(1, work, h1, to_residue)
    tent_c.wait()
    residue = res[...]
    values = []
    for m in range(4):
        weight = jnp.sum((tent[m] * residue).reshape(8, 8, 128), axis=0)
        values.append(row_sum(weight) * (1.0 / math.sqrt(64)))
    spread = jnp.where(own_block, jnp.concatenate(values, axis=1), 0.0)
    rhs = dot2(spread, GT, NT)
    offsets = diagonal(dotf(rhs, cis[...], NT), 8)
    after_own = jnp.concatenate([Zl[64:512, :], eye], axis=0)
    RV1[g] = padded(row_sum(dotf(offsets, after_own)))
    rv1 = gather_start(RV1, g, in_group, ng, v_send.at[0], v_recv.at[0])

    upward(rm2, RM2, x, nx, m_recv.at[1], Z2, Zm2)
    RM3[z] = pack_matrix(Z2[0:64, :])
    rm3 = gather_start(RM3, z, along_z, nz, m_send.at[2], m_recv.at[2])
    for h in range(nx):
        weigh(W2, h, [later(Z2, h, nx), jnp.where(h < x, later(Zm2, h, nx), 0.0)])

    own = lanes_folded(offsets)
    off_out[...] = padded(own)
    first_out[...] = pack_matrix(Pl[0:64, :])
    beside = []
    for side, peer in ((0, right), (1, left)):
        for k, (src, dst) in enumerate(
            [(work, n_s), (b, n_b), (tent, n_tent), (slot, n_slot), (pat, n_pat)]
        ):
            copy = pltpu.make_async_remote_copy(
                src_ref=src,
                dst_ref=dst.at[side],
                send_sem=n_send.at[side, k],
                recv_sem=n_recv.at[side, k],
                device_id=peer,
                device_id_type=MESH,
            )
            copy.start()
            beside.append(copy)
    for k, (src, dst) in enumerate([(first_out, n_first), (off_out, n_off)]):
        copy = pltpu.make_async_remote_copy(
            src_ref=src,
            dst_ref=dst,
            send_sem=f_send.at[k],
            recv_sem=f_recv.at[k],
            device_id=left,
            device_id_type=MESH,
        )
        copy.start()
        beside.append(copy)

    gathered(2, lambda a: F[2, a])

    def inflow(ref, weights, count):
        flat = [ref[h] + pltpu.roll(ref[h + 1], 64, 1) for h in range(0, count, 2)]
        return halves(dot2(jnp.concatenate(flat, axis=1), weights[...]))


    gather_wait(rv1, RV1, g, ng, v_recv.at[0])
    flow1 = inflow(RV1, W1, ng)
    RV2[x] = padded(flow1[:, :64])
    rv2 = gather_start(RV2, x, along_x, nx, v_send.at[1], v_recv.at[1])

    gathered(3, lambda a: I[a])
    for side, peer in ((0, right), (1, left)):
        copy = pltpu.make_async_remote_copy(
            src_ref=msg.at[side],
            dst_ref=n_mat.at[side],
            send_sem=n_send.at[side, 5],
            recv_sem=n_recv.at[side, 5],
            device_id=peer,
            device_id_type=MESH,
        )
        copy.start()
        beside.append(copy)

    scan_prefix(Pl, 8)


    gather_wait(rv2, RV2, x, nx, v_recv.at[1])
    flow2 = inflow(RV2, W2, nx)
    RV3[z] = padded(flow2[:, :64])
    rv3 = gather_start(RV3, z, along_z, nz, v_send.at[2], v_recv.at[2])

    upward(rm3, RM3, z, nz, m_recv.at[2], None, Zm3)
    A1 = Zm1[0:64, :]
    A21 = dotf(Zm2[0:64, :], A1)
    for h in range(nz):
        weigh(W3, h, [dotf(jnp.where(h < z, later(Zm3, h, nz), 0.0), A21)])

    row8 = iota((8, 64), 0)
    carried = jnp.broadcast_to(own[0:1], (8, 64))
    local = carried
    for j in range(1, 8):
        carried = dotf(carried, Xl[pl.ds(j * 64, 64), :]) + own[j : j + 1]
        local = jnp.where(row8 >= j, carried, local)
    nearer = dotf(flow2[:, 64:], A1) + flow1[:, 64:]
    for copy in beside:
        copy.wait()
    group, spot = lane8 // 16, lane8 % 16
    at_right = jnp.logical_and(spot >= 8, spot < 11)
    valid = jnp.logical_or(jnp.logical_and(spot < 3, has_left), jnp.logical_and(at_right, has_right))

    def gather_lanes(pieces, shift, mask, out):
        for k in range(8):
            moved = pltpu.roll(pieces(k), shift + 16 * k, 1)
            out = jnp.where(jnp.logical_and(group == k, mask), moved, out)
        return out

    nothing = jnp.zeros((8, 128), F32)

    def beyond(ref, *at):
        left_ref, right_ref = ref.at[(0, *at)], ref.at[(1, *at)]
        out = gather_lanes(lambda k: left_ref[pl.ds(8 * k, 8), :], 3, spot < 3, nothing)
        return gather_lanes(lambda k: right_ref[pl.ds(8 * k, 8), :], 8, at_right, out)

    def own_ends(ref, out):
        out = gather_lanes(lambda k: ref[pl.ds(8 * k, 8), :], 3, spot == 3, out)
        return gather_lanes(lambda k: ref[pl.ds(8 * k, 8), :], 8, spot == 7, out)

    b_halo = beyond(n_b)
    s_halo = beyond(n_s)
    tent_halo = [beyond(n_tent, m) for m in range(4)]
    pat_halo = []
    for r in range(2):
        rows = [jnp.broadcast_to(n_pat[e, r : r + 1, :].astype(F32), (8, 128)) for e in range(2)]
        out = gather_lanes(lambda k: rows[0], 3, spot < 3, nothing)
        pat_halo.append(gather_lanes(lambda k: rows[1], 8, at_right, out))

    def placed(A, unused):
        for t in range(4):
            from_left, from_right = n_mat[0, t, A], n_mat[1, t, A]
            at_two_left = jnp.logical_or(spot == 1, spot == 2)
            at_two_right = jnp.logical_or(spot == 8, spot == 9)
            for u in range(8):
                p = jnp.where(at_two_left, pltpu.roll(from_left, (1 - 2 * u) % 128, 1), 0.0)
                shift = (8 - 2 * u) % 128
                q = pltpu.roll(from_right, shift, 1) if shift else from_right
                Hc[t, A * 8 + u] = jnp.where(at_two_right, q, p)
        return unused

    lax.fori_loop(0, 8, placed, 0)

    place = iota((64, 512), 1) % 16
    asked = jnp.where(place < 3, place + 13, place - 8) * 4 + col // 128
    pick_halo = (q == asked).astype(BF16)
    ends = jnp.concatenate([n_slot[0, 7:8, :], n_slot[1, 0:1, :]] + [n_slot[1, 0:1, :]] * 6, axis=0)
    slots = dot1(ends.astype(F32).astype(BF16), pick_halo)
    which = (iota((8, 512), 1) % 16 >= 8).astype(jnp.int32) == iota((8, 512), 0)
    slots = row_sum(jnp.where(which, slots, 0.0))
    GT_halo = (jnp.concatenate([slots] * 8, axis=0) == q.astype(F32)).astype(BF16)
    M_next = unpack_matrix(n_first[...])
    P_next = dotf(M_next, Pl[448:512, :])
    local_next = dotf(carried, M_next, NT) + n_off[0:1, :64]

    def halo_matvec(terms):
        rows = []
        for A in range(8):
            parts = []
            for u in range(8):
                total = None
                for t, v in terms:
                    term = Hc[t, A * 8 + u] * v
                    total = term if total is None else total + term
                parts.append(total)
            rows.append(fold(parts, 0))
        return fold(rows, 1)

    def halo_apply(v):
        return halo_matvec([(1, v), (0, pltpu.roll(v, 1, 1) * pat_halo[0]), (2, pltpu.roll(v, 127, 1) * pat_halo[1])])

    gather_wait(rv3, RV3, z, nz, v_recv.at[2])
    incoming = inflow(RV3, W3, nz) + nearer

    coarse = local + lanes_folded(diagonal(dotf(incoming, Pl[...], NT), 8))
    ce_ref[...] = coarse
    weights = jnp.where(own_block, dot2(coarse, GT), 0.0)
    total = None
    for m in range(4):
        w = row_sum(weights[:, m * 128 : m * 128 + 128]) * (1.0 / math.sqrt(64))
        term = tent[m] * jnp.concatenate([w] * 8, axis=0)
        total = term if total is None else total + term
    corr[...] = total
    next_first = dotf(incoming, P_next, NT) + local_next
    two = jnp.concatenate([incoming[0:1], next_first[0:1]] + [next_first[0:1]] * 6, axis=0)
    weights = jnp.where(which, dot2(two, GT_halo), 0.0)
    total = None
    for m in range(4):
        w = row_sum(weights[:, m * 128 : m * 128 + 128]) * (1.0 / math.sqrt(64))
        term = tent_halo[m] * w
        total = term if total is None else total + term
    c_halo = own_ends(corr, jnp.where(valid, total, 0.0))

    def post(ref, halo, emit):
        def left_of(k):
            return pltpu.roll(halo, 126 - 16 * k, 1)

        def right_of(k):
            return pltpu.roll(halo, 119 - 16 * k, 1)

        apply_with(ref[...], left_of, right_of, emit)

    def to_res(rows, y):
        res[rows, :] = y

    post(corr, c_halo, to_res)

    def prolong(rows, y):
        sol_ref[rows, :] = work[rows, :] + corr[rows, :] - SMOOTH * y

    block_apply(res[...], prolong)
    s_halo = s_halo + c_halo - SMOOTH * halo_matvec([(3, halo_apply(c_halo))])
    s_halo = jnp.where(valid, s_halo, 0.0)
    s_ends = own_ends(sol_ref, s_halo)

    def smooth(rows, y):
        sol_ref[rows, :] = sol_ref[rows, :] + DAMP * y

    post(sol_ref, s_ends, to_residue)
    block_apply(res[...], smooth)
    s_halo = s_halo + DAMP * halo_matvec([(3, b_halo - halo_apply(s_ends))])
    s_halo = jnp.where(valid, s_halo, 0.0)
    post(sol_ref, s_halo, to_residue)
    block_apply(res[...], smooth)


def body(nz, nx, ng, right_side, fine_blocks, fine_inverse, pattern, tentative, slot_map, coarse_inverse, coarse_lower):
    vmem = lambda *shape: pltpu.VMEM(shape, F32)
    dma = lambda *shape: pltpu.SemaphoreType.DMA(shape)
    top = max(nz, nx, ng)
    scratch = [
        vmem(3, 64, 64, 128), vmem(64, 64, 128), vmem(64, 128), pltpu.VMEM((2, 128), jnp.int32), vmem(4, 64, 128),
        pltpu.VMEM((8, 64), jnp.int32), vmem(64, 8, 64), vmem(64, 8, 64),
        vmem(64, 128), vmem(64, 128), vmem(64, 128),
        vmem(512, 64), vmem(512, 64), vmem(512, 64), vmem(ng * 64, 64), vmem(ng * 64, 64),
        vmem(nx * 64, 64), vmem(nx * 64, 64), vmem(nz * 64, 64),
        vmem(512, 64),
        pltpu.VMEM((ng * 64, 256), BF16), pltpu.VMEM((nx * 64, 256), BF16), pltpu.VMEM((nz * 64, 128), BF16),
        vmem(ng, 32, 128), vmem(nx, 32, 128), vmem(nz, 32, 128),
        vmem(ng, 8, 128), vmem(nx, 8, 128), vmem(nz, 8, 128),
        vmem(2, 2, 8, 128), vmem(2, 2, 8, 128),
        vmem(4, 64, 8, 128), vmem(2, 4, 8, 8, 128), vmem(2, 4, 8, 8, 128), vmem(2, 4, 64, 128), vmem(2, 64, 128),
        vmem(2, 64, 128), pltpu.VMEM((2, 8, 64), jnp.int32), pltpu.VMEM((2, 2, 128), jnp.int32),
        vmem(32, 128), vmem(8, 128), vmem(8, 128), vmem(32, 128),
        dma(10), dma(3, top), dma(3, top), dma(3, top), dma(3, top), dma(2, 2), dma(2, 2),
        dma(2, 6), dma(2, 6), dma(2), dma(2),
    ]
    result, coarse = pl.pallas_call(
        functools.partial(kernel, nz, nx, ng),
        out_shape=(
            jax.ShapeDtypeStruct((64, 128), F32),
            jax.ShapeDtypeStruct((8, 64), F32),
        ),
        in_specs=[pl.BlockSpec(memory_space=pl.ANY)] * 8,
        out_specs=(
            pl.BlockSpec(memory_space=pltpu.VMEM),
            pl.BlockSpec(memory_space=pltpu.VMEM),
        ),
        scratch_shapes=scratch,
        compiler_params=pltpu.CompilerParams(
            collective_id=0, has_side_effects=True, vmem_limit_bytes=60 * 2**20
        ),
        name="v_cycle",
    )(
        right_side, fine_blocks, fine_inverse, pattern, tentative, slot_map,
        jnp.transpose(coarse_inverse, (0, 2, 1)), jnp.transpose(coarse_lower, (0, 2, 1)),
    )
    return result, coarse.T


def solution(mesh):
    slabs, ng = mesh.shape["slab"], mesh.shape["group"]
    nx = 4 if slabs % 4 == 0 and slabs > 4 else 2
    both = ("slab", "group")
    in_specs = (
        P(None, both), P(None, None, None, both), P(None, None, both), P(None, both), P(None, None, both),
        P(both, None), P(None, None, both), P(None, None, both),
    )
    return jax.shard_map(
        functools.partial(body, slabs // nx, nx, ng),
        mesh=mesh,
        in_specs=in_specs,
        out_specs=(P(None, both), P(None, both)),
        check_vma=False,
    )
```

```python
import functools
import math

import jax
import jax.numpy as jnp
from jax import lax
from jax.experimental import pallas as pl
from jax.experimental.pallas import tpu as pltpu
from jax.sharding import PartitionSpec as P

DAMP = 0.8
SMOOTH = 0.67
F32 = jnp.float32
BF16 = jnp.bfloat16
MESH = pl.DeviceIdType.MESH

NN = (((1,), (0,)), ((), ()))
NT = (((1,), (1,)), ((), ()))


def split(x):
    hi = x.astype(BF16)
    return hi, (x - hi.astype(F32)).astype(BF16)


def dot1(a, b, dims=NN):
    return lax.dot_general(a, b, dims, preferred_element_type=F32)


def halves(t):
    n = t.shape[1] // 2
    return t[:, :n] + t[:, n:]


def dotf(a, b, dims=NN):
    return lax.dot_general(a, b, dims, precision=lax.Precision.HIGHEST, preferred_element_type=F32)


def dot2(a, b, dims=NN):
    t = dot1(jnp.concatenate(split(a), axis=0), b, dims)
    return t[: a.shape[0]] + t[a.shape[0] :]


def iota(shape, dim):
    return lax.broadcasted_iota(jnp.int32, shape, dim)


def fold(parts, axis):
    step = 1 if axis == 0 else 16
    at = iota((8, 128), axis) // step

    def mix(a, b, mask, shift):
        return jnp.where(mask, a, b) + pltpu.roll(jnp.where(mask, b, a), shift * step, axis)

    q = [parts[(i + 3) % 8] for i in range(8)]
    y = [mix(q[k], q[k + 4], ((at - k) & 7) < 4, 4) for k in range(4)]
    z = [mix(y[k], y[k + 2], ((at - k) & 3) >= 2, 2) for k in range(2)]
    return mix(z[0], z[1], (at & 1) == 1, 1)


def row_sum(x):
    x = x + pltpu.roll(x, 4, 0)
    x = x + pltpu.roll(x, 2, 0)
    return x + pltpu.roll(x, 1, 0)


def matvec(terms, width, emit):
    turns = 2 if len(terms) > 1 else 4

    def one(g, unused):
        for turn in range(turns):
            first = (g * turns + turn) * 8
            parts = []
            for a in range(8):
                total = None
                for load, v in terms:
                    product = load(first + a) * v
                    total = product if total is None else total + product
                parts.append(jnp.sum(total.reshape(width // 8, 8, 128), axis=0))
            emit(pl.ds(pl.multiple_of(first, 8), 8), fold(parts, 0))
        return unused

    lax.fori_loop(0, width // 8 // turns, one, 0)


def pack_matrix(m):
    return jnp.concatenate([m[:32, :], m[32:, :]], axis=1)


def unpack_matrix(p):
    return jnp.concatenate([p[:, :64], p[:, 64:]], axis=0)


def scan_products(refs, count):
    half = 1
    while half < count:
        for start in range(0, count, 2 * half):
            mid = start + half
            left = pl.ds(start * 64, half * 64)
            for ref in refs:
                ref[left, :] = dotf(ref[left, :], ref[pl.ds(mid * 64, 64), :])
        half *= 2


def scan_prefix(ref, count):
    half = 1
    while half < count:
        for start in range(0, count, 2 * half):
            mid = start + half
            right = pl.ds(mid * 64, half * 64)
            ref[right, :] = dotf(ref[right, :], ref[pl.ds((mid - 1) * 64, 64), :])
        half *= 2


def diagonal(x, count):
    return jnp.where(iota(x.shape, 0) == iota(x.shape, 1) // 64, x, 0.0)


def lanes_folded(x):
    t = x[:, 0:128] + x[:, 128:256] + x[:, 256:384] + x[:, 384:512]
    return t[:, :64] + t[:, 64:]


def padded(x):
    return jnp.concatenate([x, jnp.zeros_like(x)], axis=1)


def kernel(
    nz, nx, ng,
    b_h, f_h, i_h, pat_h, tent_h, slot_h, ci_h, cl_h,
    sol_ref, ce_ref,
    F, I, b, pat, tent, slot, ci, cl,
    work, res, corr,
    cis, Zl, Pl, Z1, Zm1, Z2, Zm2, Zm3,
    Xl, W1, W2, W3,
    RM1, RM2, RM3, RV1, RV2, RV3, halo_out, halo_in,
    Hc, msg, n_mat, n_tent, n_b, n_s, n_slot, n_pat, n_first, n_off, off_out, first_out,
    load_sem, m_send, m_recv, v_send, v_recv, h_send, h_recv, n_send, n_recv, f_send, f_recv,
):
    slab, g = lax.axis_index("slab"), lax.axis_index("group")
    z, x = slab // nx, slab % nx
    ns = nz * nx

    def in_group(o):
        return (slab, lax.rem(g + o, ng))

    def along_x(o):
        return (z * nx + lax.rem(x + o, nx), g)

    def along_z(o):
        return (lax.rem(z + o, nz) * nx + x, g)

    at_end, at_start = g == ng - 1, g == 0
    right = (jnp.where(at_end, lax.rem(slab + 1, ns), slab), lax.rem(g + 1, ng))
    left = (jnp.where(at_start, lax.rem(slab + ns - 1, ns), slab), lax.rem(g + ng - 1, ng))

    barrier = pltpu.get_barrier_semaphore()
    peers = [along_z(o) for o in range(1, nz)] + [along_x(o) for o in range(1, nx)] + [right, left]
    peers += [in_group(o) for o in range(1, ng)]
    for peer in peers:
        pl.semaphore_signal(barrier, inc=1, device_id=peer, device_id_type=MESH)

    copies = []
    for k, (src, dst) in enumerate(
        [(ci_h, ci), (cl_h, cl), (i_h, I), (b_h, b), (slot_h, slot), (pat_h, pat),
         (f_h.at[1], F.at[1]), (f_h.at[0], F.at[0]), (f_h.at[2], F.at[2]), (tent_h, tent)]
    ):
        copy = pltpu.make_async_copy(src, dst, load_sem.at[k])
        copy.start()
        copies.append(copy)
    ci_c, cl_c, i_c, b_c, slot_c, pat_c, f1_c, f0_c, f2_c, tent_c = copies

    row64, lane64 = iota((64, 64), 0), iota((64, 64), 1)
    eye = (row64 == lane64).astype(F32)
    ci_c.wait()
    cl_c.wait()
    for j in range(8):
        cij = ci[:, j, :]
        cis[pl.ds(j * 64, 64), :] = cij
        m = -dotf(cij, cl[:, j, :])
        Pl[pl.ds(j * 64, 64), :] = m
        e = m.T
        Zl[pl.ds(j * 64, 64), :] = e
        Xl[pl.ds(j * 64, 64), :] = e
    scan_products([Zl], 8)

    def gather_start(ref, own, target, count, send, recv):
        started = []
        for o in range(1, count):
            copy = pltpu.make_async_remote_copy(
                src_ref=ref.at[own],
                dst_ref=ref.at[own],
                send_sem=send.at[o],
                recv_sem=recv.at[own],
                device_id=target(o),
                device_id_type=MESH,
            )
            copy.start()
            started.append(copy)
        return started

    def gather_wait(started, ref, own, count, recv):
        for o in range(1, count):
            other = lax.rem(own + o, count)
            pltpu.make_async_copy(ref.at[other], ref.at[other], recv.at[other]).wait()
        for copy in started:
            copy.wait_send()

    lane8, lane = iota((8, 128), 1), iota((64, 128), 1)
    has_left = jnp.logical_not(jnp.logical_and(slab == 0, at_start))
    has_right = jnp.logical_not(jnp.logical_and(slab == ns - 1, at_end))

    def halo_pack(turn, ref):
        to_right, to_left = jnp.zeros((8, 128), F32), jnp.zeros((8, 128), F32)
        for k in range(8):
            piece = ref[pl.ds(8 * k, 8), :]
            to_right = jnp.where(lane8 == k, pltpu.roll(piece, k + 1, 1), to_right)
            to_left = jnp.where(lane8 == k, pltpu.roll(piece, k, 1) if k else piece, to_left)
        halo_out[turn, 0] = to_right
        halo_out[turn, 1] = to_left

    def halo_send(turn):
        started = []
        for side, peer in ((0, right), (1, left)):
            copy = pltpu.make_async_remote_copy(
                src_ref=halo_out.at[turn, side],
                dst_ref=halo_in.at[turn, side],
                send_sem=h_send.at[turn, side],
                recv_sem=h_recv.at[turn, side],
                device_id=peer,
                device_id_type=MESH,
            )
            copy.start()
            started.append(copy)
        return started

    def apply_with(value, left_of, right_of, emit):
        before, after = [], []
        for k in range(8):
            piece = value[8 * k : 8 * k + 8]
            before.append(jnp.where(lane8 == 0, left_of(k), pltpu.roll(piece, 1, 1)))
            after.append(jnp.where(lane8 == 127, right_of(k), pltpu.roll(piece, 127, 1)))
        previous = jnp.concatenate(before, axis=0) * pat[0:1, :].astype(F32)
        following = jnp.concatenate(after, axis=0) * pat[1:2, :].astype(F32)
        matvec(
            [
                (lambda a: F[1, a], value),
                (lambda a: F[0, a], previous),
                (lambda a: F[2, a], following),
            ],
            64,
            emit,
        )

    def fine_apply(turn, ref, started, emit):
        for copy in started:
            copy.wait()
        from_left = jnp.where(has_left, halo_in[turn, 0], 0.0)
        from_right = jnp.where(has_right, halo_in[turn, 1], 0.0)

        def left_of(k):
            return pltpu.roll(from_left, 128 - k, 1) if k else from_left

        def right_of(k):
            return pltpu.roll(from_right, 127 - k, 1)

        apply_with(ref[...], left_of, right_of, emit)

    def block_apply(value, emit):
        matvec([(lambda a: I[a], value)], 64, emit)

    def to_residue(rows, y):
        res[rows, :] = b[rows, :] - y

    def sweep(turn, ref, started):
        fine_apply(turn, ref, started, to_residue)

        def emit(rows, y):
            ref[rows, :] = ref[rows, :] + DAMP * y

        block_apply(res[...], emit)

    def first(rows, y):
        work[rows, :] = DAMP * y

    i_c.wait()
    b_c.wait()
    block_apply(b[...], first)
    halo_pack(0, work)

    slot_c.wait()
    q, col = iota((64, 512), 0), iota((64, 512), 1)
    pick = (q == (col % 16) * 4 + col // 128).astype(BF16)
    own_block = iota((8, 512), 0) == (iota((8, 512), 1) % 128) // 16
    slots = dot1(slot[...].astype(F32).astype(BF16), pick)
    slots = row_sum(jnp.where(own_block, slots, 0.0))
    slots = jnp.concatenate([slots] * 8, axis=0)
    GT = (slots == q.astype(F32)).astype(BF16)

    pl.semaphore_wait(barrier, len(peers))

    h0 = halo_send(0)
    RM1[g] = pack_matrix(Zl[0:64, :])
    rm1 = gather_start(RM1, g, in_group, ng, m_send.at[0], m_recv.at[0])

    def gathered(t, load):
        def one(A, unused):
            to_right, to_left = jnp.zeros((8, 128), F32), jnp.zeros((8, 128), F32)
            for u in range(8):
                whole = load(A * 8 + u)
                edge = jnp.zeros((8, 128), F32)
                for k in range(8):
                    piece = pltpu.roll(whole[8 * k : 8 * k + 8], (2 + 16 * k) % 128, 1)
                    edge = jnp.where(lane8 // 16 == k, piece, edge)
                here = (lane8 % 16) // 2 == u
                to_right = jnp.where(here, pltpu.roll(edge, 2 * u, 1) if u else edge, to_right)
                shift = (2 * u - 2) % 128
                to_left = jnp.where(here, pltpu.roll(edge, shift, 1) if shift else edge, to_left)
            msg[0, t, A] = to_right
            msg[1, t, A] = to_left
            return unused

        lax.fori_loop(0, 8, one, 0)

    f1_c.wait()
    gathered(1, lambda a: F[1, a])
    f0_c.wait()
    gathered(0, lambda a: F[0, a])
    pat_c.wait()
    f2_c.wait()
    sweep(0, work, h0)
    halo_pack(1, work)
    h1 = halo_send(1)

    def upward(started, ref, own, count, recv, full, masked):
        gather_wait(started, ref, own, count, recv)
        for k in range(count):
            e = unpack_matrix(ref[k])
            rows = pl.ds(k * 64, 64)
            if full is not None:
                full[rows, :] = e
            masked[rows, :] = jnp.where(k < own, e, eye)
        scan_products([masked] if full is None else [full, masked], count)

    def later(ref, h, count):
        return ref[pl.ds((h + 1) * 64, 64), :] if h + 1 < count else eye

    upward(rm1, RM1, g, ng, m_recv.at[0], Z1, Zm1)
    RM2[x] = pack_matrix(Z1[0:64, :])
    rm2 = gather_start(RM2, x, along_x, nx, m_send.at[1], m_recv.at[1])
    def weigh(ref, h, parts):
        ref[pl.ds(h * 64, 64), :] = jnp.concatenate(split(jnp.concatenate(parts, axis=1)), axis=1)

    for h in range(ng):
        weigh(W1, h, [later(Z1, h, ng), jnp.where(h < g, later(Zm1, h, ng), 0.0)])

    gathered(2, lambda a: F[2, a])

    fine_apply(1, work, h1, to_residue)
    tent_c.wait()
    residue = res[...]
    values = []
    for m in range(4):
        weight = jnp.sum((tent[m] * residue).reshape(8, 8, 128), axis=0)
        values.append(row_sum(weight) * (1.0 / math.sqrt(64)))
    spread = jnp.where(own_block, jnp.concatenate(values, axis=1), 0.0)
    rhs = dot2(spread, GT, NT)
    offsets = diagonal(dotf(rhs, cis[...], NT), 8)
    after_own = jnp.concatenate([Zl[64:512, :], eye], axis=0)
    RV1[g] = padded(row_sum(dotf(offsets, after_own)))
    rv1 = gather_start(RV1, g, in_group, ng, v_send.at[0], v_recv.at[0])

    upward(rm2, RM2, x, nx, m_recv.at[1], Z2, Zm2)
    RM3[z] = pack_matrix(Z2[0:64, :])
    rm3 = gather_start(RM3, z, along_z, nz, m_send.at[2], m_recv.at[2])
    for h in range(nx):
        weigh(W2, h, [later(Z2, h, nx), jnp.where(h < x, later(Zm2, h, nx), 0.0)])

    own = lanes_folded(offsets)
    off_out[...] = padded(own)
    first_out[...] = pack_matrix(Pl[0:64, :])
    beside = []
    for side, peer in ((0, right), (1, left)):
        for k, (src, dst) in enumerate(
            [(work, n_s), (b, n_b), (tent, n_tent), (slot, n_slot), (pat, n_pat)]
        ):
            copy = pltpu.make_async_remote_copy(
                src_ref=src,
                dst_ref=dst.at[side],
                send_sem=n_send.at[side, k],
                recv_sem=n_recv.at[side, k],
                device_id=peer,
                device_id_type=MESH,
            )
            copy.start()
            beside.append(copy)
    for k, (src, dst) in enumerate([(first_out, n_first), (off_out, n_off)]):
        copy = pltpu.make_async_remote_copy(
            src_ref=src,
            dst_ref=dst,
            send_sem=f_send.at[k],
            recv_sem=f_recv.at[k],
            device_id=left,
            device_id_type=MESH,
        )
        copy.start()
        beside.append(copy)

    gathered(3, lambda a: I[a])
    for side, peer in ((0, right), (1, left)):
        copy = pltpu.make_async_remote_copy(
            src_ref=msg.at[side],
            dst_ref=n_mat.at[side],
            send_sem=n_send.at[side, 5],
            recv_sem=n_recv.at[side, 5],
            device_id=peer,
            device_id_type=MESH,
        )
        copy.start()
        beside.append(copy)


    def inflow(ref, weights, count):
        flat = [ref[h] + pltpu.roll(ref[h + 1], 64, 1) for h in range(0, count, 2)]
        return halves(dot2(jnp.concatenate(flat, axis=1), weights[...]))


    gather_wait(rv1, RV1, g, ng, v_recv.at[0])
    flow1 = inflow(RV1, W1, ng)
    RV2[x] = padded(flow1[:, :64])
    rv2 = gather_start(RV2, x, along_x, nx, v_send.at[1], v_recv.at[1])

    scan_prefix(Pl, 8)

    row8 = iota((8, 64), 0)
    carried = jnp.broadcast_to(own[0:1], (8, 64))
    local = carried
    for j in range(1, 8):
        carried = dotf(carried, Xl[pl.ds(j * 64, 64), :]) + own[j : j + 1]
        local = jnp.where(row8 >= j, carried, local)


    gather_wait(rv2, RV2, x, nx, v_recv.at[1])
    flow2 = inflow(RV2, W2, nx)
    RV3[z] = padded(flow2[:, :64])
    rv3 = gather_start(RV3, z, along_z, nz, v_send.at[2], v_recv.at[2])

    upward(rm3, RM3, z, nz, m_recv.at[2], None, Zm3)
    A1 = Zm1[0:64, :]
    A21 = dotf(Zm2[0:64, :], A1)
    for h in range(nz):
        weigh(W3, h, [dotf(jnp.where(h < z, later(Zm3, h, nz), 0.0), A21)])

    nearer = dotf(flow2[:, 64:], A1) + flow1[:, 64:]
    for copy in beside:
        copy.wait()
    group, spot = lane8 // 16, lane8 % 16
    at_right = jnp.logical_and(spot >= 8, spot < 11)
    valid = jnp.logical_or(jnp.logical_and(spot < 3, has_left), jnp.logical_and(at_right, has_right))

    def gather_lanes(pieces, shift, mask, out):
        for k in range(8):
            moved = pltpu.roll(pieces(k), shift + 16 * k, 1)
            out = jnp.where(jnp.logical_and(group == k, mask), moved, out)
        return out

    nothing = jnp.zeros((8, 128), F32)

    def beyond(ref, *at):
        left_ref, right_ref = ref.at[(0, *at)], ref.at[(1, *at)]
        out = gather_lanes(lambda k: left_ref[pl.ds(8 * k, 8), :], 3, spot < 3, nothing)
        return gather_lanes(lambda k: right_ref[pl.ds(8 * k, 8), :], 8, at_right, out)

    def own_ends(ref, out):
        out = gather_lanes(lambda k: ref[pl.ds(8 * k, 8), :], 3, spot == 3, out)
        return gather_lanes(lambda k: ref[pl.ds(8 * k, 8), :], 8, spot == 7, out)

    b_halo = beyond(n_b)
    s_halo = beyond(n_s)
    tent_halo = [beyond(n_tent, m) for m in range(4)]
    pat_halo = []
    for r in range(2):
        rows = [jnp.broadcast_to(n_pat[e, r : r + 1, :].astype(F32), (8, 128)) for e in range(2)]
        out = gather_lanes(lambda k: rows[0], 3, spot < 3, nothing)
        pat_halo.append(gather_lanes(lambda k: rows[1], 8, at_right, out))

    def placed(A, unused):
        for t in range(4):
            from_left, from_right = n_mat[0, t, A], n_mat[1, t, A]
            at_two_left = jnp.logical_or(spot == 1, spot == 2)
            at_two_right = jnp.logical_or(spot == 8, spot == 9)
            for u in range(8):
                p = jnp.where(at_two_left, pltpu.roll(from_left, (1 - 2 * u) % 128, 1), 0.0)
                shift = (8 - 2 * u) % 128
                q = pltpu.roll(from_right, shift, 1) if shift else from_right
                Hc[t, A * 8 + u] = jnp.where(at_two_right, q, p)
        return unused

    lax.fori_loop(0, 8, placed, 0)

    place = iota((64, 512), 1) % 16
    asked = jnp.where(place < 3, place + 13, place - 8) * 4 + col // 128
    pick_halo = (q == asked).astype(BF16)
    ends = jnp.concatenate([n_slot[0, 7:8, :], n_slot[1, 0:1, :]] + [n_slot[1, 0:1, :]] * 6, axis=0)
    slots = dot1(ends.astype(F32).astype(BF16), pick_halo)
    which = (iota((8, 512), 1) % 16 >= 8).astype(jnp.int32) == iota((8, 512), 0)
    slots = row_sum(jnp.where(which, slots, 0.0))
    GT_halo = (jnp.concatenate([slots] * 8, axis=0) == q.astype(F32)).astype(BF16)
    M_next = unpack_matrix(n_first[...])
    P_next = dotf(M_next, Pl[448:512, :])
    local_next = dotf(carried, M_next, NT) + n_off[0:1, :64]

    def halo_matvec(terms):
        rows = []
        for A in range(8):
            parts = []
            for u in range(8):
                total = None
                for t, v in terms:
                    term = Hc[t, A * 8 + u] * v
                    total = term if total is None else total + term
                parts.append(total)
            rows.append(fold(parts, 0))
        return fold(rows, 1)

    def halo_apply(v):
        return halo_matvec([(1, v), (0, pltpu.roll(v, 1, 1) * pat_halo[0]), (2, pltpu.roll(v, 127, 1) * pat_halo[1])])

    gather_wait(rv3, RV3, z, nz, v_recv.at[2])
    incoming = inflow(RV3, W3, nz) + nearer

    coarse = local + lanes_folded(diagonal(dotf(incoming, Pl[...], NT), 8))
    ce_ref[...] = coarse
    weights = jnp.where(own_block, dot2(coarse, GT), 0.0)
    total = None
    for m in range(4):
        w = row_sum(weights[:, m * 128 : m * 128 + 128]) * (1.0 / math.sqrt(64))
        term = tent[m] * jnp.concatenate([w] * 8, axis=0)
        total = term if total is None else total + term
    corr[...] = total
    next_first = dotf(incoming, P_next, NT) + local_next
    two = jnp.concatenate([incoming[0:1], next_first[0:1]] + [next_first[0:1]] * 6, axis=0)
    weights = jnp.where(which, dot2(two, GT_halo), 0.0)
    total = None
    for m in range(4):
        w = row_sum(weights[:, m * 128 : m * 128 + 128]) * (1.0 / math.sqrt(64))
        term = tent_halo[m] * w
        total = term if total is None else total + term
    c_halo = own_ends(corr, jnp.where(valid, total, 0.0))

    def post(ref, halo, emit):
        def left_of(k):
            return pltpu.roll(halo, 126 - 16 * k, 1)

        def right_of(k):
            return pltpu.roll(halo, 119 - 16 * k, 1)

        apply_with(ref[...], left_of, right_of, emit)

    def to_res(rows, y):
        res[rows, :] = y

    post(corr, c_halo, to_res)

    def prolong(rows, y):
        sol_ref[rows, :] = work[rows, :] + corr[rows, :] - SMOOTH * y

    block_apply(res[...], prolong)
    s_halo = s_halo + c_halo - SMOOTH * halo_matvec([(3, halo_apply(c_halo))])
    s_halo = jnp.where(valid, s_halo, 0.0)
    s_ends = own_ends(sol_ref, s_halo)

    def smooth(rows, y):
        sol_ref[rows, :] = sol_ref[rows, :] + DAMP * y

    post(sol_ref, s_ends, to_residue)
    block_apply(res[...], smooth)
    s_halo = s_halo + DAMP * halo_matvec([(3, b_halo - halo_apply(s_ends))])
    s_halo = jnp.where(valid, s_halo, 0.0)
    post(sol_ref, s_halo, to_residue)
    block_apply(res[...], smooth)


def body(nz, nx, ng, right_side, fine_blocks, fine_inverse, pattern, tentative, slot_map, coarse_inverse, coarse_lower):
    vmem = lambda *shape: pltpu.VMEM(shape, F32)
    dma = lambda *shape: pltpu.SemaphoreType.DMA(shape)
    top = max(nz, nx, ng)
    scratch = [
        vmem(3, 64, 64, 128), vmem(64, 64, 128), vmem(64, 128), pltpu.VMEM((2, 128), jnp.int32), vmem(4, 64, 128),
        pltpu.VMEM((8, 64), jnp.int32), vmem(64, 8, 64), vmem(64, 8, 64),
        vmem(64, 128), vmem(64, 128), vmem(64, 128),
        vmem(512, 64), vmem(512, 64), vmem(512, 64), vmem(ng * 64, 64), vmem(ng * 64, 64),
        vmem(nx * 64, 64), vmem(nx * 64, 64), vmem(nz * 64, 64),
        vmem(512, 64),
        pltpu.VMEM((ng * 64, 256), BF16), pltpu.VMEM((nx * 64, 256), BF16), pltpu.VMEM((nz * 64, 128), BF16),
        vmem(ng, 32, 128), vmem(nx, 32, 128), vmem(nz, 32, 128),
        vmem(ng, 8, 128), vmem(nx, 8, 128), vmem(nz, 8, 128),
        vmem(2, 2, 8, 128), vmem(2, 2, 8, 128),
        vmem(4, 64, 8, 128), vmem(2, 4, 8, 8, 128), vmem(2, 4, 8, 8, 128), vmem(2, 4, 64, 128), vmem(2, 64, 128),
        vmem(2, 64, 128), pltpu.VMEM((2, 8, 64), jnp.int32), pltpu.VMEM((2, 2, 128), jnp.int32),
        vmem(32, 128), vmem(8, 128), vmem(8, 128), vmem(32, 128),
        dma(10), dma(3, top), dma(3, top), dma(3, top), dma(3, top), dma(2, 2), dma(2, 2),
        dma(2, 6), dma(2, 6), dma(2), dma(2),
    ]
    result, coarse = pl.pallas_call(
        functools.partial(kernel, nz, nx, ng),
        out_shape=(
            jax.ShapeDtypeStruct((64, 128), F32),
            jax.ShapeDtypeStruct((8, 64), F32),
        ),
        in_specs=[pl.BlockSpec(memory_space=pl.ANY)] * 8,
        out_specs=(
            pl.BlockSpec(memory_space=pltpu.VMEM),
            pl.BlockSpec(memory_space=pltpu.VMEM),
        ),
        scratch_shapes=scratch,
        compiler_params=pltpu.CompilerParams(
            collective_id=0, has_side_effects=True, vmem_limit_bytes=60 * 2**20
        ),
        name="v_cycle",
    )(
        right_side, fine_blocks, fine_inverse, pattern, tentative, slot_map,
        jnp.transpose(coarse_inverse, (0, 2, 1)), jnp.transpose(coarse_lower, (0, 2, 1)),
    )
    return result, coarse.T


def solution(mesh):
    slabs, ng = mesh.shape["slab"], mesh.shape["group"]
    nx = 4 if slabs % 4 == 0 and slabs > 4 else 2
    both = ("slab", "group")
    in_specs = (
        P(None, both), P(None, None, None, both), P(None, None, both), P(None, both), P(None, None, both),
        P(both, None), P(None, None, both), P(None, None, both),
    )
    return jax.shard_map(
        functools.partial(body, slabs // nx, nx, ng),
        mesh=mesh,
        in_specs=in_specs,
        out_specs=(P(None, both), P(None, both)),
        check_vma=False,
    )
```

```python
import functools
import math

import jax
import jax.numpy as jnp
from jax import lax
from jax.experimental import pallas as pl
from jax.experimental.pallas import tpu as pltpu
from jax.sharding import PartitionSpec as P

DAMP = 0.8
SMOOTH = 0.67
F32 = jnp.float32
BF16 = jnp.bfloat16
MESH = pl.DeviceIdType.MESH

NN = (((1,), (0,)), ((), ()))
NT = (((1,), (1,)), ((), ()))


def split(x):
    hi = x.astype(BF16)
    return hi, (x - hi.astype(F32)).astype(BF16)


def dot1(a, b, dims=NN):
    return lax.dot_general(a, b, dims, preferred_element_type=F32)


def halves(t):
    n = t.shape[1] // 2
    return t[:, :n] + t[:, n:]


def dotf(a, b, dims=NN):
    return lax.dot_general(a, b, dims, precision=lax.Precision.HIGHEST, preferred_element_type=F32)


def dot2(a, b, dims=NN):
    t = dot1(jnp.concatenate(split(a), axis=0), b, dims)
    return t[: a.shape[0]] + t[a.shape[0] :]


def iota(shape, dim):
    return lax.broadcasted_iota(jnp.int32, shape, dim)


def fold(parts, axis):
    step = 1 if axis == 0 else 16
    at = iota((8, 128), axis) // step

    def mix(a, b, mask, shift):
        return jnp.where(mask, a, b) + pltpu.roll(jnp.where(mask, b, a), shift * step, axis)

    q = [parts[(i + 3) % 8] for i in range(8)]
    y = [mix(q[k], q[k + 4], ((at - k) & 7) < 4, 4) for k in range(4)]
    z = [mix(y[k], y[k + 2], ((at - k) & 3) >= 2, 2) for k in range(2)]
    return mix(z[0], z[1], (at & 1) == 1, 1)


def row_sum(x):
    x = x + pltpu.roll(x, 4, 0)
    x = x + pltpu.roll(x, 2, 0)
    return x + pltpu.roll(x, 1, 0)


def matvec(terms, width, emit):
    turns = 2 if len(terms) > 1 else 4

    def one(g, unused):
        for turn in range(turns):
            first = (g * turns + turn) * 8
            parts = []
            for a in range(8):
                total = None
                for load, v in terms:
                    product = load(first + a) * v
                    total = product if total is None else total + product
                parts.append(jnp.sum(total.reshape(width // 8, 8, 128), axis=0))
            emit(pl.ds(pl.multiple_of(first, 8), 8), fold(parts, 0))
        return unused

    lax.fori_loop(0, width // 8 // turns, one, 0)


def pack_matrix(m):
    return jnp.concatenate([m[:32, :], m[32:, :]], axis=1)


def unpack_matrix(p):
    return jnp.concatenate([p[:, :64], p[:, 64:]], axis=0)


def scan_products(refs, count):
    half = 1
    while half < count:
        for start in range(0, count, 2 * half):
            mid = start + half
            left = pl.ds(start * 64, half * 64)
            for ref in refs:
                ref[left, :] = dotf(ref[left, :], ref[pl.ds(mid * 64, 64), :])
        half *= 2


def scan_prefix(ref, count):
    half = 1
    while half < count:
        for start in range(0, count, 2 * half):
            mid = start + half
            right = pl.ds(mid * 64, half * 64)
            ref[right, :] = dotf(ref[right, :], ref[pl.ds((mid - 1) * 64, 64), :])
        half *= 2


def diagonal(x, count):
    return jnp.where(iota(x.shape, 0) == iota(x.shape, 1) // 64, x, 0.0)


def lanes_folded(x):
    t = x[:, 0:128] + x[:, 128:256] + x[:, 256:384] + x[:, 384:512]
    return t[:, :64] + t[:, 64:]


def padded(x):
    return jnp.concatenate([x, jnp.zeros_like(x)], axis=1)


def kernel(
    nz, nx, ng,
    b_h, f_h, i_h, pat_h, tent_h, slot_h, ci_h, cl_h,
    sol_ref, ce_ref,
    F, I, b, pat, tent, slot, ci, cl,
    work, res, corr,
    cis, Zl, Pl, Z1, Zm1, Z2, Zm2, Zm3,
    Xl, W1, W2, W3,
    RM1, RM2, RM3, RV1, RV2, RV3, halo_out, halo_in,
    Hc, msg, n_mat, vec, n_vec, n_slot, n_first, n_off, off_out, first_out,
    load_sem, m_send, m_recv, v_send, v_recv, h_send, h_recv, n_send, n_recv, f_send, f_recv,
):
    slab, g = lax.axis_index("slab"), lax.axis_index("group")
    z, x = slab // nx, slab % nx
    ns = nz * nx

    def in_group(o):
        return (slab, lax.rem(g + o, ng))

    def along_x(o):
        return (z * nx + lax.rem(x + o, nx), g)

    def along_z(o):
        return (lax.rem(z + o, nz) * nx + x, g)

    at_end, at_start = g == ng - 1, g == 0
    right = (jnp.where(at_end, lax.rem(slab + 1, ns), slab), lax.rem(g + 1, ng))
    left = (jnp.where(at_start, lax.rem(slab + ns - 1, ns), slab), lax.rem(g + ng - 1, ng))

    barrier = pltpu.get_barrier_semaphore()
    peers = [along_z(o) for o in range(1, nz)] + [along_x(o) for o in range(1, nx)] + [right, left]
    peers += [in_group(o) for o in range(1, ng)]
    for peer in peers:
        pl.semaphore_signal(barrier, inc=1, device_id=peer, device_id_type=MESH)

    copies = []
    for k, (src, dst) in enumerate(
        [(ci_h, ci), (cl_h, cl), (i_h, I), (b_h, b), (slot_h, slot), (pat_h, pat),
         (f_h.at[1], F.at[1]), (f_h.at[0], F.at[0]), (f_h.at[2], F.at[2]), (tent_h, tent)]
    ):
        copy = pltpu.make_async_copy(src, dst, load_sem.at[k])
        copy.start()
        copies.append(copy)
    ci_c, cl_c, i_c, b_c, slot_c, pat_c, f1_c, f0_c, f2_c, tent_c = copies

    row64, lane64 = iota((64, 64), 0), iota((64, 64), 1)
    eye = (row64 == lane64).astype(F32)
    ci_c.wait()
    cl_c.wait()
    for j in range(8):
        cij = ci[:, j, :]
        cis[pl.ds(j * 64, 64), :] = cij
        m = -dotf(cij, cl[:, j, :])
        Pl[pl.ds(j * 64, 64), :] = m
        e = m.T
        Zl[pl.ds(j * 64, 64), :] = e
        Xl[pl.ds(j * 64, 64), :] = e
    scan_products([Zl], 8)

    def gather_start(ref, own, target, count, send, recv):
        started = []
        for o in range(1, count):
            copy = pltpu.make_async_remote_copy(
                src_ref=ref.at[own],
                dst_ref=ref.at[own],
                send_sem=send.at[o],
                recv_sem=recv.at[own],
                device_id=target(o),
                device_id_type=MESH,
            )
            copy.start()
            started.append(copy)
        return started

    def gather_wait(started, ref, own, count, recv):
        for o in range(1, count):
            other = lax.rem(own + o, count)
            pltpu.make_async_copy(ref.at[other], ref.at[other], recv.at[other]).wait()
        for copy in started:
            copy.wait_send()

    lane8, lane = iota((8, 128), 1), iota((64, 128), 1)
    has_left = jnp.logical_not(jnp.logical_and(slab == 0, at_start))
    has_right = jnp.logical_not(jnp.logical_and(slab == ns - 1, at_end))

    def halo_pack(turn, ref):
        to_right, to_left = jnp.zeros((8, 128), F32), jnp.zeros((8, 128), F32)
        for k in range(8):
            piece = ref[pl.ds(8 * k, 8), :]
            to_right = jnp.where(lane8 == k, pltpu.roll(piece, k + 1, 1), to_right)
            to_left = jnp.where(lane8 == k, pltpu.roll(piece, k, 1) if k else piece, to_left)
        halo_out[turn, 0] = to_right
        halo_out[turn, 1] = to_left

    def halo_send(turn):
        started = []
        for side, peer in ((0, right), (1, left)):
            copy = pltpu.make_async_remote_copy(
                src_ref=halo_out.at[turn, side],
                dst_ref=halo_in.at[turn, side],
                send_sem=h_send.at[turn, side],
                recv_sem=h_recv.at[turn, side],
                device_id=peer,
                device_id_type=MESH,
            )
            copy.start()
            started.append(copy)
        return started

    def apply_with(value, left_of, right_of, emit):
        before, after = [], []
        for k in range(8):
            piece = value[8 * k : 8 * k + 8]
            before.append(jnp.where(lane8 == 0, left_of(k), pltpu.roll(piece, 1, 1)))
            after.append(jnp.where(lane8 == 127, right_of(k), pltpu.roll(piece, 127, 1)))
        previous = jnp.concatenate(before, axis=0) * pat[0:1, :].astype(F32)
        following = jnp.concatenate(after, axis=0) * pat[1:2, :].astype(F32)
        matvec(
            [
                (lambda a: F[1, a], value),
                (lambda a: F[0, a], previous),
                (lambda a: F[2, a], following),
            ],
            64,
            emit,
        )

    def fine_apply(turn, ref, started, emit):
        for copy in started:
            copy.wait()
        from_left = jnp.where(has_left, halo_in[turn, 0], 0.0)
        from_right = jnp.where(has_right, halo_in[turn, 1], 0.0)

        def left_of(k):
            return pltpu.roll(from_left, 128 - k, 1) if k else from_left

        def right_of(k):
            return pltpu.roll(from_right, 127 - k, 1)

        apply_with(ref[...], left_of, right_of, emit)

    def block_apply(value, emit):
        matvec([(lambda a: I[a], value)], 64, emit)

    def to_residue(rows, y):
        res[rows, :] = b[rows, :] - y

    def sweep(turn, ref, started):
        fine_apply(turn, ref, started, to_residue)

        def emit(rows, y):
            ref[rows, :] = ref[rows, :] + DAMP * y

        block_apply(res[...], emit)

    def first(rows, y):
        work[rows, :] = DAMP * y

    i_c.wait()
    b_c.wait()
    block_apply(b[...], first)
    halo_pack(0, work)

    slot_c.wait()
    q, col = iota((64, 512), 0), iota((64, 512), 1)
    pick = (q == (col % 16) * 4 + col // 128).astype(BF16)
    own_block = iota((8, 512), 0) == (iota((8, 512), 1) % 128) // 16
    slots = dot1(slot[...].astype(F32).astype(BF16), pick)
    slots = row_sum(jnp.where(own_block, slots, 0.0))
    slots = jnp.concatenate([slots] * 8, axis=0)
    GT = (slots == q.astype(F32)).astype(BF16)

    group, spot = lane8 // 16, lane8 % 16
    at_left, at_right = spot < 3, jnp.logical_and(spot >= 8, spot < 11)

    def gather_lanes(pieces, shift, mask, out):
        for k in range(8):
            moved = pltpu.roll(pieces(k), shift + 16 * k, 1)
            out = jnp.where(jnp.logical_and(group == k, mask), moved, out)
        return out

    nothing = jnp.zeros((8, 128), F32)

    def pack_ends(place, pieces):
        vec[0, place] = gather_lanes(pieces, 3, at_left, nothing)
        vec[1, place] = gather_lanes(pieces, 8, at_right, nothing)

    beside = []

    def tell(src, dst, k, peer, send, recv):
        copy = pltpu.make_async_remote_copy(
            src_ref=src, dst_ref=dst, send_sem=send.at[k], recv_sem=recv.at[k], device_id=peer, device_id_type=MESH
        )
        copy.start()
        beside.append(copy)

    def tell_both(src, dst, k, part):
        for side, peer in ((0, right), (1, left)):
            here = src if part is None else src.at[side, part]
            there = dst.at[side] if part is None else dst.at[side, part]
            tell(here, there, k, peer, n_send.at[side], n_recv.at[side])

    first_out[...] = pack_matrix(Pl[0:64, :])
    pack_ends(0, lambda k: b[pl.ds(8 * k, 8), :])
    pat_c.wait()
    tent_c.wait()
    for m in range(4):
        pack_ends(2 + m, lambda k, m=m: tent[m, pl.ds(8 * k, 8), :])
    for r in range(2):
        row = jnp.broadcast_to(pat[r : r + 1, :].astype(F32), (8, 128))
        pack_ends(6 + r, lambda k: row)

    pl.semaphore_wait(barrier, len(peers))

    h0 = halo_send(0)
    RM1[g] = pack_matrix(Zl[0:64, :])
    rm1 = gather_start(RM1, g, in_group, ng, m_send.at[0], m_recv.at[0])

    def gathered(t, load):
        def one(A, unused):
            to_right, to_left = jnp.zeros((8, 128), F32), jnp.zeros((8, 128), F32)
            for u in range(8):
                whole = load(A * 8 + u)
                edge = jnp.zeros((8, 128), F32)
                for k in range(8):
                    piece = pltpu.roll(whole[8 * k : 8 * k + 8], (2 + 16 * k) % 128, 1)
                    edge = jnp.where(lane8 // 16 == k, piece, edge)
                here = (lane8 % 16) // 2 == u
                to_right = jnp.where(here, pltpu.roll(edge, 2 * u, 1) if u else edge, to_right)
                shift = (2 * u - 2) % 128
                to_left = jnp.where(here, pltpu.roll(edge, shift, 1) if shift else edge, to_left)
            msg[0, t, A] = to_right
            msg[1, t, A] = to_left
            return unused

        lax.fori_loop(0, 8, one, 0)

    tell(first_out, n_first, 1, left, f_send, f_recv)
    tell_both(slot, n_slot, 4, None)
    f1_c.wait()
    gathered(1, lambda a: F[1, a])
    tell_both(msg, n_mat, 1, 1)
    f0_c.wait()
    gathered(0, lambda a: F[0, a])
    tell_both(msg, n_mat, 0, 0)
    f2_c.wait()
    sweep(0, work, h0)
    halo_pack(1, work)
    h1 = halo_send(1)

    def upward(started, ref, own, count, recv, full, masked):
        gather_wait(started, ref, own, count, recv)
        for k in range(count):
            e = unpack_matrix(ref[k])
            rows = pl.ds(k * 64, 64)
            if full is not None:
                full[rows, :] = e
            masked[rows, :] = jnp.where(k < own, e, eye)
        scan_products([masked] if full is None else [full, masked], count)

    def later(ref, h, count):
        return ref[pl.ds((h + 1) * 64, 64), :] if h + 1 < count else eye

    upward(rm1, RM1, g, ng, m_recv.at[0], Z1, Zm1)
    RM2[x] = pack_matrix(Z1[0:64, :])
    rm2 = gather_start(RM2, x, along_x, nx, m_send.at[1], m_recv.at[1])
    def weigh(ref, h, parts):
        ref[pl.ds(h * 64, 64), :] = jnp.concatenate(split(jnp.concatenate(parts, axis=1)), axis=1)

    for h in range(ng):
        weigh(W1, h, [later(Z1, h, ng), jnp.where(h < g, later(Zm1, h, ng), 0.0)])

    pack_ends(1, lambda k: work[pl.ds(8 * k, 8), :])
    for side, peer in ((0, right), (1, left)):
        tell(vec.at[side], n_vec.at[side], 5, peer, n_send.at[side], n_recv.at[side])
    gathered(2, lambda a: F[2, a])
    tell_both(msg, n_mat, 2, 2)

    fine_apply(1, work, h1, to_residue)
    residue = res[...]
    values = []
    for m in range(4):
        weight = jnp.sum((tent[m] * residue).reshape(8, 8, 128), axis=0)
        values.append(row_sum(weight) * (1.0 / math.sqrt(64)))
    spread = jnp.where(own_block, jnp.concatenate(values, axis=1), 0.0)
    rhs = dot2(spread, GT, NT)
    offsets = diagonal(dotf(rhs, cis[...], NT), 8)
    after_own = jnp.concatenate([Zl[64:512, :], eye], axis=0)
    RV1[g] = padded(row_sum(dotf(offsets, after_own)))
    rv1 = gather_start(RV1, g, in_group, ng, v_send.at[0], v_recv.at[0])

    upward(rm2, RM2, x, nx, m_recv.at[1], Z2, Zm2)
    RM3[z] = pack_matrix(Z2[0:64, :])
    rm3 = gather_start(RM3, z, along_z, nz, m_send.at[2], m_recv.at[2])
    for h in range(nx):
        weigh(W2, h, [later(Z2, h, nx), jnp.where(h < x, later(Zm2, h, nx), 0.0)])

    own = lanes_folded(offsets)
    off_out[...] = padded(own)
    tell(off_out, n_off, 0, left, f_send, f_recv)
    gathered(3, lambda a: I[a])
    tell_both(msg, n_mat, 3, 3)

    def inflow(ref, weights, count):
        flat = [ref[h] + pltpu.roll(ref[h + 1], 64, 1) for h in range(0, count, 2)]
        return halves(dot2(jnp.concatenate(flat, axis=1), weights[...]))


    gather_wait(rv1, RV1, g, ng, v_recv.at[0])
    flow1 = inflow(RV1, W1, ng)
    RV2[x] = padded(flow1[:, :64])
    rv2 = gather_start(RV2, x, along_x, nx, v_send.at[1], v_recv.at[1])

    scan_prefix(Pl, 8)

    row8 = iota((8, 64), 0)
    carried = jnp.broadcast_to(own[0:1], (8, 64))
    local = carried
    for j in range(1, 8):
        carried = dotf(carried, Xl[pl.ds(j * 64, 64), :]) + own[j : j + 1]
        local = jnp.where(row8 >= j, carried, local)


    gather_wait(rv2, RV2, x, nx, v_recv.at[1])
    flow2 = inflow(RV2, W2, nx)
    RV3[z] = padded(flow2[:, :64])
    rv3 = gather_start(RV3, z, along_z, nz, v_send.at[2], v_recv.at[2])

    upward(rm3, RM3, z, nz, m_recv.at[2], None, Zm3)
    A1 = Zm1[0:64, :]
    A21 = dotf(Zm2[0:64, :], A1)
    for h in range(nz):
        weigh(W3, h, [dotf(jnp.where(h < z, later(Zm3, h, nz), 0.0), A21)])

    nearer = dotf(flow2[:, 64:], A1) + flow1[:, 64:]
    for copy in beside:
        copy.wait()
    valid = jnp.logical_or(jnp.logical_and(at_left, has_left), jnp.logical_and(at_right, has_right))

    def own_ends(ref, out):
        out = gather_lanes(lambda k: ref[pl.ds(8 * k, 8), :], 3, spot == 3, out)
        return gather_lanes(lambda k: ref[pl.ds(8 * k, 8), :], 8, spot == 7, out)

    b_halo, s_halo, *tent_halo = [n_vec[0, k] + n_vec[1, k] for k in range(6)]
    pat_halo = [n_vec[0, k] + n_vec[1, k] for k in (6, 7)]

    def placed(A, unused):
        for t in range(4):
            from_left, from_right = n_mat[0, t, A], n_mat[1, t, A]
            at_two_left = jnp.logical_or(spot == 1, spot == 2)
            at_two_right = jnp.logical_or(spot == 8, spot == 9)
            for u in range(8):
                p = jnp.where(at_two_left, pltpu.roll(from_left, (1 - 2 * u) % 128, 1), 0.0)
                shift = (8 - 2 * u) % 128
                q = pltpu.roll(from_right, shift, 1) if shift else from_right
                Hc[t, A * 8 + u] = jnp.where(at_two_right, q, p)
        return unused

    lax.fori_loop(0, 8, placed, 0)

    place = iota((64, 512), 1) % 16
    asked = jnp.where(place < 3, place + 13, place - 8) * 4 + col // 128
    pick_halo = (q == asked).astype(BF16)
    ends = jnp.concatenate([n_slot[0, 7:8, :], n_slot[1, 0:1, :]] + [n_slot[1, 0:1, :]] * 6, axis=0)
    slots = dot1(ends.astype(F32).astype(BF16), pick_halo)
    which = (iota((8, 512), 1) % 16 >= 8).astype(jnp.int32) == iota((8, 512), 0)
    slots = row_sum(jnp.where(which, slots, 0.0))
    GT_halo = (jnp.concatenate([slots] * 8, axis=0) == q.astype(F32)).astype(BF16)
    M_next = unpack_matrix(n_first[...])
    P_next = dotf(M_next, Pl[448:512, :])
    local_next = dotf(carried, M_next, NT) + n_off[0:1, :64]

    def halo_matvec(terms):
        rows = []
        for A in range(8):
            parts = []
            for u in range(8):
                total = None
                for t, v in terms:
                    term = Hc[t, A * 8 + u] * v
                    total = term if total is None else total + term
                parts.append(total)
            rows.append(fold(parts, 0))
        return fold(rows, 1)

    def halo_apply(v):
        return halo_matvec([(1, v), (0, pltpu.roll(v, 1, 1) * pat_halo[0]), (2, pltpu.roll(v, 127, 1) * pat_halo[1])])

    gather_wait(rv3, RV3, z, nz, v_recv.at[2])
    incoming = inflow(RV3, W3, nz) + nearer

    coarse = local + lanes_folded(diagonal(dotf(incoming, Pl[...], NT), 8))
    ce_ref[...] = coarse
    weights = jnp.where(own_block, dot2(coarse, GT), 0.0)
    total = None
    for m in range(4):
        w = row_sum(weights[:, m * 128 : m * 128 + 128]) * (1.0 / math.sqrt(64))
        term = tent[m] * jnp.concatenate([w] * 8, axis=0)
        total = term if total is None else total + term
    corr[...] = total
    next_first = dotf(incoming, P_next, NT) + local_next
    two = jnp.concatenate([incoming[0:1], next_first[0:1]] + [next_first[0:1]] * 6, axis=0)
    weights = jnp.where(which, dot2(two, GT_halo), 0.0)
    total = None
    for m in range(4):
        w = row_sum(weights[:, m * 128 : m * 128 + 128]) * (1.0 / math.sqrt(64))
        term = tent_halo[m] * w
        total = term if total is None else total + term
    c_halo = own_ends(corr, jnp.where(valid, total, 0.0))

    def post(ref, halo, emit):
        def left_of(k):
            return pltpu.roll(halo, 126 - 16 * k, 1)

        def right_of(k):
            return pltpu.roll(halo, 119 - 16 * k, 1)

        apply_with(ref[...], left_of, right_of, emit)

    def to_res(rows, y):
        res[rows, :] = y

    post(corr, c_halo, to_res)

    def prolong(rows, y):
        sol_ref[rows, :] = work[rows, :] + corr[rows, :] - SMOOTH * y

    block_apply(res[...], prolong)
    s_halo = s_halo + c_halo - SMOOTH * halo_matvec([(3, halo_apply(c_halo))])
    s_halo = jnp.where(valid, s_halo, 0.0)
    s_ends = own_ends(sol_ref, s_halo)

    def smooth(rows, y):
        sol_ref[rows, :] = sol_ref[rows, :] + DAMP * y

    post(sol_ref, s_ends, to_residue)
    block_apply(res[...], smooth)
    s_halo = s_halo + DAMP * halo_matvec([(3, b_halo - halo_apply(s_ends))])
    s_halo = jnp.where(valid, s_halo, 0.0)
    post(sol_ref, s_halo, to_residue)
    block_apply(res[...], smooth)


def body(nz, nx, ng, right_side, fine_blocks, fine_inverse, pattern, tentative, slot_map, coarse_inverse, coarse_lower):
    vmem = lambda *shape: pltpu.VMEM(shape, F32)
    dma = lambda *shape: pltpu.SemaphoreType.DMA(shape)
    top = max(nz, nx, ng)
    scratch = [
        vmem(3, 64, 64, 128), vmem(64, 64, 128), vmem(64, 128), pltpu.VMEM((2, 128), jnp.int32), vmem(4, 64, 128),
        pltpu.VMEM((8, 64), jnp.int32), vmem(64, 8, 64), vmem(64, 8, 64),
        vmem(64, 128), vmem(64, 128), vmem(64, 128),
        vmem(512, 64), vmem(512, 64), vmem(512, 64), vmem(ng * 64, 64), vmem(ng * 64, 64),
        vmem(nx * 64, 64), vmem(nx * 64, 64), vmem(nz * 64, 64),
        vmem(512, 64),
        pltpu.VMEM((ng * 64, 256), BF16), pltpu.VMEM((nx * 64, 256), BF16), pltpu.VMEM((nz * 64, 128), BF16),
        vmem(ng, 32, 128), vmem(nx, 32, 128), vmem(nz, 32, 128),
        vmem(ng, 8, 128), vmem(nx, 8, 128), vmem(nz, 8, 128),
        vmem(2, 2, 8, 128), vmem(2, 2, 8, 128),
        vmem(4, 64, 8, 128), vmem(2, 4, 8, 8, 128), vmem(2, 4, 8, 8, 128), vmem(2, 8, 8, 128), vmem(2, 8, 8, 128),
        pltpu.VMEM((2, 8, 64), jnp.int32), vmem(32, 128), vmem(8, 128), vmem(8, 128), vmem(32, 128),
        dma(10), dma(3, top), dma(3, top), dma(3, top), dma(3, top), dma(2, 2), dma(2, 2),
        dma(2, 6), dma(2, 6), dma(2), dma(2),
    ]
    result, coarse = pl.pallas_call(
        functools.partial(kernel, nz, nx, ng),
        out_shape=(
            jax.ShapeDtypeStruct((64, 128), F32),
            jax.ShapeDtypeStruct((8, 64), F32),
        ),
        in_specs=[pl.BlockSpec(memory_space=pl.ANY)] * 8,
        out_specs=(
            pl.BlockSpec(memory_space=pltpu.VMEM),
            pl.BlockSpec(memory_space=pltpu.VMEM),
        ),
        scratch_shapes=scratch,
        compiler_params=pltpu.CompilerParams(
            collective_id=0, has_side_effects=True, vmem_limit_bytes=60 * 2**20
        ),
        name="v_cycle",
    )(
        right_side, fine_blocks, fine_inverse, pattern, tentative, slot_map,
        jnp.transpose(coarse_inverse, (0, 2, 1)), jnp.transpose(coarse_lower, (0, 2, 1)),
    )
    return result, coarse.T


def solution(mesh):
    slabs, ng = mesh.shape["slab"], mesh.shape["group"]
    nx = 4 if slabs % 4 == 0 and slabs > 4 else 2
    both = ("slab", "group")
    in_specs = (
        P(None, both), P(None, None, None, both), P(None, None, both), P(None, both), P(None, None, both),
        P(both, None), P(None, None, both), P(None, None, both),
    )
    return jax.shard_map(
        functools.partial(body, slabs // nx, nx, ng),
        mesh=mesh,
        in_specs=in_specs,
        out_specs=(P(None, both), P(None, both)),
        check_vma=False,
    )
```

```python
import functools
import math

import jax
import jax.numpy as jnp
from jax import lax
from jax.experimental import pallas as pl
from jax.experimental.pallas import tpu as pltpu
from jax.sharding import PartitionSpec as P

DAMP = 0.8
SMOOTH = 0.67
F32 = jnp.float32
BF16 = jnp.bfloat16
MESH = pl.DeviceIdType.MESH

NN = (((1,), (0,)), ((), ()))
NT = (((1,), (1,)), ((), ()))


def split(x):
    hi = x.astype(BF16)
    return hi, (x - hi.astype(F32)).astype(BF16)


def dot1(a, b, dims=NN):
    return lax.dot_general(a, b, dims, preferred_element_type=F32)


def halves(t):
    n = t.shape[1] // 2
    return t[:, :n] + t[:, n:]


def dotf(a, b, dims=NN):
    return lax.dot_general(a, b, dims, precision=lax.Precision.HIGHEST, preferred_element_type=F32)


def dot2(a, b, dims=NN):
    t = dot1(jnp.concatenate(split(a), axis=0), b, dims)
    return t[: a.shape[0]] + t[a.shape[0] :]


def iota(shape, dim):
    return lax.broadcasted_iota(jnp.int32, shape, dim)


def fold(parts, axis):
    step = 1 if axis == 0 else 16
    at = iota((8, 128), axis) // step

    def mix(a, b, mask, shift):
        return jnp.where(mask, a, b) + pltpu.roll(jnp.where(mask, b, a), shift * step, axis)

    q = [parts[(i + 3) % 8] for i in range(8)]
    y = [mix(q[k], q[k + 4], ((at - k) & 7) < 4, 4) for k in range(4)]
    z = [mix(y[k], y[k + 2], ((at - k) & 3) >= 2, 2) for k in range(2)]
    return mix(z[0], z[1], (at & 1) == 1, 1)


def row_sum(x):
    x = x + pltpu.roll(x, 4, 0)
    x = x + pltpu.roll(x, 2, 0)
    return x + pltpu.roll(x, 1, 0)


def matvec(terms, width, emit):
    turns = 2 if len(terms) > 1 else 4

    def one(g, unused):
        for turn in range(turns):
            first = (g * turns + turn) * 8
            parts = []
            for a in range(8):
                total = None
                for load, v in terms:
                    product = load(first + a) * v
                    total = product if total is None else total + product
                parts.append(jnp.sum(total.reshape(width // 8, 8, 128), axis=0))
            emit(pl.ds(pl.multiple_of(first, 8), 8), fold(parts, 0))
        return unused

    lax.fori_loop(0, width // 8 // turns, one, 0)


def pack_matrix(m):
    return jnp.concatenate([m[:32, :], m[32:, :]], axis=1)


def unpack_matrix(p):
    return jnp.concatenate([p[:, :64], p[:, 64:]], axis=0)


def scan_products(refs, count):
    half = 1
    while half < count:
        for start in range(0, count, 2 * half):
            mid = start + half
            left = pl.ds(start * 64, half * 64)
            for ref in refs:
                ref[left, :] = dotf(ref[left, :], ref[pl.ds(mid * 64, 64), :])
        half *= 2


def scan_prefix(ref, count):
    half = 1
    while half < count:
        for start in range(0, count, 2 * half):
            mid = start + half
            right = pl.ds(mid * 64, half * 64)
            ref[right, :] = dotf(ref[right, :], ref[pl.ds((mid - 1) * 64, 64), :])
        half *= 2


def diagonal(x, count):
    return jnp.where(iota(x.shape, 0) == iota(x.shape, 1) // 64, x, 0.0)


def lanes_folded(x):
    t = x[:, 0:128] + x[:, 128:256] + x[:, 256:384] + x[:, 384:512]
    return t[:, :64] + t[:, 64:]


def padded(x):
    return jnp.concatenate([x, jnp.zeros_like(x)], axis=1)


def kernel(
    nz, nx, ng,
    b_h, f_h, i_h, pat_h, tent_h, slot_h, ci_h, cl_h,
    sol_ref, ce_ref,
    F, I, b, pat, tent, slot, ci, cl,
    work, res, corr,
    cis, Zl, Pl, Z1, Zm1, Z2, Zm2, Zm3,
    Xl, W1, W2, W3,
    RM1, RM2, RM3, RV1, RV2, RV3, halo_out, halo_in,
    Hc, msg, n_mat, vec, n_vec, n_slot, n_first, n_off, off_out, first_out,
    load_sem, m_send, m_recv, v_send, v_recv, h_send, h_recv, n_send, n_recv, f_send, f_recv,
):
    slab, g = lax.axis_index("slab"), lax.axis_index("group")
    z, x = slab // nx, slab % nx
    ns = nz * nx

    RM3[...] = jnp.zeros_like(RM3)
    RV3[...] = jnp.zeros_like(RV3)

    def in_group(o):
        return (slab, lax.rem(g + o, ng))

    def along_x(o):
        return (z * nx + lax.rem(x + o, nx), g)

    def along_z(o):
        return (lax.rem(z + o, nz) * nx + x, g)

    at_end, at_start = g == ng - 1, g == 0
    right = (jnp.where(at_end, lax.rem(slab + 1, ns), slab), lax.rem(g + 1, ng))
    left = (jnp.where(at_start, lax.rem(slab + ns - 1, ns), slab), lax.rem(g + ng - 1, ng))

    barrier = pltpu.get_barrier_semaphore()
    for o in range(1, nz):

        @pl.when(z + o >= nz)
        def _(o=o):
            pl.semaphore_signal(barrier, inc=1, device_id=along_z(o), device_id_type=MESH)

    peers = [along_x(o) for o in range(1, nx)] + [right, left] + [in_group(o) for o in range(1, ng)]
    for peer in peers:
        pl.semaphore_signal(barrier, inc=1, device_id=peer, device_id_type=MESH)

    copies = []
    for k, (src, dst) in enumerate(
        [(ci_h, ci), (cl_h, cl), (i_h, I), (b_h, b), (slot_h, slot), (pat_h, pat),
         (f_h.at[1], F.at[1]), (f_h.at[0], F.at[0]), (f_h.at[2], F.at[2]), (tent_h, tent)]
    ):
        copy = pltpu.make_async_copy(src, dst, load_sem.at[k])
        copy.start()
        copies.append(copy)
    ci_c, cl_c, i_c, b_c, slot_c, pat_c, f1_c, f0_c, f2_c, tent_c = copies

    row64, lane64 = iota((64, 64), 0), iota((64, 64), 1)
    eye = (row64 == lane64).astype(F32)
    ci_c.wait()
    cl_c.wait()
    for j in range(8):
        cij = ci[:, j, :]
        cis[pl.ds(j * 64, 64), :] = cij
        m = -dotf(cij, cl[:, j, :])
        Pl[pl.ds(j * 64, 64), :] = m
        e = m.T
        Zl[pl.ds(j * 64, 64), :] = e
        Xl[pl.ds(j * 64, 64), :] = e
    scan_products([Zl], 8)

    def perhaps(condition, act):
        if condition is None:
            act()
        else:
            pl.when(condition)(act)

    def gather_start(ref, own, target, count, send, recv, forward=False):
        started = []
        for o in range(1, count):
            copy = pltpu.make_async_remote_copy(
                src_ref=ref.at[own],
                dst_ref=ref.at[own],
                send_sem=send.at[o],
                recv_sem=recv.at[own],
                device_id=target(o),
                device_id_type=MESH,
            )
            condition = own + o < count if forward else None
            perhaps(condition, copy.start)
            started.append((condition, copy))
        return started

    def gather_wait(started, ref, own, count, recv, forward=False):
        for o in range(1, count):
            other = lax.rem(own + o, count)
            arrival = pltpu.make_async_copy(ref.at[other], ref.at[other], recv.at[other])
            perhaps(own + o >= count if forward else None, arrival.wait)
        for condition, copy in started:
            perhaps(condition, copy.wait_send)

    lane8, lane = iota((8, 128), 1), iota((64, 128), 1)
    has_left = jnp.logical_not(jnp.logical_and(slab == 0, at_start))
    has_right = jnp.logical_not(jnp.logical_and(slab == ns - 1, at_end))

    def halo_pack(turn, ref):
        to_right, to_left = jnp.zeros((8, 128), F32), jnp.zeros((8, 128), F32)
        for k in range(8):
            piece = ref[pl.ds(8 * k, 8), :]
            to_right = jnp.where(lane8 == k, pltpu.roll(piece, k + 1, 1), to_right)
            to_left = jnp.where(lane8 == k, pltpu.roll(piece, k, 1) if k else piece, to_left)
        halo_out[turn, 0] = to_right
        halo_out[turn, 1] = to_left

    def halo_send(turn):
        started = []
        for side, peer in ((0, right), (1, left)):
            copy = pltpu.make_async_remote_copy(
                src_ref=halo_out.at[turn, side],
                dst_ref=halo_in.at[turn, side],
                send_sem=h_send.at[turn, side],
                recv_sem=h_recv.at[turn, side],
                device_id=peer,
                device_id_type=MESH,
            )
            copy.start()
            started.append(copy)
        return started

    def apply_with(value, left_of, right_of, emit):
        before, after = [], []
        for k in range(8):
            piece = value[8 * k : 8 * k + 8]
            before.append(jnp.where(lane8 == 0, left_of(k), pltpu.roll(piece, 1, 1)))
            after.append(jnp.where(lane8 == 127, right_of(k), pltpu.roll(piece, 127, 1)))
        previous = jnp.concatenate(before, axis=0) * pat[0:1, :].astype(F32)
        following = jnp.concatenate(after, axis=0) * pat[1:2, :].astype(F32)
        matvec(
            [
                (lambda a: F[1, a], value),
                (lambda a: F[0, a], previous),
                (lambda a: F[2, a], following),
            ],
            64,
            emit,
        )

    def fine_apply(turn, ref, started, emit):
        for copy in started:
            copy.wait()
        from_left = jnp.where(has_left, halo_in[turn, 0], 0.0)
        from_right = jnp.where(has_right, halo_in[turn, 1], 0.0)

        def left_of(k):
            return pltpu.roll(from_left, 128 - k, 1) if k else from_left

        def right_of(k):
            return pltpu.roll(from_right, 127 - k, 1)

        apply_with(ref[...], left_of, right_of, emit)

    def block_apply(value, emit):
        matvec([(lambda a: I[a], value)], 64, emit)

    def to_residue(rows, y):
        res[rows, :] = b[rows, :] - y

    def sweep(turn, ref, started):
        fine_apply(turn, ref, started, to_residue)

        def emit(rows, y):
            ref[rows, :] = ref[rows, :] + DAMP * y

        block_apply(res[...], emit)

    def first(rows, y):
        work[rows, :] = DAMP * y

    i_c.wait()
    b_c.wait()
    block_apply(b[...], first)
    halo_pack(0, work)

    slot_c.wait()
    q, col = iota((64, 512), 0), iota((64, 512), 1)
    pick = (q == (col % 16) * 4 + col // 128).astype(BF16)
    own_block = iota((8, 512), 0) == (iota((8, 512), 1) % 128) // 16
    slots = dot1(slot[...].astype(F32).astype(BF16), pick)
    slots = row_sum(jnp.where(own_block, slots, 0.0))
    slots = jnp.concatenate([slots] * 8, axis=0)
    GT = (slots == q.astype(F32)).astype(BF16)

    group, spot = lane8 // 16, lane8 % 16
    at_left, at_right = spot < 3, jnp.logical_and(spot >= 8, spot < 11)

    def gather_lanes(pieces, shift, mask, out):
        for k in range(8):
            moved = pltpu.roll(pieces(k), shift + 16 * k, 1)
            out = jnp.where(jnp.logical_and(group == k, mask), moved, out)
        return out

    nothing = jnp.zeros((8, 128), F32)

    def pack_ends(place, pieces):
        vec[0, place] = gather_lanes(pieces, 3, at_left, nothing)
        vec[1, place] = gather_lanes(pieces, 8, at_right, nothing)

    beside = []

    def tell(src, dst, k, peer, send, recv):
        copy = pltpu.make_async_remote_copy(
            src_ref=src, dst_ref=dst, send_sem=send.at[k], recv_sem=recv.at[k], device_id=peer, device_id_type=MESH
        )
        copy.start()
        beside.append(copy)

    def tell_both(src, dst, k, part):
        for side, peer in ((0, right), (1, left)):
            here = src if part is None else src.at[side, part]
            there = dst.at[side] if part is None else dst.at[side, part]
            tell(here, there, k, peer, n_send.at[side], n_recv.at[side])

    first_out[...] = pack_matrix(Pl[0:64, :])
    pack_ends(0, lambda k: b[pl.ds(8 * k, 8), :])
    pat_c.wait()
    tent_c.wait()
    for m in range(4):
        pack_ends(2 + m, lambda k, m=m: tent[m, pl.ds(8 * k, 8), :])
    for r in range(2):
        row = jnp.broadcast_to(pat[r : r + 1, :].astype(F32), (8, 128))
        pack_ends(6 + r, lambda k: row)

    pl.semaphore_wait(barrier, len(peers) + nz - 1 - z)

    h0 = halo_send(0)
    RM1[g] = pack_matrix(Zl[0:64, :])
    rm1 = gather_start(RM1, g, in_group, ng, m_send.at[0], m_recv.at[0])

    def gathered(t, load):
        def one(A, unused):
            to_right, to_left = jnp.zeros((8, 128), F32), jnp.zeros((8, 128), F32)
            for u in range(8):
                whole = load(A * 8 + u)
                edge = jnp.zeros((8, 128), F32)
                for k in range(8):
                    piece = pltpu.roll(whole[8 * k : 8 * k + 8], (2 + 16 * k) % 128, 1)
                    edge = jnp.where(lane8 // 16 == k, piece, edge)
                here = (lane8 % 16) // 2 == u
                to_right = jnp.where(here, pltpu.roll(edge, 2 * u, 1) if u else edge, to_right)
                shift = (2 * u - 2) % 128
                to_left = jnp.where(here, pltpu.roll(edge, shift, 1) if shift else edge, to_left)
            msg[0, t, A] = to_right
            msg[1, t, A] = to_left
            return unused

        lax.fori_loop(0, 8, one, 0)

    tell(first_out, n_first, 1, left, f_send, f_recv)
    tell_both(slot, n_slot, 4, None)
    f1_c.wait()
    gathered(1, lambda a: F[1, a])
    tell_both(msg, n_mat, 1, 1)
    f0_c.wait()
    gathered(0, lambda a: F[0, a])
    tell_both(msg, n_mat, 0, 0)
    f2_c.wait()
    sweep(0, work, h0)
    halo_pack(1, work)
    h1 = halo_send(1)

    def upward(started, ref, own, count, recv, full, masked):
        gather_wait(started, ref, own, count, recv, full is None)
        for k in range(count):
            e = unpack_matrix(ref[k])
            rows = pl.ds(k * 64, 64)
            if full is not None:
                full[rows, :] = e
            masked[rows, :] = jnp.where(k < own, e, eye)
        scan_products([masked] if full is None else [full, masked], count)

    def later(ref, h, count):
        return ref[pl.ds((h + 1) * 64, 64), :] if h + 1 < count else eye

    upward(rm1, RM1, g, ng, m_recv.at[0], Z1, Zm1)
    RM2[x] = pack_matrix(Z1[0:64, :])
    rm2 = gather_start(RM2, x, along_x, nx, m_send.at[1], m_recv.at[1])
    def weigh(ref, h, parts):
        ref[pl.ds(h * 64, 64), :] = jnp.concatenate(split(jnp.concatenate(parts, axis=1)), axis=1)

    for h in range(ng):
        weigh(W1, h, [later(Z1, h, ng), jnp.where(h < g, later(Zm1, h, ng), 0.0)])

    pack_ends(1, lambda k: work[pl.ds(8 * k, 8), :])
    for side, peer in ((0, right), (1, left)):
        tell(vec.at[side], n_vec.at[side], 5, peer, n_send.at[side], n_recv.at[side])
    gathered(2, lambda a: F[2, a])
    tell_both(msg, n_mat, 2, 2)

    fine_apply(1, work, h1, to_residue)
    residue = res[...]
    values = []
    for m in range(4):
        weight = jnp.sum((tent[m] * residue).reshape(8, 8, 128), axis=0)
        values.append(row_sum(weight) * (1.0 / math.sqrt(64)))
    spread = jnp.where(own_block, jnp.concatenate(values, axis=1), 0.0)
    rhs = dot2(spread, GT, NT)
    offsets = diagonal(dotf(rhs, cis[...], NT), 8)
    after_own = jnp.concatenate([Zl[64:512, :], eye], axis=0)
    RV1[g] = padded(row_sum(dotf(offsets, after_own)))
    rv1 = gather_start(RV1, g, in_group, ng, v_send.at[0], v_recv.at[0])

    upward(rm2, RM2, x, nx, m_recv.at[1], Z2, Zm2)
    RM3[z] = pack_matrix(Z2[0:64, :])
    rm3 = gather_start(RM3, z, along_z, nz, m_send.at[2], m_recv.at[2], True)
    for h in range(nx):
        weigh(W2, h, [later(Z2, h, nx), jnp.where(h < x, later(Zm2, h, nx), 0.0)])

    own = lanes_folded(offsets)
    off_out[...] = padded(own)
    tell(off_out, n_off, 0, left, f_send, f_recv)
    gathered(3, lambda a: I[a])
    tell_both(msg, n_mat, 3, 3)

    def inflow(ref, weights, count):
        flat = [ref[h] + pltpu.roll(ref[h + 1], 64, 1) for h in range(0, count, 2)]
        return halves(dot2(jnp.concatenate(flat, axis=1), weights[...]))


    gather_wait(rv1, RV1, g, ng, v_recv.at[0])
    flow1 = inflow(RV1, W1, ng)
    RV2[x] = padded(flow1[:, :64])
    rv2 = gather_start(RV2, x, along_x, nx, v_send.at[1], v_recv.at[1])

    scan_prefix(Pl, 8)

    row8 = iota((8, 64), 0)
    carried = jnp.broadcast_to(own[0:1], (8, 64))
    local = carried
    for j in range(1, 8):
        carried = dotf(carried, Xl[pl.ds(j * 64, 64), :]) + own[j : j + 1]
        local = jnp.where(row8 >= j, carried, local)


    gather_wait(rv2, RV2, x, nx, v_recv.at[1])
    flow2 = inflow(RV2, W2, nx)
    RV3[z] = padded(flow2[:, :64])
    rv3 = gather_start(RV3, z, along_z, nz, v_send.at[2], v_recv.at[2], True)

    upward(rm3, RM3, z, nz, m_recv.at[2], None, Zm3)
    A1 = Zm1[0:64, :]
    A21 = dotf(Zm2[0:64, :], A1)
    for h in range(nz):
        weigh(W3, h, [dotf(jnp.where(h < z, later(Zm3, h, nz), 0.0), A21)])

    nearer = dotf(flow2[:, 64:], A1) + flow1[:, 64:]
    for copy in beside:
        copy.wait()
    valid = jnp.logical_or(jnp.logical_and(at_left, has_left), jnp.logical_and(at_right, has_right))

    def own_ends(ref, out):
        out = gather_lanes(lambda k: ref[pl.ds(8 * k, 8), :], 3, spot == 3, out)
        return gather_lanes(lambda k: ref[pl.ds(8 * k, 8), :], 8, spot == 7, out)

    b_halo, s_halo, *tent_halo = [n_vec[0, k] + n_vec[1, k] for k in range(6)]
    pat_halo = [n_vec[0, k] + n_vec[1, k] for k in (6, 7)]

    def placed(A, unused):
        for t in range(4):
            from_left, from_right = n_mat[0, t, A], n_mat[1, t, A]
            at_two_left = jnp.logical_or(spot == 1, spot == 2)
            at_two_right = jnp.logical_or(spot == 8, spot == 9)
            for u in range(8):
                p = jnp.where(at_two_left, pltpu.roll(from_left, (1 - 2 * u) % 128, 1), 0.0)
                shift = (8 - 2 * u) % 128
                q = pltpu.roll(from_right, shift, 1) if shift else from_right
                Hc[t, A * 8 + u] = jnp.where(at_two_right, q, p)
        return unused

    lax.fori_loop(0, 8, placed, 0)

    place = iota((64, 512), 1) % 16
    asked = jnp.where(place < 3, place + 13, place - 8) * 4 + col // 128
    pick_halo = (q == asked).astype(BF16)
    ends = jnp.concatenate([n_slot[0, 7:8, :], n_slot[1, 0:1, :]] + [n_slot[1, 0:1, :]] * 6, axis=0)
    slots = dot1(ends.astype(F32).astype(BF16), pick_halo)
    which = (iota((8, 512), 1) % 16 >= 8).astype(jnp.int32) == iota((8, 512), 0)
    slots = row_sum(jnp.where(which, slots, 0.0))
    GT_halo = (jnp.concatenate([slots] * 8, axis=0) == q.astype(F32)).astype(BF16)
    M_next = unpack_matrix(n_first[...])
    P_next = dotf(M_next, Pl[448:512, :])
    local_next = dotf(carried, M_next, NT) + n_off[0:1, :64]

    def halo_matvec(terms):
        rows = []
        for A in range(8):
            parts = []
            for u in range(8):
                total = None
                for t, v in terms:
                    term = Hc[t, A * 8 + u] * v
                    total = term if total is None else total + term
                parts.append(total)
            rows.append(fold(parts, 0))
        return fold(rows, 1)

    def halo_apply(v):
        return halo_matvec([(1, v), (0, pltpu.roll(v, 1, 1) * pat_halo[0]), (2, pltpu.roll(v, 127, 1) * pat_halo[1])])

    gather_wait(rv3, RV3, z, nz, v_recv.at[2], True)
    incoming = inflow(RV3, W3, nz) + nearer

    coarse = local + lanes_folded(diagonal(dotf(incoming, Pl[...], NT), 8))
    ce_ref[...] = coarse
    weights = jnp.where(own_block, dot2(coarse, GT), 0.0)
    total = None
    for m in range(4):
        w = row_sum(weights[:, m * 128 : m * 128 + 128]) * (1.0 / math.sqrt(64))
        term = tent[m] * jnp.concatenate([w] * 8, axis=0)
        total = term if total is None else total + term
    corr[...] = total
    next_first = dotf(incoming, P_next, NT) + local_next
    two = jnp.concatenate([incoming[0:1], next_first[0:1]] + [next_first[0:1]] * 6, axis=0)
    weights = jnp.where(which, dot2(two, GT_halo), 0.0)
    total = None
    for m in range(4):
        w = row_sum(weights[:, m * 128 : m * 128 + 128]) * (1.0 / math.sqrt(64))
        term = tent_halo[m] * w
        total = term if total is None else total + term
    c_halo = own_ends(corr, jnp.where(valid, total, 0.0))

    def post(ref, halo, emit):
        def left_of(k):
            return pltpu.roll(halo, 126 - 16 * k, 1)

        def right_of(k):
            return pltpu.roll(halo, 119 - 16 * k, 1)

        apply_with(ref[...], left_of, right_of, emit)

    def to_res(rows, y):
        res[rows, :] = y

    post(corr, c_halo, to_res)

    def prolong(rows, y):
        sol_ref[rows, :] = work[rows, :] + corr[rows, :] - SMOOTH * y

    block_apply(res[...], prolong)
    s_halo = s_halo + c_halo - SMOOTH * halo_matvec([(3, halo_apply(c_halo))])
    s_halo = jnp.where(valid, s_halo, 0.0)
    s_ends = own_ends(sol_ref, s_halo)

    def smooth(rows, y):
        sol_ref[rows, :] = sol_ref[rows, :] + DAMP * y

    post(sol_ref, s_ends, to_residue)
    block_apply(res[...], smooth)
    s_halo = s_halo + DAMP * halo_matvec([(3, b_halo - halo_apply(s_ends))])
    s_halo = jnp.where(valid, s_halo, 0.0)
    post(sol_ref, s_halo, to_residue)
    block_apply(res[...], smooth)


def body(nz, nx, ng, right_side, fine_blocks, fine_inverse, pattern, tentative, slot_map, coarse_inverse, coarse_lower):
    vmem = lambda *shape: pltpu.VMEM(shape, F32)
    dma = lambda *shape: pltpu.SemaphoreType.DMA(shape)
    top = max(nz, nx, ng)
    scratch = [
        vmem(3, 64, 64, 128), vmem(64, 64, 128), vmem(64, 128), pltpu.VMEM((2, 128), jnp.int32), vmem(4, 64, 128),
        pltpu.VMEM((8, 64), jnp.int32), vmem(64, 8, 64), vmem(64, 8, 64),
        vmem(64, 128), vmem(64, 128), vmem(64, 128),
        vmem(512, 64), vmem(512, 64), vmem(512, 64), vmem(ng * 64, 64), vmem(ng * 64, 64),
        vmem(nx * 64, 64), vmem(nx * 64, 64), vmem(nz * 64, 64),
        vmem(512, 64),
        pltpu.VMEM((ng * 64, 256), BF16), pltpu.VMEM((nx * 64, 256), BF16), pltpu.VMEM((nz * 64, 128), BF16),
        vmem(ng, 32, 128), vmem(nx, 32, 128), vmem(nz, 32, 128),
        vmem(ng, 8, 128), vmem(nx, 8, 128), vmem(nz, 8, 128),
        vmem(2, 2, 8, 128), vmem(2, 2, 8, 128),
        vmem(4, 64, 8, 128), vmem(2, 4, 8, 8, 128), vmem(2, 4, 8, 8, 128), vmem(2, 8, 8, 128), vmem(2, 8, 8, 128),
        pltpu.VMEM((2, 8, 64), jnp.int32), vmem(32, 128), vmem(8, 128), vmem(8, 128), vmem(32, 128),
        dma(10), dma(3, top), dma(3, top), dma(3, top), dma(3, top), dma(2, 2), dma(2, 2),
        dma(2, 6), dma(2, 6), dma(2), dma(2),
    ]
    result, coarse = pl.pallas_call(
        functools.partial(kernel, nz, nx, ng),
        out_shape=(
            jax.ShapeDtypeStruct((64, 128), F32),
            jax.ShapeDtypeStruct((8, 64), F32),
        ),
        in_specs=[pl.BlockSpec(memory_space=pl.ANY)] * 8,
        out_specs=(
            pl.BlockSpec(memory_space=pltpu.VMEM),
            pl.BlockSpec(memory_space=pltpu.VMEM),
        ),
        scratch_shapes=scratch,
        compiler_params=pltpu.CompilerParams(
            collective_id=0, has_side_effects=True, vmem_limit_bytes=60 * 2**20
        ),
        name="v_cycle",
    )(
        right_side, fine_blocks, fine_inverse, pattern, tentative, slot_map,
        jnp.transpose(coarse_inverse, (0, 2, 1)), jnp.transpose(coarse_lower, (0, 2, 1)),
    )
    return result, coarse.T


def solution(mesh):
    slabs, ng = mesh.shape["slab"], mesh.shape["group"]
    nx = 4 if slabs % 4 == 0 and slabs > 4 else 2
    both = ("slab", "group")
    in_specs = (
        P(None, both), P(None, None, None, both), P(None, None, both), P(None, both), P(None, None, both),
        P(both, None), P(None, None, both), P(None, None, both),
    )
    return jax.shard_map(
        functools.partial(body, slabs // nx, nx, ng),
        mesh=mesh,
        in_specs=in_specs,
        out_specs=(P(None, both), P(None, both)),
        check_vma=False,
    )
```

```python
import functools
import math

import jax
import jax.numpy as jnp
from jax import lax
from jax.experimental import pallas as pl
from jax.experimental.pallas import tpu as pltpu
from jax.sharding import PartitionSpec as P

DAMP = 0.8
SMOOTH = 0.67
F32 = jnp.float32
BF16 = jnp.bfloat16
MESH = pl.DeviceIdType.MESH

NN = (((1,), (0,)), ((), ()))
NT = (((1,), (1,)), ((), ()))


def split(x):
    hi = x.astype(BF16)
    return hi, (x - hi.astype(F32)).astype(BF16)


def dot1(a, b, dims=NN):
    return lax.dot_general(a, b, dims, preferred_element_type=F32)


def halves(t):
    n = t.shape[1] // 2
    return t[:, :n] + t[:, n:]


def dotf(a, b, dims=NN):
    return lax.dot_general(a, b, dims, precision=lax.Precision.HIGHEST, preferred_element_type=F32)


def dot2(a, b, dims=NN):
    t = dot1(jnp.concatenate(split(a), axis=0), b, dims)
    return t[: a.shape[0]] + t[a.shape[0] :]


def iota(shape, dim):
    return lax.broadcasted_iota(jnp.int32, shape, dim)


def fold(parts, axis):
    step = 1 if axis == 0 else 16
    at = iota((8, 128), axis) // step

    def mix(a, b, mask, shift):
        return jnp.where(mask, a, b) + pltpu.roll(jnp.where(mask, b, a), shift * step, axis)

    q = [parts[(i + 3) % 8] for i in range(8)]
    y = [mix(q[k], q[k + 4], ((at - k) & 7) < 4, 4) for k in range(4)]
    z = [mix(y[k], y[k + 2], ((at - k) & 3) >= 2, 2) for k in range(2)]
    return mix(z[0], z[1], (at & 1) == 1, 1)


def row_sum(x):
    x = x + pltpu.roll(x, 4, 0)
    x = x + pltpu.roll(x, 2, 0)
    return x + pltpu.roll(x, 1, 0)


def matvec(terms, width, emit):
    turns = 4 if len(terms) > 1 else 8

    def one(g, unused):
        for turn in range(turns):
            first = (g * turns + turn) * 8
            parts = []
            for a in range(8):
                total = None
                for load, v in terms:
                    product = load(first + a) * v
                    total = product if total is None else total + product
                parts.append(jnp.sum(total.reshape(width // 8, 8, 128), axis=0))
            emit(pl.ds(pl.multiple_of(first, 8), 8), fold(parts, 0))
        return unused

    lax.fori_loop(0, width // 8 // turns, one, 0)


def pack_matrix(m):
    return jnp.concatenate([m[:32, :], m[32:, :]], axis=1)


def unpack_matrix(p):
    return jnp.concatenate([p[:, :64], p[:, 64:]], axis=0)


def scan_products(refs, count):
    half = 1
    while half < count:
        for start in range(0, count, 2 * half):
            mid = start + half
            left = pl.ds(start * 64, half * 64)
            for ref in refs:
                ref[left, :] = dotf(ref[left, :], ref[pl.ds(mid * 64, 64), :])
        half *= 2


def scan_prefix(ref, count):
    half = 1
    while half < count:
        for start in range(0, count, 2 * half):
            mid = start + half
            right = pl.ds(mid * 64, half * 64)
            ref[right, :] = dotf(ref[right, :], ref[pl.ds((mid - 1) * 64, 64), :])
        half *= 2


def diagonal(x, count):
    return jnp.where(iota(x.shape, 0) == iota(x.shape, 1) // 64, x, 0.0)


def lanes_folded(x):
    t = x[:, 0:128] + x[:, 128:256] + x[:, 256:384] + x[:, 384:512]
    return t[:, :64] + t[:, 64:]


def padded(x):
    return jnp.concatenate([x, jnp.zeros_like(x)], axis=1)


def kernel(
    nz, nx, ng,
    b_h, f_h, i_h, pat_h, tent_h, slot_h, ci_h, cl_h,
    sol_ref, ce_ref,
    F, I, b, pat, tent, slot, ci, cl,
    work, res, corr,
    cis, Zl, Pl, Z1, Zm1, Z2, Zm2, Zm3,
    Xl, W1, W2, W3,
    RM1, RM2, RM3, RV1, RV2, RV3, halo_out, halo_in,
    Hc, msg, n_mat, vec, n_vec, n_slot, n_first, n_off, off_out, first_out,
    load_sem, m_send, m_recv, v_send, v_recv, h_send, h_recv, n_send, n_recv, f_send, f_recv,
):
    slab, g = lax.axis_index("slab"), lax.axis_index("group")
    z, x = slab // nx, slab % nx
    ns = nz * nx

    RM3[...] = jnp.zeros_like(RM3)
    RV3[...] = jnp.zeros_like(RV3)

    def in_group(o):
        return (slab, lax.rem(g + o, ng))

    def along_x(o):
        return (z * nx + lax.rem(x + o, nx), g)

    def along_z(o):
        return (lax.rem(z + o, nz) * nx + x, g)

    at_end, at_start = g == ng - 1, g == 0
    right = (jnp.where(at_end, lax.rem(slab + 1, ns), slab), lax.rem(g + 1, ng))
    left = (jnp.where(at_start, lax.rem(slab + ns - 1, ns), slab), lax.rem(g + ng - 1, ng))

    barrier = pltpu.get_barrier_semaphore()
    for o in range(1, nz):

        @pl.when(z + o >= nz)
        def _(o=o):
            pl.semaphore_signal(barrier, inc=1, device_id=along_z(o), device_id_type=MESH)

    peers = [along_x(o) for o in range(1, nx)] + [right, left] + [in_group(o) for o in range(1, ng)]
    for peer in peers:
        pl.semaphore_signal(barrier, inc=1, device_id=peer, device_id_type=MESH)

    copies = []
    for k, (src, dst) in enumerate(
        [(ci_h, ci), (cl_h, cl), (i_h, I), (b_h, b), (slot_h, slot), (pat_h, pat),
         (f_h.at[1], F.at[1]), (f_h.at[0], F.at[0]), (f_h.at[2], F.at[2]), (tent_h, tent)]
    ):
        copy = pltpu.make_async_copy(src, dst, load_sem.at[k])
        copy.start()
        copies.append(copy)
    ci_c, cl_c, i_c, b_c, slot_c, pat_c, f1_c, f0_c, f2_c, tent_c = copies

    row64, lane64 = iota((64, 64), 0), iota((64, 64), 1)
    eye = (row64 == lane64).astype(F32)
    ci_c.wait()
    cl_c.wait()
    for j in range(8):
        cij = ci[:, j, :]
        cis[pl.ds(j * 64, 64), :] = cij
        m = -dotf(cij, cl[:, j, :])
        Pl[pl.ds(j * 64, 64), :] = m
        e = m.T
        Zl[pl.ds(j * 64, 64), :] = e
        Xl[pl.ds(j * 64, 64), :] = e
    scan_products([Zl], 8)

    def perhaps(condition, act):
        if condition is None:
            act()
        else:
            pl.when(condition)(act)

    def gather_start(ref, own, target, count, send, recv, forward=False):
        started = []
        for o in range(1, count):
            copy = pltpu.make_async_remote_copy(
                src_ref=ref.at[own],
                dst_ref=ref.at[own],
                send_sem=send.at[o],
                recv_sem=recv.at[own],
                device_id=target(o),
                device_id_type=MESH,
            )
            condition = own + o < count if forward else None
            perhaps(condition, copy.start)
            started.append((condition, copy))
        return started

    def gather_wait(started, ref, own, count, recv, forward=False):
        for o in range(1, count):
            other = lax.rem(own + o, count)
            arrival = pltpu.make_async_copy(ref.at[other], ref.at[other], recv.at[other])
            perhaps(own + o >= count if forward else None, arrival.wait)
        for condition, copy in started:
            perhaps(condition, copy.wait_send)

    lane8, lane = iota((8, 128), 1), iota((64, 128), 1)
    has_left = jnp.logical_not(jnp.logical_and(slab == 0, at_start))
    has_right = jnp.logical_not(jnp.logical_and(slab == ns - 1, at_end))

    def halo_pack(turn, ref):
        to_right, to_left = jnp.zeros((8, 128), F32), jnp.zeros((8, 128), F32)
        for k in range(8):
            piece = ref[pl.ds(8 * k, 8), :]
            to_right = jnp.where(lane8 == k, pltpu.roll(piece, k + 1, 1), to_right)
            to_left = jnp.where(lane8 == k, pltpu.roll(piece, k, 1) if k else piece, to_left)
        halo_out[turn, 0] = to_right
        halo_out[turn, 1] = to_left

    def halo_send(turn):
        started = []
        for side, peer in ((0, right), (1, left)):
            copy = pltpu.make_async_remote_copy(
                src_ref=halo_out.at[turn, side],
                dst_ref=halo_in.at[turn, side],
                send_sem=h_send.at[turn, side],
                recv_sem=h_recv.at[turn, side],
                device_id=peer,
                device_id_type=MESH,
            )
            copy.start()
            started.append(copy)
        return started

    def apply_with(value, left_of, right_of, emit):
        before, after = [], []
        for k in range(8):
            piece = value[8 * k : 8 * k + 8]
            before.append(jnp.where(lane8 == 0, left_of(k), pltpu.roll(piece, 1, 1)))
            after.append(jnp.where(lane8 == 127, right_of(k), pltpu.roll(piece, 127, 1)))
        previous = jnp.concatenate(before, axis=0) * pat[0:1, :].astype(F32)
        following = jnp.concatenate(after, axis=0) * pat[1:2, :].astype(F32)
        matvec(
            [
                (lambda a: F[1, a], value),
                (lambda a: F[0, a], previous),
                (lambda a: F[2, a], following),
            ],
            64,
            emit,
        )

    def fine_apply(turn, ref, started, emit):
        for copy in started:
            copy.wait()
        from_left = jnp.where(has_left, halo_in[turn, 0], 0.0)
        from_right = jnp.where(has_right, halo_in[turn, 1], 0.0)

        def left_of(k):
            return pltpu.roll(from_left, 128 - k, 1) if k else from_left

        def right_of(k):
            return pltpu.roll(from_right, 127 - k, 1)

        apply_with(ref[...], left_of, right_of, emit)

    def block_apply(value, emit):
        matvec([(lambda a: I[a], value)], 64, emit)

    def to_residue(rows, y):
        res[rows, :] = b[rows, :] - y

    def sweep(turn, ref, started):
        fine_apply(turn, ref, started, to_residue)

        def emit(rows, y):
            ref[rows, :] = ref[rows, :] + DAMP * y

        block_apply(res[...], emit)

    def first(rows, y):
        work[rows, :] = DAMP * y

    i_c.wait()
    b_c.wait()
    block_apply(b[...], first)
    halo_pack(0, work)

    slot_c.wait()
    q, col = iota((64, 512), 0), iota((64, 512), 1)
    pick = (q == (col % 16) * 4 + col // 128).astype(BF16)
    own_block = iota((8, 512), 0) == (iota((8, 512), 1) % 128) // 16
    slots = dot1(slot[...].astype(F32).astype(BF16), pick)
    slots = row_sum(jnp.where(own_block, slots, 0.0))
    slots = jnp.concatenate([slots] * 8, axis=0)
    GT = (slots == q.astype(F32)).astype(BF16)

    group, spot = lane8 // 16, lane8 % 16
    at_left, at_right = spot < 3, jnp.logical_and(spot >= 8, spot < 11)

    def gather_lanes(pieces, shift, mask, out):
        for k in range(8):
            moved = pltpu.roll(pieces(k), shift + 16 * k, 1)
            out = jnp.where(jnp.logical_and(group == k, mask), moved, out)
        return out

    nothing = jnp.zeros((8, 128), F32)

    def pack_ends(place, pieces):
        vec[0, place] = gather_lanes(pieces, 3, at_left, nothing)
        vec[1, place] = gather_lanes(pieces, 8, at_right, nothing)

    beside = {}

    def tell(src, dst, k, peer, send, recv, tag):
        copy = pltpu.make_async_remote_copy(
            src_ref=src, dst_ref=dst, send_sem=send.at[k], recv_sem=recv.at[k], device_id=peer, device_id_type=MESH
        )
        copy.start()
        beside.setdefault(tag, []).append(copy)

    def told(*tags):
        for tag in tags:
            for copy in beside[tag]:
                copy.wait()

    def tell_both(src, dst, k, part):
        for side, peer in ((0, right), (1, left)):
            here = src if part is None else src.at[side, part]
            there = dst.at[side] if part is None else dst.at[side, part]
            tell(here, there, k, peer, n_send.at[side], n_recv.at[side], k)

    first_out[...] = pack_matrix(Pl[0:64, :])
    pack_ends(0, lambda k: b[pl.ds(8 * k, 8), :])
    pat_c.wait()
    tent_c.wait()
    for m in range(4):
        pack_ends(2 + m, lambda k, m=m: tent[m, pl.ds(8 * k, 8), :])
    for r in range(2):
        row = jnp.broadcast_to(pat[r : r + 1, :].astype(F32), (8, 128))
        pack_ends(6 + r, lambda k: row)

    pl.semaphore_wait(barrier, len(peers) + nz - 1 - z)

    h0 = halo_send(0)
    RM1[g] = pack_matrix(Zl[0:64, :])
    rm1 = gather_start(RM1, g, in_group, ng, m_send.at[0], m_recv.at[0])

    def gathered(t, load):
        def one(A, unused):
            to_right, to_left = jnp.zeros((8, 128), F32), jnp.zeros((8, 128), F32)
            for u in range(8):
                whole = load(A * 8 + u)
                edge = jnp.zeros((8, 128), F32)
                for k in range(8):
                    piece = pltpu.roll(whole[8 * k : 8 * k + 8], (2 + 16 * k) % 128, 1)
                    edge = jnp.where(lane8 // 16 == k, piece, edge)
                here = (lane8 % 16) // 2 == u
                to_right = jnp.where(here, pltpu.roll(edge, 2 * u, 1) if u else edge, to_right)
                shift = (2 * u - 2) % 128
                to_left = jnp.where(here, pltpu.roll(edge, shift, 1) if shift else edge, to_left)
            msg[0, t, A] = to_right
            msg[1, t, A] = to_left
            return unused

        lax.fori_loop(0, 8, one, 0)

    tell(first_out, n_first, 1, left, f_send, f_recv, "first")
    tell_both(slot, n_slot, 4, None)
    f1_c.wait()
    gathered(1, lambda a: F[1, a])
    tell_both(msg, n_mat, 1, 1)
    f0_c.wait()
    gathered(0, lambda a: F[0, a])
    tell_both(msg, n_mat, 0, 0)
    f2_c.wait()
    sweep(0, work, h0)
    halo_pack(1, work)
    h1 = halo_send(1)

    def upward(started, ref, own, count, recv, full, masked):
        gather_wait(started, ref, own, count, recv, full is None)
        for k in range(count):
            e = unpack_matrix(ref[k])
            rows = pl.ds(k * 64, 64)
            if full is not None:
                full[rows, :] = e
            masked[rows, :] = jnp.where(k < own, e, eye)
        scan_products([masked] if full is None else [full, masked], count)

    def later(ref, h, count):
        return ref[pl.ds((h + 1) * 64, 64), :] if h + 1 < count else eye

    upward(rm1, RM1, g, ng, m_recv.at[0], Z1, Zm1)
    RM2[x] = pack_matrix(Z1[0:64, :])
    rm2 = gather_start(RM2, x, along_x, nx, m_send.at[1], m_recv.at[1])
    def weigh(ref, h, parts):
        ref[pl.ds(h * 64, 64), :] = jnp.concatenate(split(jnp.concatenate(parts, axis=1)), axis=1)

    for h in range(ng):
        weigh(W1, h, [later(Z1, h, ng), jnp.where(h < g, later(Zm1, h, ng), 0.0)])

    pack_ends(1, lambda k: work[pl.ds(8 * k, 8), :])
    for side, peer in ((0, right), (1, left)):
        tell(vec.at[side], n_vec.at[side], 5, peer, n_send.at[side], n_recv.at[side], 5)
    gathered(2, lambda a: F[2, a])
    tell_both(msg, n_mat, 2, 2)

    fine_apply(1, work, h1, to_residue)
    residue = res[...]
    values = []
    for m in range(4):
        weight = jnp.sum((tent[m] * residue).reshape(8, 8, 128), axis=0)
        values.append(row_sum(weight) * (1.0 / math.sqrt(64)))
    spread = jnp.where(own_block, jnp.concatenate(values, axis=1), 0.0)
    rhs = dot2(spread, GT, NT)
    offsets = diagonal(dotf(rhs, cis[...], NT), 8)
    after_own = jnp.concatenate([Zl[64:512, :], eye], axis=0)
    RV1[g] = padded(row_sum(dotf(offsets, after_own)))
    rv1 = gather_start(RV1, g, in_group, ng, v_send.at[0], v_recv.at[0])

    upward(rm2, RM2, x, nx, m_recv.at[1], Z2, Zm2)
    RM3[z] = pack_matrix(Z2[0:64, :])
    rm3 = gather_start(RM3, z, along_z, nz, m_send.at[2], m_recv.at[2], True)
    for h in range(nx):
        weigh(W2, h, [later(Z2, h, nx), jnp.where(h < x, later(Zm2, h, nx), 0.0)])

    own = lanes_folded(offsets)
    off_out[...] = padded(own)
    tell(off_out, n_off, 0, left, f_send, f_recv, "off")
    gathered(3, lambda a: I[a])
    tell_both(msg, n_mat, 3, 3)

    def inflow(ref, weights, count):
        flat = [ref[h] + pltpu.roll(ref[h + 1], 64, 1) for h in range(0, count, 2)]
        return halves(dot2(jnp.concatenate(flat, axis=1), weights[...]))


    gather_wait(rv1, RV1, g, ng, v_recv.at[0])
    flow1 = inflow(RV1, W1, ng)
    RV2[x] = padded(flow1[:, :64])
    rv2 = gather_start(RV2, x, along_x, nx, v_send.at[1], v_recv.at[1])

    scan_prefix(Pl, 8)

    row8 = iota((8, 64), 0)
    carried = jnp.broadcast_to(own[0:1], (8, 64))
    local = carried
    for j in range(1, 8):
        carried = dotf(carried, Xl[pl.ds(j * 64, 64), :]) + own[j : j + 1]
        local = jnp.where(row8 >= j, carried, local)


    told(5)
    valid = jnp.logical_or(jnp.logical_and(at_left, has_left), jnp.logical_and(at_right, has_right))

    def own_ends(ref, out):
        out = gather_lanes(lambda k: ref[pl.ds(8 * k, 8), :], 3, spot == 3, out)
        return gather_lanes(lambda k: ref[pl.ds(8 * k, 8), :], 8, spot == 7, out)

    b_halo, s_halo, *tent_halo = [n_vec[0, k] + n_vec[1, k] for k in range(6)]
    pat_halo = [n_vec[0, k] + n_vec[1, k] for k in (6, 7)]

    def place(t):
        at_two_left = jnp.logical_or(spot == 1, spot == 2)
        at_two_right = jnp.logical_or(spot == 8, spot == 9)

        def one(A, unused):
            from_left, from_right = n_mat[0, t, A], n_mat[1, t, A]
            for u in range(8):
                p = jnp.where(at_two_left, pltpu.roll(from_left, (1 - 2 * u) % 128, 1), 0.0)
                shift = (8 - 2 * u) % 128
                q = pltpu.roll(from_right, shift, 1) if shift else from_right
                Hc[t, A * 8 + u] = jnp.where(at_two_right, q, p)
            return unused

        lax.fori_loop(0, 8, one, 0)

    told(1, 0, 2)
    place(1)
    place(0)
    place(2)

    told(4, "first")
    near = iota((64, 512), 1) % 16
    asked = jnp.where(near < 3, near + 13, near - 8) * 4 + col // 128
    pick_halo = (q == asked).astype(BF16)
    ends = jnp.concatenate([n_slot[0, 7:8, :], n_slot[1, 0:1, :]] + [n_slot[1, 0:1, :]] * 6, axis=0)
    slots = dot1(ends.astype(F32).astype(BF16), pick_halo)
    which = (iota((8, 512), 1) % 16 >= 8).astype(jnp.int32) == iota((8, 512), 0)
    slots = row_sum(jnp.where(which, slots, 0.0))
    GT_halo = (jnp.concatenate([slots] * 8, axis=0) == q.astype(F32)).astype(BF16)
    M_next = unpack_matrix(n_first[...])
    P_next = dotf(M_next, Pl[448:512, :])

    gather_wait(rv2, RV2, x, nx, v_recv.at[1])
    flow2 = inflow(RV2, W2, nx)
    RV3[z] = padded(flow2[:, :64])
    rv3 = gather_start(RV3, z, along_z, nz, v_send.at[2], v_recv.at[2], True)

    upward(rm3, RM3, z, nz, m_recv.at[2], None, Zm3)
    A1 = Zm1[0:64, :]
    A21 = dotf(Zm2[0:64, :], A1)
    for h in range(nz):
        weigh(W3, h, [dotf(jnp.where(h < z, later(Zm3, h, nz), 0.0), A21)])

    nearer = dotf(flow2[:, 64:], A1) + flow1[:, 64:]
    told(3)
    place(3)
    told("off")
    local_next = dotf(carried, M_next, NT) + n_off[0:1, :64]

    def halo_matvec(terms):
        rows = []
        for A in range(8):
            parts = []
            for u in range(8):
                total = None
                for t, v in terms:
                    term = Hc[t, A * 8 + u] * v
                    total = term if total is None else total + term
                parts.append(total)
            rows.append(fold(parts, 0))
        return fold(rows, 1)

    def halo_apply(v):
        return halo_matvec([(1, v), (0, pltpu.roll(v, 1, 1) * pat_halo[0]), (2, pltpu.roll(v, 127, 1) * pat_halo[1])])

    gather_wait(rv3, RV3, z, nz, v_recv.at[2], True)
    incoming = inflow(RV3, W3, nz) + nearer

    coarse = local + lanes_folded(diagonal(dotf(incoming, Pl[...], NT), 8))
    ce_ref[...] = coarse
    weights = jnp.where(own_block, dot2(coarse, GT), 0.0)
    total = None
    for m in range(4):
        w = row_sum(weights[:, m * 128 : m * 128 + 128]) * (1.0 / math.sqrt(64))
        term = tent[m] * jnp.concatenate([w] * 8, axis=0)
        total = term if total is None else total + term
    corr[...] = total
    next_first = dotf(incoming, P_next, NT) + local_next
    two = jnp.concatenate([incoming[0:1], next_first[0:1]] + [next_first[0:1]] * 6, axis=0)
    weights = jnp.where(which, dot2(two, GT_halo), 0.0)
    total = None
    for m in range(4):
        w = row_sum(weights[:, m * 128 : m * 128 + 128]) * (1.0 / math.sqrt(64))
        term = tent_halo[m] * w
        total = term if total is None else total + term
    c_halo = own_ends(corr, jnp.where(valid, total, 0.0))

    def post(ref, halo, emit):
        def left_of(k):
            return pltpu.roll(halo, 126 - 16 * k, 1)

        def right_of(k):
            return pltpu.roll(halo, 119 - 16 * k, 1)

        apply_with(ref[...], left_of, right_of, emit)

    def to_res(rows, y):
        res[rows, :] = y

    post(corr, c_halo, to_res)

    def prolong(rows, y):
        sol_ref[rows, :] = work[rows, :] + corr[rows, :] - SMOOTH * y

    block_apply(res[...], prolong)
    s_halo = s_halo + c_halo - SMOOTH * halo_matvec([(3, halo_apply(c_halo))])
    s_halo = jnp.where(valid, s_halo, 0.0)
    s_ends = own_ends(sol_ref, s_halo)

    def smooth(rows, y):
        sol_ref[rows, :] = sol_ref[rows, :] + DAMP * y

    post(sol_ref, s_ends, to_residue)
    block_apply(res[...], smooth)
    s_halo = s_halo + DAMP * halo_matvec([(3, b_halo - halo_apply(s_ends))])
    s_halo = jnp.where(valid, s_halo, 0.0)
    post(sol_ref, s_halo, to_residue)
    block_apply(res[...], smooth)


def body(nz, nx, ng, right_side, fine_blocks, fine_inverse, pattern, tentative, slot_map, coarse_inverse, coarse_lower):
    vmem = lambda *shape: pltpu.VMEM(shape, F32)
    dma = lambda *shape: pltpu.SemaphoreType.DMA(shape)
    top = max(nz, nx, ng)
    scratch = [
        vmem(3, 64, 64, 128), vmem(64, 64, 128), vmem(64, 128), pltpu.VMEM((2, 128), jnp.int32), vmem(4, 64, 128),
        pltpu.VMEM((8, 64), jnp.int32), vmem(64, 8, 64), vmem(64, 8, 64),
        vmem(64, 128), vmem(64, 128), vmem(64, 128),
        vmem(512, 64), vmem(512, 64), vmem(512, 64), vmem(ng * 64, 64), vmem(ng * 64, 64),
        vmem(nx * 64, 64), vmem(nx * 64, 64), vmem(nz * 64, 64),
        vmem(512, 64),
        pltpu.VMEM((ng * 64, 256), BF16), pltpu.VMEM((nx * 64, 256), BF16), pltpu.VMEM((nz * 64, 128), BF16),
        vmem(ng, 32, 128), vmem(nx, 32, 128), vmem(nz, 32, 128),
        vmem(ng, 8, 128), vmem(nx, 8, 128), vmem(nz, 8, 128),
        vmem(2, 2, 8, 128), vmem(2, 2, 8, 128),
        vmem(4, 64, 8, 128), vmem(2, 4, 8, 8, 128), vmem(2, 4, 8, 8, 128), vmem(2, 8, 8, 128), vmem(2, 8, 8, 128),
        pltpu.VMEM((2, 8, 64), jnp.int32), vmem(32, 128), vmem(8, 128), vmem(8, 128), vmem(32, 128),
        dma(10), dma(3, top), dma(3, top), dma(3, top), dma(3, top), dma(2, 2), dma(2, 2),
        dma(2, 6), dma(2, 6), dma(2), dma(2),
    ]
    result, coarse = pl.pallas_call(
        functools.partial(kernel, nz, nx, ng),
        out_shape=(
            jax.ShapeDtypeStruct((64, 128), F32),
            jax.ShapeDtypeStruct((8, 64), F32),
        ),
        in_specs=[pl.BlockSpec(memory_space=pl.ANY)] * 8,
        out_specs=(
            pl.BlockSpec(memory_space=pltpu.VMEM),
            pl.BlockSpec(memory_space=pltpu.VMEM),
        ),
        scratch_shapes=scratch,
        compiler_params=pltpu.CompilerParams(
            collective_id=0, has_side_effects=True, vmem_limit_bytes=60 * 2**20
        ),
        name="v_cycle",
    )(
        right_side, fine_blocks, fine_inverse, pattern, tentative, slot_map,
        jnp.transpose(coarse_inverse, (0, 2, 1)), jnp.transpose(coarse_lower, (0, 2, 1)),
    )
    return result, coarse.T


def solution(mesh):
    slabs, ng = mesh.shape["slab"], mesh.shape["group"]
    nx = 4 if slabs % 4 == 0 and slabs > 4 else 2
    both = ("slab", "group")
    in_specs = (
        P(None, both), P(None, None, None, both), P(None, None, both), P(None, both), P(None, None, both),
        P(both, None), P(None, None, both), P(None, None, both),
    )
    return jax.shard_map(
        functools.partial(body, slabs // nx, nx, ng),
        mesh=mesh,
        in_specs=in_specs,
        out_specs=(P(None, both), P(None, both)),
        check_vma=False,
    )
```

```python
import functools
import math

import jax
import jax.numpy as jnp
from jax import lax
from jax.experimental import pallas as pl
from jax.experimental.pallas import tpu as pltpu
from jax.sharding import PartitionSpec as P

DAMP = 0.8
SMOOTH = 0.67
F32 = jnp.float32
BF16 = jnp.bfloat16
MESH = pl.DeviceIdType.MESH

NN = (((1,), (0,)), ((), ()))
NT = (((1,), (1,)), ((), ()))


def split(x):
    hi = x.astype(BF16)
    return hi, (x - hi.astype(F32)).astype(BF16)


def dot1(a, b, dims=NN):
    return lax.dot_general(a, b, dims, preferred_element_type=F32)


def halves(t):
    n = t.shape[1] // 2
    return t[:, :n] + t[:, n:]


def dotf(a, b, dims=NN):
    return lax.dot_general(a, b, dims, precision=lax.Precision.HIGHEST, preferred_element_type=F32)


def dot2(a, b, dims=NN):
    t = dot1(jnp.concatenate(split(a), axis=0), b, dims)
    return t[: a.shape[0]] + t[a.shape[0] :]


def iota(shape, dim):
    return lax.broadcasted_iota(jnp.int32, shape, dim)


def fold(parts, axis):
    step = 1 if axis == 0 else 16
    at = iota((8, 128), axis) // step

    def mix(a, b, mask, shift):
        return jnp.where(mask, a, b) + pltpu.roll(jnp.where(mask, b, a), shift * step, axis)

    q = [parts[(i + 3) % 8] for i in range(8)]
    y = [mix(q[k], q[k + 4], ((at - k) & 7) < 4, 4) for k in range(4)]
    z = [mix(y[k], y[k + 2], ((at - k) & 3) >= 2, 2) for k in range(2)]
    return mix(z[0], z[1], (at & 1) == 1, 1)


def row_sum(x):
    x = x + pltpu.roll(x, 4, 0)
    x = x + pltpu.roll(x, 2, 0)
    return x + pltpu.roll(x, 1, 0)


def matvec(terms, width, emit):
    turns = 2 if len(terms) > 1 else 4

    def one(g, unused):
        for turn in range(turns):
            first = (g * turns + turn) * 8
            parts = []
            for a in range(8):
                total = None
                for load, v in terms:
                    product = load(first + a) * v
                    total = product if total is None else total + product
                parts.append(jnp.sum(total.reshape(width // 8, 8, 128), axis=0))
            emit(pl.ds(pl.multiple_of(first, 8), 8), fold(parts, 0))
        return unused

    lax.fori_loop(0, width // 8 // turns, one, 0)


def pack_matrix(m):
    return jnp.concatenate([m[:32, :], m[32:, :]], axis=1)


def unpack_matrix(p):
    return jnp.concatenate([p[:, :64], p[:, 64:]], axis=0)


def scan_products(refs, count):
    half = 1
    while half < count:
        for start in range(0, count, 2 * half):
            mid = start + half
            left = pl.ds(start * 64, half * 64)
            for ref in refs:
                ref[left, :] = dotf(ref[left, :], ref[pl.ds(mid * 64, 64), :])
        half *= 2


def scan_prefix(ref, count):
    half = 1
    while half < count:
        for start in range(0, count, 2 * half):
            mid = start + half
            right = pl.ds(mid * 64, half * 64)
            ref[right, :] = dotf(ref[right, :], ref[pl.ds((mid - 1) * 64, 64), :])
        half *= 2


def diagonal(x, count):
    return jnp.where(iota(x.shape, 0) == iota(x.shape, 1) // 64, x, 0.0)


def lanes_folded(x):
    t = x[:, 0:128] + x[:, 128:256] + x[:, 256:384] + x[:, 384:512]
    return t[:, :64] + t[:, 64:]


def padded(x):
    return jnp.concatenate([x, jnp.zeros_like(x)], axis=1)


def kernel(
    nz, nx, ng,
    b_h, f_h, i_h, pat_h, tent_h, slot_h, ci_h, cl_h,
    sol_ref, ce_ref,
    F, I, b, pat, tent, slot, ci, cl,
    work, res, corr,
    cis, Zl, Pl, Z1, Zm1, Z2, Zm2, Zm3,
    Xl, W1, W2, W3,
    RM1, RM2, RM3, RV1, RV2, RV3, halo_out, halo_in,
    Hc, msg, n_mat, vec, n_vec, n_slot, n_first, n_off, off_out, first_out,
    load_sem, m_send, m_recv, v_send, v_recv, h_send, h_recv, n_send, n_recv, f_send, f_recv,
):
    slab, g = lax.axis_index("slab"), lax.axis_index("group")
    z, x = slab // nx, slab % nx
    ns = nz * nx

    RM3[...] = jnp.zeros_like(RM3)
    RV3[...] = jnp.zeros_like(RV3)

    def in_group(o):
        return (slab, lax.rem(g + o, ng))

    def along_x(o):
        return (z * nx + lax.rem(x + o, nx), g)

    def along_z(o):
        return (lax.rem(z + o, nz) * nx + x, g)

    at_end, at_start = g == ng - 1, g == 0
    right = (jnp.where(at_end, lax.rem(slab + 1, ns), slab), lax.rem(g + 1, ng))
    left = (jnp.where(at_start, lax.rem(slab + ns - 1, ns), slab), lax.rem(g + ng - 1, ng))

    barrier = pltpu.get_barrier_semaphore()
    for o in range(1, nz):

        @pl.when(z + o >= nz)
        def _(o=o):
            pl.semaphore_signal(barrier, inc=1, device_id=along_z(o), device_id_type=MESH)

    peers = [along_x(o) for o in range(1, nx)] + [right, left] + [in_group(o) for o in range(1, ng)]
    for peer in peers:
        pl.semaphore_signal(barrier, inc=1, device_id=peer, device_id_type=MESH)

    copies = []
    for k, (src, dst) in enumerate(
        [(ci_h, ci), (cl_h, cl), (i_h, I), (b_h, b), (slot_h, slot), (pat_h, pat),
         (f_h.at[1], F.at[1]), (f_h.at[0], F.at[0]), (f_h.at[2], F.at[2]), (tent_h, tent)]
    ):
        copy = pltpu.make_async_copy(src, dst, load_sem.at[k])
        copy.start()
        copies.append(copy)
    ci_c, cl_c, i_c, b_c, slot_c, pat_c, f1_c, f0_c, f2_c, tent_c = copies

    row64, lane64 = iota((64, 64), 0), iota((64, 64), 1)
    eye = (row64 == lane64).astype(F32)
    ci_c.wait()
    cl_c.wait()
    for j in range(8):
        cij = ci[:, j, :]
        cis[pl.ds(j * 64, 64), :] = cij
        m = -dotf(cij, cl[:, j, :])
        Pl[pl.ds(j * 64, 64), :] = m
        e = m.T
        Zl[pl.ds(j * 64, 64), :] = e
        Xl[pl.ds(j * 64, 64), :] = e
    scan_products([Zl], 8)

    sends = []

    def perhaps(condition, act):
        if condition is None:
            act()
        else:
            pl.when(condition)(act)

    def gather_start(ref, own, target, count, send, recv, forward=False):
        started = []
        for o in range(1, count):
            copy = pltpu.make_async_remote_copy(
                src_ref=ref.at[own],
                dst_ref=ref.at[own],
                send_sem=send.at[o],
                recv_sem=recv.at[own],
                device_id=target(o),
                device_id_type=MESH,
            )
            condition = own + o < count if forward else None
            perhaps(condition, copy.start)
            started.append((condition, copy))
        return started

    def gather_wait(started, ref, own, count, recv, forward=False):
        for o in range(1, count):
            other = lax.rem(own + o, count)
            arrival = pltpu.make_async_copy(ref.at[other], ref.at[other], recv.at[other])
            perhaps(own + o >= count if forward else None, arrival.wait)
        sends.extend(started)

    lane8, lane = iota((8, 128), 1), iota((64, 128), 1)
    has_left = jnp.logical_not(jnp.logical_and(slab == 0, at_start))
    has_right = jnp.logical_not(jnp.logical_and(slab == ns - 1, at_end))

    def halo_pack(turn, ref):
        to_right, to_left = jnp.zeros((8, 128), F32), jnp.zeros((8, 128), F32)
        for k in range(8):
            piece = ref[pl.ds(8 * k, 8), :]
            to_right = jnp.where(lane8 == k, pltpu.roll(piece, k + 1, 1), to_right)
            to_left = jnp.where(lane8 == k, pltpu.roll(piece, k, 1) if k else piece, to_left)
        halo_out[turn, 0] = to_right
        halo_out[turn, 1] = to_left

    def halo_send(turn):
        started = []
        for side, peer in ((0, right), (1, left)):
            copy = pltpu.make_async_remote_copy(
                src_ref=halo_out.at[turn, side],
                dst_ref=halo_in.at[turn, side],
                send_sem=h_send.at[turn, side],
                recv_sem=h_recv.at[turn, side],
                device_id=peer,
                device_id_type=MESH,
            )
            copy.start()
            started.append(copy)
        return started

    def apply_with(value, left_of, right_of, emit):
        before, after = [], []
        for k in range(8):
            piece = value[8 * k : 8 * k + 8]
            before.append(jnp.where(lane8 == 0, left_of(k), pltpu.roll(piece, 1, 1)))
            after.append(jnp.where(lane8 == 127, right_of(k), pltpu.roll(piece, 127, 1)))
        previous = jnp.concatenate(before, axis=0) * pat[0:1, :].astype(F32)
        following = jnp.concatenate(after, axis=0) * pat[1:2, :].astype(F32)
        matvec(
            [
                (lambda a: F[1, a], value),
                (lambda a: F[0, a], previous),
                (lambda a: F[2, a], following),
            ],
            64,
            emit,
        )

    def fine_apply(turn, ref, started, emit):
        for copy in started:
            copy.wait_recv()
            sends.append((None, copy))
        from_left = jnp.where(has_left, halo_in[turn, 0], 0.0)
        from_right = jnp.where(has_right, halo_in[turn, 1], 0.0)

        def left_of(k):
            return pltpu.roll(from_left, 128 - k, 1) if k else from_left

        def right_of(k):
            return pltpu.roll(from_right, 127 - k, 1)

        apply_with(ref[...], left_of, right_of, emit)

    def block_apply(value, emit):
        matvec([(lambda a: I[a], value)], 64, emit)

    def to_residue(rows, y):
        res[rows, :] = b[rows, :] - y

    def sweep(turn, ref, started):
        fine_apply(turn, ref, started, to_residue)

        def emit(rows, y):
            ref[rows, :] = ref[rows, :] + DAMP * y

        block_apply(res[...], emit)

    def first(rows, y):
        work[rows, :] = DAMP * y

    i_c.wait()
    b_c.wait()
    block_apply(b[...], first)
    halo_pack(0, work)

    slot_c.wait()
    q, col = iota((64, 512), 0), iota((64, 512), 1)
    pick = (q == (col % 16) * 4 + col // 128).astype(BF16)
    own_block = iota((8, 512), 0) == (iota((8, 512), 1) % 128) // 16
    slots = dot1(slot[...].astype(F32).astype(BF16), pick)
    slots = row_sum(jnp.where(own_block, slots, 0.0))
    slots = jnp.concatenate([slots] * 8, axis=0)
    GT = (slots == q.astype(F32)).astype(BF16)

    group, spot = lane8 // 16, lane8 % 16
    at_left, at_right = spot < 3, jnp.logical_and(spot >= 8, spot < 11)

    def gather_lanes(pieces, shift, mask, out):
        for k in range(8):
            moved = pltpu.roll(pieces(k), shift + 16 * k, 1)
            out = jnp.where(jnp.logical_and(group == k, mask), moved, out)
        return out

    nothing = jnp.zeros((8, 128), F32)

    def pack_ends(place, pieces):
        vec[0, place] = gather_lanes(pieces, 3, at_left, nothing)
        vec[1, place] = gather_lanes(pieces, 8, at_right, nothing)

    beside = []

    def tell(src, dst, k, peer, send, recv):
        copy = pltpu.make_async_remote_copy(
            src_ref=src, dst_ref=dst, send_sem=send.at[k], recv_sem=recv.at[k], device_id=peer, device_id_type=MESH
        )
        copy.start()
        beside.append(copy)

    def tell_both(src, dst, k, part):
        for side, peer in ((0, right), (1, left)):
            here = src if part is None else src.at[side, part]
            there = dst.at[side] if part is None else dst.at[side, part]
            tell(here, there, k, peer, n_send.at[side], n_recv.at[side])

    first_out[...] = pack_matrix(Pl[0:64, :])
    pack_ends(0, lambda k: b[pl.ds(8 * k, 8), :])
    pat_c.wait()
    tent_c.wait()
    for m in range(4):
        pack_ends(2 + m, lambda k, m=m: tent[m, pl.ds(8 * k, 8), :])
    for r in range(2):
        row = jnp.broadcast_to(pat[r : r + 1, :].astype(F32), (8, 128))
        pack_ends(6 + r, lambda k: row)

    pl.semaphore_wait(barrier, len(peers) + nz - 1 - z)

    h0 = halo_send(0)
    RM1[g] = pack_matrix(Zl[0:64, :])
    rm1 = gather_start(RM1, g, in_group, ng, m_send.at[0], m_recv.at[0])

    def gathered(t, load):
        def one(A, unused):
            to_right, to_left = jnp.zeros((8, 128), F32), jnp.zeros((8, 128), F32)
            for u in range(8):
                whole = load(A * 8 + u)
                edge = jnp.zeros((8, 128), F32)
                for k in range(8):
                    piece = pltpu.roll(whole[8 * k : 8 * k + 8], (2 + 16 * k) % 128, 1)
                    edge = jnp.where(lane8 // 16 == k, piece, edge)
                here = (lane8 % 16) // 2 == u
                to_right = jnp.where(here, pltpu.roll(edge, 2 * u, 1) if u else edge, to_right)
                shift = (2 * u - 2) % 128
                to_left = jnp.where(here, pltpu.roll(edge, shift, 1) if shift else edge, to_left)
            msg[0, t, A] = to_right
            msg[1, t, A] = to_left
            return unused

        lax.fori_loop(0, 8, one, 0)

    tell(first_out, n_first, 1, left, f_send, f_recv)
    tell_both(slot, n_slot, 4, None)
    f1_c.wait()
    gathered(1, lambda a: F[1, a])
    tell_both(msg, n_mat, 1, 1)
    f0_c.wait()
    gathered(0, lambda a: F[0, a])
    tell_both(msg, n_mat, 0, 0)
    f2_c.wait()
    sweep(0, work, h0)
    halo_pack(1, work)
    h1 = halo_send(1)

    def upward(started, ref, own, count, recv, full, masked):
        gather_wait(started, ref, own, count, recv, full is None)
        for k in range(count):
            e = unpack_matrix(ref[k])
            rows = pl.ds(k * 64, 64)
            if full is not None:
                full[rows, :] = e
            masked[rows, :] = jnp.where(k < own, e, eye)
        scan_products([masked] if full is None else [full, masked], count)

    def later(ref, h, count):
        return ref[pl.ds((h + 1) * 64, 64), :] if h + 1 < count else eye

    upward(rm1, RM1, g, ng, m_recv.at[0], Z1, Zm1)
    RM2[x] = pack_matrix(Z1[0:64, :])
    rm2 = gather_start(RM2, x, along_x, nx, m_send.at[1], m_recv.at[1])
    def weigh(ref, h, parts):
        ref[pl.ds(h * 64, 64), :] = jnp.concatenate(split(jnp.concatenate(parts, axis=1)), axis=1)

    for h in range(ng):
        weigh(W1, h, [later(Z1, h, ng), jnp.where(h < g, later(Zm1, h, ng), 0.0)])

    pack_ends(1, lambda k: work[pl.ds(8 * k, 8), :])
    for side, peer in ((0, right), (1, left)):
        tell(vec.at[side], n_vec.at[side], 5, peer, n_send.at[side], n_recv.at[side])
    gathered(2, lambda a: F[2, a])
    tell_both(msg, n_mat, 2, 2)

    fine_apply(1, work, h1, to_residue)
    residue = res[...]
    values = []
    for m in range(4):
        weight = jnp.sum((tent[m] * residue).reshape(8, 8, 128), axis=0)
        values.append(row_sum(weight) * (1.0 / math.sqrt(64)))
    spread = jnp.where(own_block, jnp.concatenate(values, axis=1), 0.0)
    rhs = dot2(spread, GT, NT)
    offsets = diagonal(dotf(rhs, cis[...], NT), 8)
    after_own = jnp.concatenate([Zl[64:512, :], eye], axis=0)
    RV1[g] = padded(row_sum(dotf(offsets, after_own)))
    rv1 = gather_start(RV1, g, in_group, ng, v_send.at[0], v_recv.at[0])

    upward(rm2, RM2, x, nx, m_recv.at[1], Z2, Zm2)
    RM3[z] = pack_matrix(Z2[0:64, :])
    rm3 = gather_start(RM3, z, along_z, nz, m_send.at[2], m_recv.at[2], True)
    for h in range(nx):
        weigh(W2, h, [later(Z2, h, nx), jnp.where(h < x, later(Zm2, h, nx), 0.0)])

    own = lanes_folded(offsets)
    off_out[...] = padded(own)
    tell(off_out, n_off, 0, left, f_send, f_recv)
    gathered(3, lambda a: I[a])
    tell_both(msg, n_mat, 3, 3)

    def inflow(ref, weights, count):
        flat = [ref[h] + pltpu.roll(ref[h + 1], 64, 1) for h in range(0, count, 2)]
        return halves(dot2(jnp.concatenate(flat, axis=1), weights[...]))


    gather_wait(rv1, RV1, g, ng, v_recv.at[0])
    flow1 = inflow(RV1, W1, ng)
    RV2[x] = padded(flow1[:, :64])
    rv2 = gather_start(RV2, x, along_x, nx, v_send.at[1], v_recv.at[1])

    scan_prefix(Pl, 8)

    row8 = iota((8, 64), 0)
    carried = jnp.broadcast_to(own[0:1], (8, 64))
    local = carried
    for j in range(1, 8):
        carried = dotf(carried, Xl[pl.ds(j * 64, 64), :]) + own[j : j + 1]
        local = jnp.where(row8 >= j, carried, local)


    gather_wait(rv2, RV2, x, nx, v_recv.at[1])
    flow2 = inflow(RV2, W2, nx)
    RV3[z] = padded(flow2[:, :64])
    rv3 = gather_start(RV3, z, along_z, nz, v_send.at[2], v_recv.at[2], True)

    upward(rm3, RM3, z, nz, m_recv.at[2], None, Zm3)
    A1 = Zm1[0:64, :]
    A21 = dotf(Zm2[0:64, :], A1)
    for h in range(nz):
        weigh(W3, h, [dotf(jnp.where(h < z, later(Zm3, h, nz), 0.0), A21)])

    nearer = dotf(flow2[:, 64:], A1) + flow1[:, 64:]
    for copy in beside:
        copy.wait_recv()
        sends.append((None, copy))
    valid = jnp.logical_or(jnp.logical_and(at_left, has_left), jnp.logical_and(at_right, has_right))

    def own_ends(ref, out):
        out = gather_lanes(lambda k: ref[pl.ds(8 * k, 8), :], 3, spot == 3, out)
        return gather_lanes(lambda k: ref[pl.ds(8 * k, 8), :], 8, spot == 7, out)

    b_halo, s_halo, *tent_halo = [n_vec[0, k] + n_vec[1, k] for k in range(6)]
    pat_halo = [n_vec[0, k] + n_vec[1, k] for k in (6, 7)]

    def placed(A, unused):
        for t in range(4):
            from_left, from_right = n_mat[0, t, A], n_mat[1, t, A]
            at_two_left = jnp.logical_or(spot == 1, spot == 2)
            at_two_right = jnp.logical_or(spot == 8, spot == 9)
            for u in range(8):
                p = jnp.where(at_two_left, pltpu.roll(from_left, (1 - 2 * u) % 128, 1), 0.0)
                shift = (8 - 2 * u) % 128
                q = pltpu.roll(from_right, shift, 1) if shift else from_right
                Hc[t, A * 8 + u] = jnp.where(at_two_right, q, p)
        return unused

    lax.fori_loop(0, 8, placed, 0)

    place = iota((64, 512), 1) % 16
    asked = jnp.where(place < 3, place + 13, place - 8) * 4 + col // 128
    pick_halo = (q == asked).astype(BF16)
    ends = jnp.concatenate([n_slot[0, 7:8, :], n_slot[1, 0:1, :]] + [n_slot[1, 0:1, :]] * 6, axis=0)
    slots = dot1(ends.astype(F32).astype(BF16), pick_halo)
    which = (iota((8, 512), 1) % 16 >= 8).astype(jnp.int32) == iota((8, 512), 0)
    slots = row_sum(jnp.where(which, slots, 0.0))
    GT_halo = (jnp.concatenate([slots] * 8, axis=0) == q.astype(F32)).astype(BF16)
    M_next = unpack_matrix(n_first[...])
    P_next = dotf(M_next, Pl[448:512, :])
    local_next = dotf(carried, M_next, NT) + n_off[0:1, :64]

    def halo_matvec(terms):
        rows = []
        for A in range(8):
            parts = []
            for u in range(8):
                total = None
                for t, v in terms:
                    term = Hc[t, A * 8 + u] * v
                    total = term if total is None else total + term
                parts.append(total)
            rows.append(fold(parts, 0))
        return fold(rows, 1)

    def halo_apply(v):
        return halo_matvec([(1, v), (0, pltpu.roll(v, 1, 1) * pat_halo[0]), (2, pltpu.roll(v, 127, 1) * pat_halo[1])])

    gather_wait(rv3, RV3, z, nz, v_recv.at[2], True)
    incoming = inflow(RV3, W3, nz) + nearer

    coarse = local + lanes_folded(diagonal(dotf(incoming, Pl[...], NT), 8))
    ce_ref[...] = coarse
    weights = jnp.where(own_block, dot2(coarse, GT), 0.0)
    total = None
    for m in range(4):
        w = row_sum(weights[:, m * 128 : m * 128 + 128]) * (1.0 / math.sqrt(64))
        term = tent[m] * jnp.concatenate([w] * 8, axis=0)
        total = term if total is None else total + term
    corr[...] = total
    next_first = dotf(incoming, P_next, NT) + local_next
    two = jnp.concatenate([incoming[0:1], next_first[0:1]] + [next_first[0:1]] * 6, axis=0)
    weights = jnp.where(which, dot2(two, GT_halo), 0.0)
    total = None
    for m in range(4):
        w = row_sum(weights[:, m * 128 : m * 128 + 128]) * (1.0 / math.sqrt(64))
        term = tent_halo[m] * w
        total = term if total is None else total + term
    c_halo = own_ends(corr, jnp.where(valid, total, 0.0))

    def post(ref, halo, emit):
        def left_of(k):
            return pltpu.roll(halo, 126 - 16 * k, 1)

        def right_of(k):
            return pltpu.roll(halo, 119 - 16 * k, 1)

        apply_with(ref[...], left_of, right_of, emit)

    def to_res(rows, y):
        res[rows, :] = y

    post(corr, c_halo, to_res)

    def prolong(rows, y):
        sol_ref[rows, :] = work[rows, :] + corr[rows, :] - SMOOTH * y

    block_apply(res[...], prolong)
    s_halo = s_halo + c_halo - SMOOTH * halo_matvec([(3, halo_apply(c_halo))])
    s_halo = jnp.where(valid, s_halo, 0.0)
    s_ends = own_ends(sol_ref, s_halo)

    def smooth(rows, y):
        sol_ref[rows, :] = sol_ref[rows, :] + DAMP * y

    post(sol_ref, s_ends, to_residue)
    block_apply(res[...], smooth)
    s_halo = s_halo + DAMP * halo_matvec([(3, b_halo - halo_apply(s_ends))])
    s_halo = jnp.where(valid, s_halo, 0.0)
    post(sol_ref, s_halo, to_residue)
    block_apply(res[...], smooth)
    for condition, copy in sends:
        perhaps(condition, copy.wait_send)


def body(nz, nx, ng, right_side, fine_blocks, fine_inverse, pattern, tentative, slot_map, coarse_inverse, coarse_lower):
    vmem = lambda *shape: pltpu.VMEM(shape, F32)
    dma = lambda *shape: pltpu.SemaphoreType.DMA(shape)
    top = max(nz, nx, ng)
    scratch = [
        vmem(3, 64, 64, 128), vmem(64, 64, 128), vmem(64, 128), pltpu.VMEM((2, 128), jnp.int32), vmem(4, 64, 128),
        pltpu.VMEM((8, 64), jnp.int32), vmem(64, 8, 64), vmem(64, 8, 64),
        vmem(64, 128), vmem(64, 128), vmem(64, 128),
        vmem(512, 64), vmem(512, 64), vmem(512, 64), vmem(ng * 64, 64), vmem(ng * 64, 64),
        vmem(nx * 64, 64), vmem(nx * 64, 64), vmem(nz * 64, 64),
        vmem(512, 64),
        pltpu.VMEM((ng * 64, 256), BF16), pltpu.VMEM((nx * 64, 256), BF16), pltpu.VMEM((nz * 64, 128), BF16),
        vmem(ng, 32, 128), vmem(nx, 32, 128), vmem(nz, 32, 128),
        vmem(ng, 8, 128), vmem(nx, 8, 128), vmem(nz, 8, 128),
        vmem(2, 2, 8, 128), vmem(2, 2, 8, 128),
        vmem(4, 64, 8, 128), vmem(2, 4, 8, 8, 128), vmem(2, 4, 8, 8, 128), vmem(2, 8, 8, 128), vmem(2, 8, 8, 128),
        pltpu.VMEM((2, 8, 64), jnp.int32), vmem(32, 128), vmem(8, 128), vmem(8, 128), vmem(32, 128),
        dma(10), dma(3, top), dma(3, top), dma(3, top), dma(3, top), dma(2, 2), dma(2, 2),
        dma(2, 6), dma(2, 6), dma(2), dma(2),
    ]
    result, coarse = pl.pallas_call(
        functools.partial(kernel, nz, nx, ng),
        out_shape=(
            jax.ShapeDtypeStruct((64, 128), F32),
            jax.ShapeDtypeStruct((8, 64), F32),
        ),
        in_specs=[pl.BlockSpec(memory_space=pl.ANY)] * 8,
        out_specs=(
            pl.BlockSpec(memory_space=pltpu.VMEM),
            pl.BlockSpec(memory_space=pltpu.VMEM),
        ),
        scratch_shapes=scratch,
        compiler_params=pltpu.CompilerParams(
            collective_id=0, has_side_effects=True, vmem_limit_bytes=60 * 2**20
        ),
        name="v_cycle",
    )(
        right_side, fine_blocks, fine_inverse, pattern, tentative, slot_map,
        jnp.transpose(coarse_inverse, (0, 2, 1)), jnp.transpose(coarse_lower, (0, 2, 1)),
    )
    return result, coarse.T


def solution(mesh):
    slabs, ng = mesh.shape["slab"], mesh.shape["group"]
    nx = 4 if slabs % 4 == 0 and slabs > 4 else 2
    both = ("slab", "group")
    in_specs = (
        P(None, both), P(None, None, None, both), P(None, None, both), P(None, both), P(None, None, both),
        P(both, None), P(None, None, both), P(None, None, both),
    )
    return jax.shard_map(
        functools.partial(body, slabs // nx, nx, ng),
        mesh=mesh,
        in_specs=in_specs,
        out_specs=(P(None, both), P(None, both)),
        check_vma=False,
    )
```

```python
import functools
import math

import jax
import jax.numpy as jnp
from jax import lax
from jax.experimental import pallas as pl
from jax.experimental.pallas import tpu as pltpu
from jax.sharding import PartitionSpec as P

DAMP = 0.8
SMOOTH = 0.67
F32 = jnp.float32
BF16 = jnp.bfloat16
MESH = pl.DeviceIdType.MESH

NN = (((1,), (0,)), ((), ()))
NT = (((1,), (1,)), ((), ()))


def split(x):
    hi = x.astype(BF16)
    return hi, (x - hi.astype(F32)).astype(BF16)


def dot1(a, b, dims=NN):
    return lax.dot_general(a, b, dims, preferred_element_type=F32)


def halves(t):
    n = t.shape[1] // 2
    return t[:, :n] + t[:, n:]


def dotf(a, b, dims=NN):
    return lax.dot_general(a, b, dims, precision=lax.Precision.HIGHEST, preferred_element_type=F32)


def dot2(a, b, dims=NN):
    t = dot1(jnp.concatenate(split(a), axis=0), b, dims)
    return t[: a.shape[0]] + t[a.shape[0] :]


def iota(shape, dim):
    return lax.broadcasted_iota(jnp.int32, shape, dim)


def fold(parts, axis):
    step = 1 if axis == 0 else 16
    at = iota((8, 128), axis) // step

    def mix(a, b, mask, shift):
        return jnp.where(mask, a, b) + pltpu.roll(jnp.where(mask, b, a), shift * step, axis)

    q = [parts[(i + 3) % 8] for i in range(8)]
    y = [mix(q[k], q[k + 4], ((at - k) & 7) < 4, 4) for k in range(4)]
    z = [mix(y[k], y[k + 2], ((at - k) & 3) >= 2, 2) for k in range(2)]
    return mix(z[0], z[1], (at & 1) == 1, 1)


def row_sum(x):
    x = x + pltpu.roll(x, 4, 0)
    x = x + pltpu.roll(x, 2, 0)
    return x + pltpu.roll(x, 1, 0)


def matvec(terms, width, emit):
    turns = 2 if len(terms) > 1 else 4

    def one(g, unused):
        for turn in range(turns):
            first = (g * turns + turn) * 8
            parts = []
            for a in range(8):
                total = None
                for load, v in terms:
                    product = load(first + a) * v
                    total = product if total is None else total + product
                parts.append(jnp.sum(total.reshape(width // 8, 8, 128), axis=0))
            emit(pl.ds(pl.multiple_of(first, 8), 8), fold(parts, 0))
        return unused

    lax.fori_loop(0, width // 8 // turns, one, 0)


def pack_matrix(m):
    return jnp.concatenate([m[:32, :], m[32:, :]], axis=1)


def unpack_matrix(p):
    return jnp.concatenate([p[:, :64], p[:, 64:]], axis=0)


def scan_products(refs, count):
    half = 1
    while half < count:
        for start in range(0, count, 2 * half):
            mid = start + half
            left = pl.ds(start * 64, half * 64)
            for ref in refs:
                ref[left, :] = dotf(ref[left, :], ref[pl.ds(mid * 64, 64), :])
        half *= 2


def scan_prefix(ref, count):
    half = 1
    while half < count:
        for start in range(0, count, 2 * half):
            mid = start + half
            right = pl.ds(mid * 64, half * 64)
            ref[right, :] = dotf(ref[right, :], ref[pl.ds((mid - 1) * 64, 64), :])
        half *= 2


def diagonal(x, count):
    return jnp.where(iota(x.shape, 0) == iota(x.shape, 1) // 64, x, 0.0)


def lanes_folded(x):
    t = x[:, 0:128] + x[:, 128:256] + x[:, 256:384] + x[:, 384:512]
    return t[:, :64] + t[:, 64:]


def padded(x):
    return jnp.concatenate([x, jnp.zeros_like(x)], axis=1)


def kernel(
    nz, nx, ng,
    b_h, f_h, i_h, pat_h, tent_h, slot_h, ci_h, cl_h,
    sol_ref, ce_ref,
    F, I, b, pat, tent, slot, ci, cl,
    work, res, corr,
    cis, Zl, Pl, Z1, Zm1, Z2, Zm2, Zm3,
    Xl, W1, W2, W3,
    RM1, RM2, RM3, RV1, RV2, RV3, halo_out, halo_in,
    Hc, msg, n_mat, vec, n_vec, n_slot, n_first, n_off, off_out, first_out,
    load_sem, m_send, m_recv, v_send, v_recv, h_send, h_recv, n_send, n_recv, f_send, f_recv,
):
    slab, g = lax.axis_index("slab"), lax.axis_index("group")
    z, x = slab // nx, slab % nx
    ns = nz * nx

    RM3[...] = jnp.zeros_like(RM3)
    RV3[...] = jnp.zeros_like(RV3)
    W3[...] = jnp.zeros_like(W3)

    def in_group(o):
        return (slab, lax.rem(g + o, ng))

    def along_x(o):
        return (z * nx + lax.rem(x + o, nx), g)

    def along_z(o):
        return (lax.rem(z + o, nz) * nx + x, g)

    at_end, at_start = g == ng - 1, g == 0
    right = (jnp.where(at_end, lax.rem(slab + 1, ns), slab), lax.rem(g + 1, ng))
    left = (jnp.where(at_start, lax.rem(slab + ns - 1, ns), slab), lax.rem(g + ng - 1, ng))

    barrier = pltpu.get_barrier_semaphore()
    for o in range(1, nz):

        @pl.when(z + o >= nz)
        def _(o=o):
            pl.semaphore_signal(barrier, inc=1, device_id=along_z(o), device_id_type=MESH)

    peers = [along_x(o) for o in range(1, nx)] + [right, left] + [in_group(o) for o in range(1, ng)]
    for peer in peers:
        pl.semaphore_signal(barrier, inc=1, device_id=peer, device_id_type=MESH)

    copies = []
    for k, (src, dst) in enumerate(
        [(ci_h, ci), (cl_h, cl), (i_h, I), (b_h, b), (slot_h, slot), (pat_h, pat),
         (f_h.at[1], F.at[1]), (f_h.at[0], F.at[0]), (f_h.at[2], F.at[2]), (tent_h, tent)]
    ):
        copy = pltpu.make_async_copy(src, dst, load_sem.at[k])
        copy.start()
        copies.append(copy)
    ci_c, cl_c, i_c, b_c, slot_c, pat_c, f1_c, f0_c, f2_c, tent_c = copies

    row64, lane64 = iota((64, 64), 0), iota((64, 64), 1)
    eye = (row64 == lane64).astype(F32)
    ci_c.wait()
    cl_c.wait()
    for j in range(8):
        cij = ci[:, j, :]
        cis[pl.ds(j * 64, 64), :] = cij
        m = -dotf(cij, cl[:, j, :])
        Pl[pl.ds(j * 64, 64), :] = m
        e = m.T
        Zl[pl.ds(j * 64, 64), :] = e
        Xl[pl.ds(j * 64, 64), :] = e
    scan_products([Zl], 8)

    def perhaps(condition, act):
        if condition is None:
            act()
        else:
            pl.when(condition)(act)

    def gather_start(ref, own, target, count, send, recv, forward=False):
        started = []
        for o in range(1, count):
            copy = pltpu.make_async_remote_copy(
                src_ref=ref.at[own],
                dst_ref=ref.at[own],
                send_sem=send.at[o],
                recv_sem=recv.at[own],
                device_id=target(o),
                device_id_type=MESH,
            )
            condition = own + o < count if forward else None
            perhaps(condition, copy.start)
            started.append((condition, copy))
        return started

    def gather_wait(started, ref, own, count, recv, forward=False):
        for o in range(1, count):
            other = lax.rem(own + o, count)
            arrival = pltpu.make_async_copy(ref.at[other], ref.at[other], recv.at[other])
            perhaps(own + o >= count if forward else None, arrival.wait)
        for condition, copy in started:
            perhaps(condition, copy.wait_send)

    lane8, lane = iota((8, 128), 1), iota((64, 128), 1)
    has_left = jnp.logical_not(jnp.logical_and(slab == 0, at_start))
    has_right = jnp.logical_not(jnp.logical_and(slab == ns - 1, at_end))

    def halo_pack(turn, ref):
        to_right, to_left = jnp.zeros((8, 128), F32), jnp.zeros((8, 128), F32)
        for k in range(8):
            piece = ref[pl.ds(8 * k, 8), :]
            to_right = jnp.where(lane8 == k, pltpu.roll(piece, k + 1, 1), to_right)
            to_left = jnp.where(lane8 == k, pltpu.roll(piece, k, 1) if k else piece, to_left)
        halo_out[turn, 0] = to_right
        halo_out[turn, 1] = to_left

    def halo_send(turn):
        started = []
        for side, peer in ((0, right), (1, left)):
            copy = pltpu.make_async_remote_copy(
                src_ref=halo_out.at[turn, side],
                dst_ref=halo_in.at[turn, side],
                send_sem=h_send.at[turn, side],
                recv_sem=h_recv.at[turn, side],
                device_id=peer,
                device_id_type=MESH,
            )
            copy.start()
            started.append(copy)
        return started

    def apply_with(value, left_of, right_of, emit):
        before, after = [], []
        for k in range(8):
            piece = value[8 * k : 8 * k + 8]
            before.append(jnp.where(lane8 == 0, left_of(k), pltpu.roll(piece, 1, 1)))
            after.append(jnp.where(lane8 == 127, right_of(k), pltpu.roll(piece, 127, 1)))
        previous = jnp.concatenate(before, axis=0) * pat[0:1, :].astype(F32)
        following = jnp.concatenate(after, axis=0) * pat[1:2, :].astype(F32)
        matvec(
            [
                (lambda a: F[1, a], value),
                (lambda a: F[0, a], previous),
                (lambda a: F[2, a], following),
            ],
            64,
            emit,
        )

    def fine_apply(turn, ref, started, emit):
        for copy in started:
            copy.wait()
        from_left = jnp.where(has_left, halo_in[turn, 0], 0.0)
        from_right = jnp.where(has_right, halo_in[turn, 1], 0.0)

        def left_of(k):
            return pltpu.roll(from_left, 128 - k, 1) if k else from_left

        def right_of(k):
            return pltpu.roll(from_right, 127 - k, 1)

        apply_with(ref[...], left_of, right_of, emit)

    def block_apply(value, emit):
        matvec([(lambda a: I[a], value)], 64, emit)

    def to_residue(rows, y):
        res[rows, :] = b[rows, :] - y

    def sweep(turn, ref, started):
        fine_apply(turn, ref, started, to_residue)

        def emit(rows, y):
            ref[rows, :] = ref[rows, :] + DAMP * y

        block_apply(res[...], emit)

    def first(rows, y):
        work[rows, :] = DAMP * y

    i_c.wait()
    b_c.wait()
    block_apply(b[...], first)
    halo_pack(0, work)

    slot_c.wait()
    q, col = iota((64, 512), 0), iota((64, 512), 1)
    pick = (q == (col % 16) * 4 + col // 128).astype(BF16)
    own_block = iota((8, 512), 0) == (iota((8, 512), 1) % 128) // 16
    slots = dot1(slot[...].astype(F32).astype(BF16), pick)
    slots = row_sum(jnp.where(own_block, slots, 0.0))
    slots = jnp.concatenate([slots] * 8, axis=0)
    GT = (slots == q.astype(F32)).astype(BF16)

    group, spot = lane8 // 16, lane8 % 16
    at_left, at_right = spot < 3, jnp.logical_and(spot >= 8, spot < 11)

    def gather_lanes(pieces, shift, mask, out):
        for k in range(8):
            moved = pltpu.roll(pieces(k), shift + 16 * k, 1)
            out = jnp.where(jnp.logical_and(group == k, mask), moved, out)
        return out

    nothing = jnp.zeros((8, 128), F32)

    def pack_ends(place, pieces):
        vec[0, place] = gather_lanes(pieces, 3, at_left, nothing)
        vec[1, place] = gather_lanes(pieces, 8, at_right, nothing)

    beside = []

    def tell(src, dst, k, peer, send, recv):
        copy = pltpu.make_async_remote_copy(
            src_ref=src, dst_ref=dst, send_sem=send.at[k], recv_sem=recv.at[k], device_id=peer, device_id_type=MESH
        )
        copy.start()
        beside.append(copy)

    def tell_both(src, dst, k, part):
        for side, peer in ((0, right), (1, left)):
            here = src if part is None else src.at[side, part]
            there = dst.at[side] if part is None else dst.at[side, part]
            tell(here, there, k, peer, n_send.at[side], n_recv.at[side])

    first_out[...] = pack_matrix(Pl[0:64, :])
    pack_ends(0, lambda k: b[pl.ds(8 * k, 8), :])
    pat_c.wait()
    tent_c.wait()
    for m in range(4):
        pack_ends(2 + m, lambda k, m=m: tent[m, pl.ds(8 * k, 8), :])
    for r in range(2):
        row = jnp.broadcast_to(pat[r : r + 1, :].astype(F32), (8, 128))
        pack_ends(6 + r, lambda k: row)

    pl.semaphore_wait(barrier, len(peers) + nz - 1 - z)

    h0 = halo_send(0)
    RM1[g] = pack_matrix(Zl[0:64, :])
    rm1 = gather_start(RM1, g, in_group, ng, m_send.at[0], m_recv.at[0])

    def gathered(t, load):
        def one(A, unused):
            to_right, to_left = jnp.zeros((8, 128), F32), jnp.zeros((8, 128), F32)
            for u in range(8):
                whole = load(A * 8 + u)
                edge = jnp.zeros((8, 128), F32)
                for k in range(8):
                    piece = pltpu.roll(whole[8 * k : 8 * k + 8], (2 + 16 * k) % 128, 1)
                    edge = jnp.where(lane8 // 16 == k, piece, edge)
                here = (lane8 % 16) // 2 == u
                to_right = jnp.where(here, pltpu.roll(edge, 2 * u, 1) if u else edge, to_right)
                shift = (2 * u - 2) % 128
                to_left = jnp.where(here, pltpu.roll(edge, shift, 1) if shift else edge, to_left)
            msg[0, t, A] = to_right
            msg[1, t, A] = to_left
            return unused

        lax.fori_loop(0, 8, one, 0)

    tell(first_out, n_first, 1, left, f_send, f_recv)
    tell_both(slot, n_slot, 4, None)
    f1_c.wait()
    gathered(1, lambda a: F[1, a])
    tell_both(msg, n_mat, 1, 1)
    f0_c.wait()
    gathered(0, lambda a: F[0, a])
    tell_both(msg, n_mat, 0, 0)
    f2_c.wait()
    sweep(0, work, h0)
    halo_pack(1, work)
    h1 = halo_send(1)

    def upward(started, ref, own, count, recv, full, masked):
        gather_wait(started, ref, own, count, recv, full is None)
        for k in range(count):
            e = unpack_matrix(ref[k])
            rows = pl.ds(k * 64, 64)
            if full is not None:
                full[rows, :] = e
            masked[rows, :] = jnp.where(k < own, e, eye)
        scan_products([masked] if full is None else [full, masked], count)

    def later(ref, h, count):
        return ref[pl.ds((h + 1) * 64, 64), :] if h + 1 < count else eye

    upward(rm1, RM1, g, ng, m_recv.at[0], Z1, Zm1)
    RM2[x] = pack_matrix(Z1[0:64, :])
    rm2 = gather_start(RM2, x, along_x, nx, m_send.at[1], m_recv.at[1])
    def weigh(ref, h, parts):
        ref[pl.ds(h * 64, 64), :] = jnp.concatenate(split(jnp.concatenate(parts, axis=1)), axis=1)

    for h in range(ng):
        weigh(W1, h, [later(Z1, h, ng), jnp.where(h < g, later(Zm1, h, ng), 0.0)])

    pack_ends(1, lambda k: work[pl.ds(8 * k, 8), :])
    for side, peer in ((0, right), (1, left)):
        tell(vec.at[side], n_vec.at[side], 5, peer, n_send.at[side], n_recv.at[side])
    gathered(2, lambda a: F[2, a])
    tell_both(msg, n_mat, 2, 2)

    fine_apply(1, work, h1, to_residue)
    residue = res[...]
    values = []
    for m in range(4):
        weight = jnp.sum((tent[m] * residue).reshape(8, 8, 128), axis=0)
        values.append(row_sum(weight) * (1.0 / math.sqrt(64)))
    spread = jnp.where(own_block, jnp.concatenate(values, axis=1), 0.0)
    rhs = dot2(spread, GT, NT)
    offsets = diagonal(dotf(rhs, cis[...], NT), 8)
    after_own = jnp.concatenate([Zl[64:512, :], eye], axis=0)
    RV1[g] = padded(row_sum(dotf(offsets, after_own)))
    rv1 = gather_start(RV1, g, in_group, ng, v_send.at[0], v_recv.at[0])

    upward(rm2, RM2, x, nx, m_recv.at[1], Z2, Zm2)
    RM3[z] = pack_matrix(Z2[0:64, :])
    rm3 = gather_start(RM3, z, along_z, nz, m_send.at[2], m_recv.at[2], True)
    for h in range(nx):
        weigh(W2, h, [later(Z2, h, nx), jnp.where(h < x, later(Zm2, h, nx), 0.0)])

    own = lanes_folded(offsets)
    off_out[...] = padded(own)
    tell(off_out, n_off, 0, left, f_send, f_recv)
    gathered(3, lambda a: I[a])
    tell_both(msg, n_mat, 3, 3)

    def inflow(ref, weights, count):
        flat = [ref[h] + pltpu.roll(ref[h + 1], 64, 1) for h in range(0, count, 2)]
        return halves(dot2(jnp.concatenate(flat, axis=1), weights[...]))


    gather_wait(rv1, RV1, g, ng, v_recv.at[0])
    flow1 = inflow(RV1, W1, ng)
    RV2[x] = padded(flow1[:, :64])
    rv2 = gather_start(RV2, x, along_x, nx, v_send.at[1], v_recv.at[1])

    scan_prefix(Pl, 8)

    row8 = iota((8, 64), 0)
    carried = jnp.broadcast_to(own[0:1], (8, 64))
    local = carried
    for j in range(1, 8):
        carried = dotf(carried, Xl[pl.ds(j * 64, 64), :]) + own[j : j + 1]
        local = jnp.where(row8 >= j, carried, local)


    gather_wait(rv2, RV2, x, nx, v_recv.at[1])
    flow2 = inflow(RV2, W2, nx)
    RV3[z] = padded(flow2[:, :64])
    rv3 = gather_start(RV3, z, along_z, nz, v_send.at[2], v_recv.at[2], True)

    A1 = Zm1[0:64, :]

    @pl.when(z > 0)
    def _():
        upward(rm3, RM3, z, nz, m_recv.at[2], None, Zm3)
        A21 = dotf(Zm2[0:64, :], Zm1[0:64, :])
        for h in range(nz):
            weigh(W3, h, [dotf(jnp.where(h < z, later(Zm3, h, nz), 0.0), A21)])

    @pl.when(z == 0)
    def _():
        for condition, copy in rm3:
            perhaps(condition, copy.wait_send)


    nearer = dotf(flow2[:, 64:], A1) + flow1[:, 64:]
    for copy in beside:
        copy.wait()
    valid = jnp.logical_or(jnp.logical_and(at_left, has_left), jnp.logical_and(at_right, has_right))

    def own_ends(ref, out):
        out = gather_lanes(lambda k: ref[pl.ds(8 * k, 8), :], 3, spot == 3, out)
        return gather_lanes(lambda k: ref[pl.ds(8 * k, 8), :], 8, spot == 7, out)

    b_halo, s_halo, *tent_halo = [n_vec[0, k] + n_vec[1, k] for k in range(6)]
    pat_halo = [n_vec[0, k] + n_vec[1, k] for k in (6, 7)]

    def placed(A, unused):
        for t in range(4):
            from_left, from_right = n_mat[0, t, A], n_mat[1, t, A]
            at_two_left = jnp.logical_or(spot == 1, spot == 2)
            at_two_right = jnp.logical_or(spot == 8, spot == 9)
            for u in range(8):
                p = jnp.where(at_two_left, pltpu.roll(from_left, (1 - 2 * u) % 128, 1), 0.0)
                shift = (8 - 2 * u) % 128
                q = pltpu.roll(from_right, shift, 1) if shift else from_right
                Hc[t, A * 8 + u] = jnp.where(at_two_right, q, p)
        return unused

    lax.fori_loop(0, 8, placed, 0)

    place = iota((64, 512), 1) % 16
    asked = jnp.where(place < 3, place + 13, place - 8) * 4 + col // 128
    pick_halo = (q == asked).astype(BF16)
    ends = jnp.concatenate([n_slot[0, 7:8, :], n_slot[1, 0:1, :]] + [n_slot[1, 0:1, :]] * 6, axis=0)
    slots = dot1(ends.astype(F32).astype(BF16), pick_halo)
    which = (iota((8, 512), 1) % 16 >= 8).astype(jnp.int32) == iota((8, 512), 0)
    slots = row_sum(jnp.where(which, slots, 0.0))
    GT_halo = (jnp.concatenate([slots] * 8, axis=0) == q.astype(F32)).astype(BF16)
    M_next = unpack_matrix(n_first[...])
    P_next = dotf(M_next, Pl[448:512, :])
    local_next = dotf(carried, M_next, NT) + n_off[0:1, :64]

    def halo_matvec(terms):
        rows = []
        for A in range(8):
            parts = []
            for u in range(8):
                total = None
                for t, v in terms:
                    term = Hc[t, A * 8 + u] * v
                    total = term if total is None else total + term
                parts.append(total)
            rows.append(fold(parts, 0))
        return fold(rows, 1)

    def halo_apply(v):
        return halo_matvec([(1, v), (0, pltpu.roll(v, 1, 1) * pat_halo[0]), (2, pltpu.roll(v, 127, 1) * pat_halo[1])])

    gather_wait(rv3, RV3, z, nz, v_recv.at[2], True)
    incoming = inflow(RV3, W3, nz) + nearer

    coarse = local + lanes_folded(diagonal(dotf(incoming, Pl[...], NT), 8))
    ce_ref[...] = coarse
    weights = jnp.where(own_block, dot2(coarse, GT), 0.0)
    total = None
    for m in range(4):
        w = row_sum(weights[:, m * 128 : m * 128 + 128]) * (1.0 / math.sqrt(64))
        term = tent[m] * jnp.concatenate([w] * 8, axis=0)
        total = term if total is None else total + term
    corr[...] = total
    next_first = dotf(incoming, P_next, NT) + local_next
    two = jnp.concatenate([incoming[0:1], next_first[0:1]] + [next_first[0:1]] * 6, axis=0)
    weights = jnp.where(which, dot2(two, GT_halo), 0.0)
    total = None
    for m in range(4):
        w = row_sum(weights[:, m * 128 : m * 128 + 128]) * (1.0 / math.sqrt(64))
        term = tent_halo[m] * w
        total = term if total is None else total + term
    c_halo = own_ends(corr, jnp.where(valid, total, 0.0))

    def post(ref, halo, emit):
        def left_of(k):
            return pltpu.roll(halo, 126 - 16 * k, 1)

        def right_of(k):
            return pltpu.roll(halo, 119 - 16 * k, 1)

        apply_with(ref[...], left_of, right_of, emit)

    def to_res(rows, y):
        res[rows, :] = y

    post(corr, c_halo, to_res)

    def prolong(rows, y):
        sol_ref[rows, :] = work[rows, :] + corr[rows, :] - SMOOTH * y

    block_apply(res[...], prolong)
    s_halo = s_halo + c_halo - SMOOTH * halo_matvec([(3, halo_apply(c_halo))])
    s_halo = jnp.where(valid, s_halo, 0.0)
    s_ends = own_ends(sol_ref, s_halo)

    def smooth(rows, y):
        sol_ref[rows, :] = sol_ref[rows, :] + DAMP * y

    post(sol_ref, s_ends, to_residue)
    block_apply(res[...], smooth)
    s_halo = s_halo + DAMP * halo_matvec([(3, b_halo - halo_apply(s_ends))])
    s_halo = jnp.where(valid, s_halo, 0.0)
    post(sol_ref, s_halo, to_residue)
    block_apply(res[...], smooth)


def body(nz, nx, ng, right_side, fine_blocks, fine_inverse, pattern, tentative, slot_map, coarse_inverse, coarse_lower):
    vmem = lambda *shape: pltpu.VMEM(shape, F32)
    dma = lambda *shape: pltpu.SemaphoreType.DMA(shape)
    top = max(nz, nx, ng)
    scratch = [
        vmem(3, 64, 64, 128), vmem(64, 64, 128), vmem(64, 128), pltpu.VMEM((2, 128), jnp.int32), vmem(4, 64, 128),
        pltpu.VMEM((8, 64), jnp.int32), vmem(64, 8, 64), vmem(64, 8, 64),
        vmem(64, 128), vmem(64, 128), vmem(64, 128),
        vmem(512, 64), vmem(512, 64), vmem(512, 64), vmem(ng * 64, 64), vmem(ng * 64, 64),
        vmem(nx * 64, 64), vmem(nx * 64, 64), vmem(nz * 64, 64),
        vmem(512, 64),
        pltpu.VMEM((ng * 64, 256), BF16), pltpu.VMEM((nx * 64, 256), BF16), pltpu.VMEM((nz * 64, 128), BF16),
        vmem(ng, 32, 128), vmem(nx, 32, 128), vmem(nz, 32, 128),
        vmem(ng, 8, 128), vmem(nx, 8, 128), vmem(nz, 8, 128),
        vmem(2, 2, 8, 128), vmem(2, 2, 8, 128),
        vmem(4, 64, 8, 128), vmem(2, 4, 8, 8, 128), vmem(2, 4, 8, 8, 128), vmem(2, 8, 8, 128), vmem(2, 8, 8, 128),
        pltpu.VMEM((2, 8, 64), jnp.int32), vmem(32, 128), vmem(8, 128), vmem(8, 128), vmem(32, 128),
        dma(10), dma(3, top), dma(3, top), dma(3, top), dma(3, top), dma(2, 2), dma(2, 2),
        dma(2, 6), dma(2, 6), dma(2), dma(2),
    ]
    result, coarse = pl.pallas_call(
        functools.partial(kernel, nz, nx, ng),
        out_shape=(
            jax.ShapeDtypeStruct((64, 128), F32),
            jax.ShapeDtypeStruct((8, 64), F32),
        ),
        in_specs=[pl.BlockSpec(memory_space=pl.ANY)] * 8,
        out_specs=(
            pl.BlockSpec(memory_space=pltpu.VMEM),
            pl.BlockSpec(memory_space=pltpu.VMEM),
        ),
        scratch_shapes=scratch,
        compiler_params=pltpu.CompilerParams(
            collective_id=0, has_side_effects=True, vmem_limit_bytes=60 * 2**20
        ),
        name="v_cycle",
    )(
        right_side, fine_blocks, fine_inverse, pattern, tentative, slot_map,
        jnp.transpose(coarse_inverse, (0, 2, 1)), jnp.transpose(coarse_lower, (0, 2, 1)),
    )
    return result, coarse.T


def solution(mesh):
    slabs, ng = mesh.shape["slab"], mesh.shape["group"]
    nx = 4 if slabs % 4 == 0 and slabs > 4 else 2
    both = ("slab", "group")
    in_specs = (
        P(None, both), P(None, None, None, both), P(None, None, both), P(None, both), P(None, None, both),
        P(both, None), P(None, None, both), P(None, None, both),
    )
    return jax.shard_map(
        functools.partial(body, slabs // nx, nx, ng),
        mesh=mesh,
        in_specs=in_specs,
        out_specs=(P(None, both), P(None, both)),
        check_vma=False,
    )
```

```python
import functools
import math

import jax
import jax.numpy as jnp
from jax import lax
from jax.experimental import pallas as pl
from jax.experimental.pallas import tpu as pltpu
from jax.sharding import PartitionSpec as P

DAMP = 0.8
SMOOTH = 0.67
F32 = jnp.float32
BF16 = jnp.bfloat16
MESH = pl.DeviceIdType.MESH

NN = (((1,), (0,)), ((), ()))
NT = (((1,), (1,)), ((), ()))


def split(x):
    hi = x.astype(BF16)
    return hi, (x - hi.astype(F32)).astype(BF16)


def dot1(a, b, dims=NN):
    return lax.dot_general(a, b, dims, preferred_element_type=F32)


def halves(t):
    n = t.shape[1] // 2
    return t[:, :n] + t[:, n:]


def dotf(a, b, dims=NN):
    return lax.dot_general(a, b, dims, precision=lax.Precision.HIGHEST, preferred_element_type=F32)


def dot2(a, b, dims=NN):
    t = dot1(jnp.concatenate(split(a), axis=0), b, dims)
    return t[: a.shape[0]] + t[a.shape[0] :]


def iota(shape, dim):
    return lax.broadcasted_iota(jnp.int32, shape, dim)


def fold(parts, axis):
    step = 1 if axis == 0 else 16
    at = iota((8, 128), axis) // step

    def mix(a, b, mask, shift):
        return jnp.where(mask, a, b) + pltpu.roll(jnp.where(mask, b, a), shift * step, axis)

    q = [parts[(i + 3) % 8] for i in range(8)]
    y = [mix(q[k], q[k + 4], ((at - k) & 7) < 4, 4) for k in range(4)]
    z = [mix(y[k], y[k + 2], ((at - k) & 3) >= 2, 2) for k in range(2)]
    return mix(z[0], z[1], (at & 1) == 1, 1)


def row_sum(x):
    x = x + pltpu.roll(x, 4, 0)
    x = x + pltpu.roll(x, 2, 0)
    return x + pltpu.roll(x, 1, 0)


def matvec(terms, width, emit):
    turns = 2 if len(terms) > 1 else 4

    def one(g, unused):
        for turn in range(turns):
            first = (g * turns + turn) * 8
            parts = []
            for a in range(8):
                total = None
                for load, v in terms:
                    product = load(first + a) * v
                    total = product if total is None else total + product
                parts.append(jnp.sum(total.reshape(width // 8, 8, 128), axis=0))
            emit(pl.ds(pl.multiple_of(first, 8), 8), fold(parts, 0))
        return unused

    lax.fori_loop(0, width // 8 // turns, one, 0)


def pack_matrix(m):
    return jnp.concatenate([m[:32, :], m[32:, :]], axis=1)


def unpack_matrix(p):
    return jnp.concatenate([p[:, :64], p[:, 64:]], axis=0)


def scan_products(refs, count):
    half = 1
    while half < count:
        for start in range(0, count, 2 * half):
            mid = start + half
            left = pl.ds(start * 64, half * 64)
            for ref in refs:
                ref[left, :] = dotf(ref[left, :], ref[pl.ds(mid * 64, 64), :])
        half *= 2


def scan_prefix(ref, count):
    half = 1
    while half < count:
        for start in range(0, count, 2 * half):
            mid = start + half
            right = pl.ds(mid * 64, half * 64)
            ref[right, :] = dotf(ref[right, :], ref[pl.ds((mid - 1) * 64, 64), :])
        half *= 2


def diagonal(x, count):
    return jnp.where(iota(x.shape, 0) == iota(x.shape, 1) // 64, x, 0.0)


def lanes_folded(x):
    t = x[:, 0:128] + x[:, 128:256] + x[:, 256:384] + x[:, 384:512]
    return t[:, :64] + t[:, 64:]


def padded(x):
    return jnp.concatenate([x, jnp.zeros_like(x)], axis=1)


def kernel(
    nz, nx, ng,
    b_h, f_h, i_h, pat_h, tent_h, slot_h, ci_h, cl_h,
    sol_ref, ce_ref,
    F, I, b, pat, tent, slot, ci, cl,
    work, res, corr,
    cis, Zl, Pl, Z1, Zm1, Z2, Zm2, Zm3,
    Xl, W1, W2, W3,
    RM1, RM2, RM3, RV1, RV2, RV3, halo_out, halo_in,
    Hc, msg, n_mat, vec, n_vec, n_slot, n_first, n_off, off_out, first_out,
    load_sem, m_send, m_recv, v_send, v_recv, h_send, h_recv, n_send, n_recv, f_send, f_recv,
):
    slab, g = lax.axis_index("slab"), lax.axis_index("group")
    z, x = slab // nx, slab % nx
    ns = nz * nx

    RM3[...] = jnp.zeros_like(RM3)
    RV3[...] = jnp.zeros_like(RV3)
    W3[...] = jnp.zeros_like(W3)

    def in_group(o):
        return (slab, lax.rem(g + o, ng))

    def along_x(o):
        return (z * nx + lax.rem(x + o, nx), g)

    def along_z(o):
        return (lax.rem(z + o, nz) * nx + x, g)

    at_end, at_start = g == ng - 1, g == 0
    right = (jnp.where(at_end, lax.rem(slab + 1, ns), slab), lax.rem(g + 1, ng))
    left = (jnp.where(at_start, lax.rem(slab + ns - 1, ns), slab), lax.rem(g + ng - 1, ng))

    barrier = pltpu.get_barrier_semaphore()
    for o in range(1, nz):

        @pl.when(z + o >= nz)
        def _(o=o):
            pl.semaphore_signal(barrier, inc=1, device_id=along_z(o), device_id_type=MESH)

    peers = [along_x(o) for o in range(1, nx)] + [right, left] + [in_group(o) for o in range(1, ng)]
    for peer in peers:
        pl.semaphore_signal(barrier, inc=1, device_id=peer, device_id_type=MESH)

    copies = []
    for k, (src, dst) in enumerate(
        [(ci_h, ci), (cl_h, cl), (i_h, I), (b_h, b), (slot_h, slot), (pat_h, pat),
         (f_h.at[1], F.at[1]), (f_h.at[0], F.at[0]), (f_h.at[2], F.at[2]), (tent_h, tent)]
    ):
        copy = pltpu.make_async_copy(src, dst, load_sem.at[k])
        copy.start()
        copies.append(copy)
    ci_c, cl_c, i_c, b_c, slot_c, pat_c, f1_c, f0_c, f2_c, tent_c = copies

    row64, lane64 = iota((64, 64), 0), iota((64, 64), 1)
    eye = (row64 == lane64).astype(F32)
    ci_c.wait()
    cl_c.wait()
    for j in range(8):
        cij = ci[:, j, :]
        cis[pl.ds(j * 64, 64), :] = cij
        m = -dotf(cij, cl[:, j, :])
        Pl[pl.ds(j * 64, 64), :] = m
        e = m.T
        Zl[pl.ds(j * 64, 64), :] = e
        Xl[pl.ds(j * 64, 64), :] = e
    scan_products([Zl], 8)

    sends = []

    def perhaps(condition, act):
        if condition is None:
            act()
        else:
            pl.when(condition)(act)

    def gather_start(ref, own, target, count, send, recv, forward=False):
        started = []
        for o in range(1, count):
            copy = pltpu.make_async_remote_copy(
                src_ref=ref.at[own],
                dst_ref=ref.at[own],
                send_sem=send.at[o],
                recv_sem=recv.at[own],
                device_id=target(o),
                device_id_type=MESH,
            )
            condition = own + o < count if forward else None
            perhaps(condition, copy.start)
            started.append((condition, copy))
        return started

    def gather_wait(started, ref, own, count, recv, forward=False):
        for o in range(1, count):
            other = lax.rem(own + o, count)
            arrival = pltpu.make_async_copy(ref.at[other], ref.at[other], recv.at[other])
            perhaps(own + o >= count if forward else None, arrival.wait)
        sends.extend(started)

    lane8, lane = iota((8, 128), 1), iota((64, 128), 1)
    has_left = jnp.logical_not(jnp.logical_and(slab == 0, at_start))
    has_right = jnp.logical_not(jnp.logical_and(slab == ns - 1, at_end))

    def halo_pack(turn, ref):
        to_right, to_left = jnp.zeros((8, 128), F32), jnp.zeros((8, 128), F32)
        for k in range(8):
            piece = ref[pl.ds(8 * k, 8), :]
            to_right = jnp.where(lane8 == k, pltpu.roll(piece, k + 1, 1), to_right)
            to_left = jnp.where(lane8 == k, pltpu.roll(piece, k, 1) if k else piece, to_left)
        halo_out[turn, 0] = to_right
        halo_out[turn, 1] = to_left

    def halo_send(turn):
        started = []
        for side, peer in ((0, right), (1, left)):
            copy = pltpu.make_async_remote_copy(
                src_ref=halo_out.at[turn, side],
                dst_ref=halo_in.at[turn, side],
                send_sem=h_send.at[turn, side],
                recv_sem=h_recv.at[turn, side],
                device_id=peer,
                device_id_type=MESH,
            )
            copy.start()
            started.append(copy)
        return started

    def apply_with(value, left_of, right_of, emit):
        before, after = [], []
        for k in range(8):
            piece = value[8 * k : 8 * k + 8]
            before.append(jnp.where(lane8 == 0, left_of(k), pltpu.roll(piece, 1, 1)))
            after.append(jnp.where(lane8 == 127, right_of(k), pltpu.roll(piece, 127, 1)))
        previous = jnp.concatenate(before, axis=0) * pat[0:1, :].astype(F32)
        following = jnp.concatenate(after, axis=0) * pat[1:2, :].astype(F32)
        matvec(
            [
                (lambda a: F[1, a], value),
                (lambda a: F[0, a], previous),
                (lambda a: F[2, a], following),
            ],
            64,
            emit,
        )

    def fine_apply(turn, ref, started, emit):
        for copy in started:
            copy.wait()
        from_left = jnp.where(has_left, halo_in[turn, 0], 0.0)
        from_right = jnp.where(has_right, halo_in[turn, 1], 0.0)

        def left_of(k):
            return pltpu.roll(from_left, 128 - k, 1) if k else from_left

        def right_of(k):
            return pltpu.roll(from_right, 127 - k, 1)

        apply_with(ref[...], left_of, right_of, emit)

    def block_apply(value, emit):
        matvec([(lambda a: I[a], value)], 64, emit)

    def to_residue(rows, y):
        res[rows, :] = b[rows, :] - y

    def sweep(turn, ref, started):
        fine_apply(turn, ref, started, to_residue)

        def emit(rows, y):
            ref[rows, :] = ref[rows, :] + DAMP * y

        block_apply(res[...], emit)

    def first(rows, y):
        work[rows, :] = DAMP * y

    i_c.wait()
    b_c.wait()
    block_apply(b[...], first)
    halo_pack(0, work)

    slot_c.wait()
    q, col = iota((64, 512), 0), iota((64, 512), 1)
    pick = (q == (col % 16) * 4 + col // 128).astype(BF16)
    own_block = iota((8, 512), 0) == (iota((8, 512), 1) % 128) // 16
    slots = dot1(slot[...].astype(F32).astype(BF16), pick)
    slots = row_sum(jnp.where(own_block, slots, 0.0))
    slots = jnp.concatenate([slots] * 8, axis=0)
    GT = (slots == q.astype(F32)).astype(BF16)

    group, spot = lane8 // 16, lane8 % 16
    at_left, at_right = spot < 3, jnp.logical_and(spot >= 8, spot < 11)

    def gather_lanes(pieces, shift, mask, out):
        for k in range(8):
            moved = pltpu.roll(pieces(k), shift + 16 * k, 1)
            out = jnp.where(jnp.logical_and(group == k, mask), moved, out)
        return out

    nothing = jnp.zeros((8, 128), F32)

    def pack_ends(place, pieces):
        vec[0, place] = gather_lanes(pieces, 3, at_left, nothing)
        vec[1, place] = gather_lanes(pieces, 8, at_right, nothing)

    beside = []

    def tell(src, dst, k, peer, send, recv):
        copy = pltpu.make_async_remote_copy(
            src_ref=src, dst_ref=dst, send_sem=send.at[k], recv_sem=recv.at[k], device_id=peer, device_id_type=MESH
        )
        copy.start()
        beside.append(copy)

    def tell_both(src, dst, k, part):
        for side, peer in ((0, right), (1, left)):
            here = src if part is None else src.at[side, part]
            there = dst.at[side] if part is None else dst.at[side, part]
            tell(here, there, k, peer, n_send.at[side], n_recv.at[side])

    first_out[...] = pack_matrix(Pl[0:64, :])
    pack_ends(0, lambda k: b[pl.ds(8 * k, 8), :])
    pat_c.wait()
    tent_c.wait()
    for m in range(4):
        pack_ends(2 + m, lambda k, m=m: tent[m, pl.ds(8 * k, 8), :])
    for r in range(2):
        row = jnp.broadcast_to(pat[r : r + 1, :].astype(F32), (8, 128))
        pack_ends(6 + r, lambda k: row)

    pl.semaphore_wait(barrier, len(peers) + nz - 1 - z)

    h0 = halo_send(0)
    RM1[g] = pack_matrix(Zl[0:64, :])
    rm1 = gather_start(RM1, g, in_group, ng, m_send.at[0], m_recv.at[0])

    def gathered(t, load):
        def one(A, unused):
            to_right, to_left = jnp.zeros((8, 128), F32), jnp.zeros((8, 128), F32)
            for u in range(8):
                whole = load(A * 8 + u)
                edge = jnp.zeros((8, 128), F32)
                for k in range(8):
                    piece = pltpu.roll(whole[8 * k : 8 * k + 8], (2 + 16 * k) % 128, 1)
                    edge = jnp.where(lane8 // 16 == k, piece, edge)
                here = (lane8 % 16) // 2 == u
                to_right = jnp.where(here, pltpu.roll(edge, 2 * u, 1) if u else edge, to_right)
                shift = (2 * u - 2) % 128
                to_left = jnp.where(here, pltpu.roll(edge, shift, 1) if shift else edge, to_left)
            msg[0, t, A] = to_right
            msg[1, t, A] = to_left
            return unused

        lax.fori_loop(0, 8, one, 0)

    tell(first_out, n_first, 1, left, f_send, f_recv)
    tell_both(slot, n_slot, 4, None)
    f1_c.wait()
    gathered(1, lambda a: F[1, a])
    tell_both(msg, n_mat, 1, 1)
    f0_c.wait()
    gathered(0, lambda a: F[0, a])
    tell_both(msg, n_mat, 0, 0)
    f2_c.wait()
    sweep(0, work, h0)
    halo_pack(1, work)
    h1 = halo_send(1)

    def upward(started, ref, own, count, recv, full, masked):
        gather_wait(started, ref, own, count, recv, full is None)
        for k in range(count):
            e = unpack_matrix(ref[k])
            rows = pl.ds(k * 64, 64)
            if full is not None:
                full[rows, :] = e
            masked[rows, :] = jnp.where(k < own, e, eye)
        scan_products([masked] if full is None else [full, masked], count)

    def later(ref, h, count):
        return ref[pl.ds((h + 1) * 64, 64), :] if h + 1 < count else eye

    upward(rm1, RM1, g, ng, m_recv.at[0], Z1, Zm1)
    RM2[x] = pack_matrix(Z1[0:64, :])
    rm2 = gather_start(RM2, x, along_x, nx, m_send.at[1], m_recv.at[1])
    def weigh(ref, h, parts):
        ref[pl.ds(h * 64, 64), :] = jnp.concatenate(split(jnp.concatenate(parts, axis=1)), axis=1)

    for h in range(ng):
        weigh(W1, h, [later(Z1, h, ng), jnp.where(h < g, later(Zm1, h, ng), 0.0)])

    pack_ends(1, lambda k: work[pl.ds(8 * k, 8), :])
    for side, peer in ((0, right), (1, left)):
        tell(vec.at[side], n_vec.at[side], 5, peer, n_send.at[side], n_recv.at[side])
    gathered(2, lambda a: F[2, a])
    tell_both(msg, n_mat, 2, 2)

    fine_apply(1, work, h1, to_residue)
    residue = res[...]
    values = []
    for m in range(4):
        weight = jnp.sum((tent[m] * residue).reshape(8, 8, 128), axis=0)
        values.append(row_sum(weight) * (1.0 / math.sqrt(64)))
    spread = jnp.where(own_block, jnp.concatenate(values, axis=1), 0.0)
    rhs = dot2(spread, GT, NT)
    offsets = diagonal(dotf(rhs, cis[...], NT), 8)
    after_own = jnp.concatenate([Zl[64:512, :], eye], axis=0)
    RV1[g] = padded(row_sum(dotf(offsets, after_own)))
    rv1 = gather_start(RV1, g, in_group, ng, v_send.at[0], v_recv.at[0])

    upward(rm2, RM2, x, nx, m_recv.at[1], Z2, Zm2)
    RM3[z] = pack_matrix(Z2[0:64, :])
    rm3 = gather_start(RM3, z, along_z, nz, m_send.at[2], m_recv.at[2], True)
    for h in range(nx):
        weigh(W2, h, [later(Z2, h, nx), jnp.where(h < x, later(Zm2, h, nx), 0.0)])

    own = lanes_folded(offsets)
    off_out[...] = padded(own)
    tell(off_out, n_off, 0, left, f_send, f_recv)
    gathered(3, lambda a: I[a])
    tell_both(msg, n_mat, 3, 3)

    def inflow(ref, weights, count):
        flat = [ref[h] + pltpu.roll(ref[h + 1], 64, 1) for h in range(0, count, 2)]
        return halves(dot2(jnp.concatenate(flat, axis=1), weights[...]))


    gather_wait(rv1, RV1, g, ng, v_recv.at[0])
    flow1 = inflow(RV1, W1, ng)
    RV2[x] = padded(flow1[:, :64])
    rv2 = gather_start(RV2, x, along_x, nx, v_send.at[1], v_recv.at[1])

    scan_prefix(Pl, 8)

    row8 = iota((8, 64), 0)
    carried = jnp.broadcast_to(own[0:1], (8, 64))
    local = carried
    for j in range(1, 8):
        carried = dotf(carried, Xl[pl.ds(j * 64, 64), :]) + own[j : j + 1]
        local = jnp.where(row8 >= j, carried, local)


    gather_wait(rv2, RV2, x, nx, v_recv.at[1])
    flow2 = inflow(RV2, W2, nx)
    RV3[z] = padded(flow2[:, :64])
    rv3 = gather_start(RV3, z, along_z, nz, v_send.at[2], v_recv.at[2], True)

    A1 = Zm1[0:64, :]

    @pl.when(z > 0)
    def _():
        upward(rm3, RM3, z, nz, m_recv.at[2], None, Zm3)
        A21 = dotf(Zm2[0:64, :], Zm1[0:64, :])
        for h in range(nz):
            weigh(W3, h, [dotf(jnp.where(h < z, later(Zm3, h, nz), 0.0), A21)])


    nearer = dotf(flow2[:, 64:], A1) + flow1[:, 64:]
    for copy in beside:
        copy.wait()
    valid = jnp.logical_or(jnp.logical_and(at_left, has_left), jnp.logical_and(at_right, has_right))

    def own_ends(ref, out):
        out = gather_lanes(lambda k: ref[pl.ds(8 * k, 8), :], 3, spot == 3, out)
        return gather_lanes(lambda k: ref[pl.ds(8 * k, 8), :], 8, spot == 7, out)

    b_halo, s_halo, *tent_halo = [n_vec[0, k] + n_vec[1, k] for k in range(6)]
    pat_halo = [n_vec[0, k] + n_vec[1, k] for k in (6, 7)]

    def placed(A, unused):
        for t in range(4):
            from_left, from_right = n_mat[0, t, A], n_mat[1, t, A]
            at_two_left = jnp.logical_or(spot == 1, spot == 2)
            at_two_right = jnp.logical_or(spot == 8, spot == 9)
            for u in range(8):
                p = jnp.where(at_two_left, pltpu.roll(from_left, (1 - 2 * u) % 128, 1), 0.0)
                shift = (8 - 2 * u) % 128
                q = pltpu.roll(from_right, shift, 1) if shift else from_right
                Hc[t, A * 8 + u] = jnp.where(at_two_right, q, p)
        return unused

    lax.fori_loop(0, 8, placed, 0)

    place = iota((64, 512), 1) % 16
    asked = jnp.where(place < 3, place + 13, place - 8) * 4 + col // 128
    pick_halo = (q == asked).astype(BF16)
    ends = jnp.concatenate([n_slot[0, 7:8, :], n_slot[1, 0:1, :]] + [n_slot[1, 0:1, :]] * 6, axis=0)
    slots = dot1(ends.astype(F32).astype(BF16), pick_halo)
    which = (iota((8, 512), 1) % 16 >= 8).astype(jnp.int32) == iota((8, 512), 0)
    slots = row_sum(jnp.where(which, slots, 0.0))
    GT_halo = (jnp.concatenate([slots] * 8, axis=0) == q.astype(F32)).astype(BF16)
    M_next = unpack_matrix(n_first[...])
    P_next = dotf(M_next, Pl[448:512, :])
    local_next = dotf(carried, M_next, NT) + n_off[0:1, :64]

    def halo_matvec(terms):
        rows = []
        for A in range(8):
            parts = []
            for u in range(8):
                total = None
                for t, v in terms:
                    term = Hc[t, A * 8 + u] * v
                    total = term if total is None else total + term
                parts.append(total)
            rows.append(fold(parts, 0))
        return fold(rows, 1)

    def halo_apply(v):
        return halo_matvec([(1, v), (0, pltpu.roll(v, 1, 1) * pat_halo[0]), (2, pltpu.roll(v, 127, 1) * pat_halo[1])])

    gather_wait(rv3, RV3, z, nz, v_recv.at[2], True)
    incoming = inflow(RV3, W3, nz) + nearer

    coarse = local + lanes_folded(diagonal(dotf(incoming, Pl[...], NT), 8))
    ce_ref[...] = coarse
    weights = jnp.where(own_block, dot2(coarse, GT), 0.0)
    total = None
    for m in range(4):
        w = row_sum(weights[:, m * 128 : m * 128 + 128]) * (1.0 / math.sqrt(64))
        term = tent[m] * jnp.concatenate([w] * 8, axis=0)
        total = term if total is None else total + term
    corr[...] = total
    next_first = dotf(incoming, P_next, NT) + local_next
    two = jnp.concatenate([incoming[0:1], next_first[0:1]] + [next_first[0:1]] * 6, axis=0)
    weights = jnp.where(which, dot2(two, GT_halo), 0.0)
    total = None
    for m in range(4):
        w = row_sum(weights[:, m * 128 : m * 128 + 128]) * (1.0 / math.sqrt(64))
        term = tent_halo[m] * w
        total = term if total is None else total + term
    c_halo = own_ends(corr, jnp.where(valid, total, 0.0))

    def post(ref, halo, emit):
        def left_of(k):
            return pltpu.roll(halo, 126 - 16 * k, 1)

        def right_of(k):
            return pltpu.roll(halo, 119 - 16 * k, 1)

        apply_with(ref[...], left_of, right_of, emit)

    def to_res(rows, y):
        res[rows, :] = y

    post(corr, c_halo, to_res)

    def prolong(rows, y):
        sol_ref[rows, :] = work[rows, :] + corr[rows, :] - SMOOTH * y

    block_apply(res[...], prolong)
    s_halo = s_halo + c_halo - SMOOTH * halo_matvec([(3, halo_apply(c_halo))])
    s_halo = jnp.where(valid, s_halo, 0.0)
    s_ends = own_ends(sol_ref, s_halo)

    def smooth(rows, y):
        sol_ref[rows, :] = sol_ref[rows, :] + DAMP * y

    post(sol_ref, s_ends, to_residue)
    block_apply(res[...], smooth)
    s_halo = s_halo + DAMP * halo_matvec([(3, b_halo - halo_apply(s_ends))])
    s_halo = jnp.where(valid, s_halo, 0.0)
    post(sol_ref, s_halo, to_residue)
    block_apply(res[...], smooth)
    for condition, copy in sends:
        perhaps(condition, copy.wait_send)


def body(nz, nx, ng, right_side, fine_blocks, fine_inverse, pattern, tentative, slot_map, coarse_inverse, coarse_lower):
    vmem = lambda *shape: pltpu.VMEM(shape, F32)
    dma = lambda *shape: pltpu.SemaphoreType.DMA(shape)
    top = max(nz, nx, ng)
    scratch = [
        vmem(3, 64, 64, 128), vmem(64, 64, 128), vmem(64, 128), pltpu.VMEM((2, 128), jnp.int32), vmem(4, 64, 128),
        pltpu.VMEM((8, 64), jnp.int32), vmem(64, 8, 64), vmem(64, 8, 64),
        vmem(64, 128), vmem(64, 128), vmem(64, 128),
        vmem(512, 64), vmem(512, 64), vmem(512, 64), vmem(ng * 64, 64), vmem(ng * 64, 64),
        vmem(nx * 64, 64), vmem(nx * 64, 64), vmem(nz * 64, 64),
        vmem(512, 64),
        pltpu.VMEM((ng * 64, 256), BF16), pltpu.VMEM((nx * 64, 256), BF16), pltpu.VMEM((nz * 64, 128), BF16),
        vmem(ng, 32, 128), vmem(nx, 32, 128), vmem(nz, 32, 128),
        vmem(ng, 8, 128), vmem(nx, 8, 128), vmem(nz, 8, 128),
        vmem(2, 2, 8, 128), vmem(2, 2, 8, 128),
        vmem(4, 64, 8, 128), vmem(2, 4, 8, 8, 128), vmem(2, 4, 8, 8, 128), vmem(2, 8, 8, 128), vmem(2, 8, 8, 128),
        pltpu.VMEM((2, 8, 64), jnp.int32), vmem(32, 128), vmem(8, 128), vmem(8, 128), vmem(32, 128),
        dma(10), dma(3, top), dma(3, top), dma(3, top), dma(3, top), dma(2, 2), dma(2, 2),
        dma(2, 6), dma(2, 6), dma(2), dma(2),
    ]
    result, coarse = pl.pallas_call(
        functools.partial(kernel, nz, nx, ng),
        out_shape=(
            jax.ShapeDtypeStruct((64, 128), F32),
            jax.ShapeDtypeStruct((8, 64), F32),
        ),
        in_specs=[pl.BlockSpec(memory_space=pl.ANY)] * 8,
        out_specs=(
            pl.BlockSpec(memory_space=pltpu.VMEM),
            pl.BlockSpec(memory_space=pltpu.VMEM),
        ),
        scratch_shapes=scratch,
        compiler_params=pltpu.CompilerParams(
            collective_id=0, has_side_effects=True, vmem_limit_bytes=60 * 2**20
        ),
        name="v_cycle",
    )(
        right_side, fine_blocks, fine_inverse, pattern, tentative, slot_map,
        jnp.transpose(coarse_inverse, (0, 2, 1)), jnp.transpose(coarse_lower, (0, 2, 1)),
    )
    return result, coarse.T


def solution(mesh):
    slabs, ng = mesh.shape["slab"], mesh.shape["group"]
    nx = 4 if slabs % 4 == 0 and slabs > 4 else 2
    both = ("slab", "group")
    in_specs = (
        P(None, both), P(None, None, None, both), P(None, None, both), P(None, both), P(None, None, both),
        P(both, None), P(None, None, both), P(None, None, both),
    )
    return jax.shard_map(
        functools.partial(body, slabs // nx, nx, ng),
        mesh=mesh,
        in_specs=in_specs,
        out_specs=(P(None, both), P(None, both)),
        check_vma=False,
    )
```
